32 devices in a mesh: fsdp: 8 (over y, x, core), seq: 4 (over z).
Axes of the slice: x: 2, y: 2, z: 4, core: 2. Of those that a mesh axis runs over, the one named last changes fastest.
Arguments:
- tokens: bfloat16 [16384, 768], P(('fsdp', 'seq')), may hold values from -6 to 6
- doc_lengths: int32 [8, 3], P('fsdp'), may hold values from 1 to 1024, 2048 in all within a row
- gain_attn: bfloat16 [768], P('fsdp'), may hold values from 0.5 to 1.5
- query_weight: bfloat16 [768, 768], P('fsdp'), may hold values from -0.02734375 to 0.02734375
- key_weight: bfloat16 [768, 768], P('fsdp'), may hold values from -0.21875 to 0.21875
- value_weight: bfloat16 [768, 768], P('fsdp'), may hold values from -0.21875 to 0.21875
- out_weight: bfloat16 [768, 768], P('fsdp'), may hold values from -0.875 to 0.875
- bias_table: bfloat16 [384], P('fsdp'), may hold values from -4 to 4
- gain_ff: bfloat16 [768], P('fsdp'), may hold values from 0.5 to 1.5
- ff_in: bfloat16 [768, 3072], P('fsdp'), may hold values from -0.21875 to 0.21875
- ff_out: bfloat16 [3072, 768], P('fsdp'), may hold values from -0.109375 to 0.109375
- gain_self: bfloat16 [768], P('fsdp'), may hold values from 0.5 to 1.5
- self_value: bfloat16 [768, 768], P('fsdp'), may hold values from -0.21875 to 0.21875
- self_out: bfloat16 [768, 768], P('fsdp'), may hold values from -0.21875 to 0.21875
- gain_cross: bfloat16 [768], P('fsdp'), may hold values from 0.5 to 1.5
- cross_query: bfloat16 [768, 768], P('fsdp'), may hold values from -0.02734375 to 0.02734375
- cross_key: bfloat16 [768, 768], P('fsdp'), may hold values from -0.21875 to 0.21875
- cross_value: bfloat16 [768, 768], P('fsdp'), may hold values from -0.21875 to 0.21875
- cross_out: bfloat16 [768, 768], P('fsdp'), may hold values from -0.875 to 0.875
- gain_dff: bfloat16 [768], P('fsdp'), may hold values from 0.5 to 1.5
- dff_in: bfloat16 [768, 3072], P('fsdp'), may hold values from -0.21875 to 0.21875
- dff_out: bfloat16 [3072, 768], P('fsdp'), may hold values from -0.109375 to 0.109375
- enc_cot: bfloat16 [16384, 768], P(('fsdp', 'seq')), may hold values from -6 to 6
- dec_cot: bfloat16 [24, 768], P('fsdp'), may hold values from -6 to 6
Outputs:
- enc_hidden: float32 [16384, 768], P(('fsdp', 'seq'))
- dec_hidden: float32 [24, 768], P('fsdp')
- tokens_grad: float32 [16384, 768], P(('fsdp', 'seq'))
- gain_attn_grad: float32 [768], P('fsdp')
- query_weight_grad: float32 [768, 768], P('fsdp')
- key_weight_grad: float32 [768, 768], P('fsdp')
- value_weight_grad: float32 [768, 768], P('fsdp')
- out_weight_grad: float32 [768, 768], P('fsdp')
- bias_table_grad: float32 [384], P('fsdp')
- gain_ff_grad: float32 [768], P('fsdp')
- ff_in_grad: float32 [768, 3072], P('fsdp')
- ff_out_grad: float32 [3072, 768], P('fsdp')
- gain_self_grad: float32 [768], P('fsdp')
- self_value_grad: float32 [768, 768], P('fsdp')
- self_out_grad: float32 [768, 768], P('fsdp')
- gain_cross_grad: float32 [768], P('fsdp')
- cross_query_grad: float32 [768, 768], P('fsdp')
- cross_key_grad: float32 [768, 768], P('fsdp')
- cross_value_grad: float32 [768, 768], P('fsdp')
- cross_out_grad: float32 [768, 768], P('fsdp')
- gain_dff_grad: float32 [768], P('fsdp')
- dff_in_grad: float32 [768, 3072], P('fsdp')
- dff_out_grad: float32 [3072, 768], P('fsdp')
The draws below stay inside these ranges and needn't reach their ends.
Inputs may be any that keep to these rules, and one draw needn't show every extreme that they name: `doc_lengths`: row g gives, in order, the lengths of the 3 documents that make up tokens g * 2048 to (g + 1) * 2048 - 1; every row sums to 2048, and in every row the longest is exactly 1024.
All inputs are finite; a program needn't handle non-finite values.
Results may differ from the reference program's by a relative error of at most 0.022.
Values may be sent and summed in bfloat16 or wider, within the bound.
A program may use at most 256 MiB of HBM per device.

```python
import math
import jax
import jax.numpy as jnp
import numpy as np
from jax import lax

D = 768
HEADS = 12
HEAD = 64
FF = 3072
BUCKETS = 32
DOCS = 3
GROUP_TOK = 2048
DOC_MAX = 1024
GROUPS = 8
TOKENS = 16384
DEC_ROWS = 24


def steps_of(rng, extent, shards, low, largest):
    def one(position, parts):
        draws = jax.random.uniform(jax.random.fold_in(jax.random.fold_in(rng, 6), position), (parts,), jnp.float32, low / len(shards), largest / len(shards))
        return jnp.repeat(jnp.exp(draws), extent[position] // parts).reshape((-1,) + (1,) * (len(extent) - position - 1))

    factor_of = one(*shards[0])
    for cut in shards[1:]:
        factor_of = factor_of * one(*cut)
    return factor_of


def profile(number_of, total, bound, slope):
    weights = [(1 << 20) // math.isqrt(rank ** slope) + 1 for rank in range(2, number_of + 1)]
    rest, counts = total - bound - (number_of - 1), [1] * (number_of - 1)
    while rest > 0:
        candidates = [i for i in range(number_of - 1) if counts[i] < bound]
        mass, budget = sum([weights[i] for i in candidates]), rest
        for i in candidates:
            extra = min(bound - counts[i], max(1, budget * weights[i] // mass), rest)
            counts[i] = counts[i] + extra
            rest = rest - extra
    return np.array([bound] + counts)


def uneven(own_key, count, total, reach, skew):
    if count == 2:
        one = jax.random.randint(own_key, (), max(1, total - reach), min(reach, total - 1) + 1)
        return jnp.stack([one, total - one])
    lengths = jnp.asarray(profile(count, total, reach, skew), jnp.int32)
    twos = (count - 1) // 2
    source_of, receiver = lengths[1:1 + 2 * twos:2], lengths[2:2 + 2 * twos:2]
    room = jnp.minimum(source_of - 1, reach - receiver)
    passed = jax.random.randint(jax.random.fold_in(own_key, 1), (twos,), 0, 1 << 20) % (room + 1)
    lengths = lengths.at[1:1 + 2 * twos:2].set(source_of - passed).at[2:2 + 2 * twos:2].set(receiver + passed)
    return lengths[jax.random.permutation(jax.random.fold_in(own_key, 2), count)]


def centred(own_key, shape, scale, reach, pieces=(), kind=jnp.bfloat16):
    gain = steps_of(own_key, shape, pieces, -0.22, 0.18) if pieces else 1.0
    array = jax.random.normal(own_key, shape, jnp.float32) * scale * gain
    return jnp.minimum(jnp.maximum(array, -reach), reach).astype(kind)


def setup_inputs(seed: int = 0) -> dict:
    key_of = jax.random.split(jax.random.key(seed), 25)
    return {
        "tokens": centred(key_of[0], (TOKENS, D), 1.0, 6.0, ((0, 32),)),
        "doc_lengths": jax.vmap(lambda own: uneven(own, DOCS, GROUP_TOK, DOC_MAX, 1))(jax.random.split(key_of[1], GROUPS)).reshape((GROUPS, DOCS)).astype(jnp.int32),
        "gain_attn": jnp.clip(1.0 + 0.1 * jax.random.normal(key_of[2], (D,), jnp.float32), 0.5, 1.5).astype(jnp.bfloat16),
        "query_weight": centred(key_of[3], (D, D), (D * HEAD) ** -0.5, 0.02734375, ((0, 8),)),
        "key_weight": centred(key_of[4], (D, D), D ** -0.5, 0.21875, ((0, 8),)),
        "value_weight": centred(key_of[5], (D, D), D ** -0.5, 0.21875, ((0, 8),)),
        "out_weight": centred(key_of[6], (D, D), (max(D // 16, 4)) ** -0.5, 0.875, ((0, 8),)),
        "bias_table": centred(key_of[7], (HEADS * BUCKETS,), 1.0, 4.0, ((0, 8),)),
        "gain_ff": jnp.clip(1.0 + 0.1 * jax.random.normal(key_of[8], (D,), jnp.float32), 0.5, 1.5).astype(jnp.bfloat16),
        "ff_in": centred(key_of[9], (D, FF), D ** -0.5, 0.21875, ((0, 8),)),
        "ff_out": centred(key_of[10], (FF, D), FF ** -0.5, 0.109375, ((0, 8),)),
        "gain_self": jnp.clip(1.0 + 0.1 * jax.random.normal(key_of[11], (D,), jnp.float32), 0.5, 1.5).astype(jnp.bfloat16),
        "self_value": centred(key_of[12], (D, D), D ** -0.5, 0.21875, ((0, 8),)),
        "self_out": centred(key_of[13], (D, D), D ** -0.5, 0.21875, ((0, 8),)),
        "gain_cross": jnp.clip(1.0 + 0.1 * jax.random.normal(key_of[14], (D,), jnp.float32), 0.5, 1.5).astype(jnp.bfloat16),
        "cross_query": centred(key_of[15], (D, D), (D * HEAD) ** -0.5, 0.02734375, ((0, 8),)),
        "cross_key": centred(key_of[16], (D, D), D ** -0.5, 0.21875, ((0, 8),)),
        "cross_value": centred(key_of[17], (D, D), D ** -0.5, 0.21875, ((0, 8),)),
        "cross_out": centred(key_of[18], (D, D), (max(D // 16, 4)) ** -0.5, 0.875, ((0, 8),)),
        "gain_dff": jnp.clip(1.0 + 0.1 * jax.random.normal(key_of[19], (D,), jnp.float32), 0.5, 1.5).astype(jnp.bfloat16),
        "dff_in": centred(key_of[20], (D, FF), D ** -0.5, 0.21875, ((0, 8),)),
        "dff_out": centred(key_of[21], (FF, D), FF ** -0.5, 0.109375, ((0, 8),)),
        "enc_cot": centred(key_of[22], (TOKENS, D), 1.0, 6.0, ((0, 32),)),
        "dec_cot": centred(key_of[23], (DEC_ROWS, D), 1.0, 6.0, ((0, 8),)),
    }


epsilon = 1e-06
LIMITS = (12, 16, 23, 32, 46, 64, 91)
highest = lax.Precision.HIGHEST

@jax.custom_vjp
def low(v):
    return lax.optimization_barrier(v.astype(jnp.bfloat16)).astype(jnp.float32)

@jax.custom_vjp
def low_back(v):
    return v

def low_keep(v):
    return (low(v), None)

def low_pass(kept, grad):
    return (grad,)

def back_keep(v):
    return (v, None)

def back_low(kept, grad):
    return (low(grad),)
low.defvjp(low_keep, low_pass)
low_back.defvjp(back_keep, back_low)

def rounded_both(values):
    return low(low_back(values))

def matmul_high(left_side, right_side):
    return jnp.dot(left_side, right_side, precision=highest, preferred_element_type=jnp.float32)

def bucket_of(relative):
    distance = jnp.abs(relative).astype(jnp.int32)
    bucket = jnp.minimum(distance, 8).astype(jnp.int32)
    for bound_value in LIMITS:
        bucket = (bucket + (distance >= bound_value).astype(jnp.int32)).astype(jnp.int32)
    return (bucket + 16 * (relative > 0).astype(jnp.int32)).astype(jnp.int32)

def rms_norm(values, gain_vec):
    inverse = lax.rsqrt(lax.optimization_barrier(jnp.mean(values * values, axis=-1, keepdims=True)) + epsilon)
    return values * inverse * gain_vec

def smooth_gate(values):
    return jax.nn.gelu(values, approximate=True)

def group_layers(tokens_group, lengths_group, params):
    gain_attn, query_weight, key_weight, value_weight, out_weight, bias_table, gain_ff, ff_in, ff_out, gain_self, self_value, self_out, gain_cross, cross_query, cross_key, cross_value, cross_out, gain_dff, dff_in, dff_out = params
    group_tok = tokens_group.shape[0]
    block_rows = min(512, group_tok)
    lengths_group = lengths_group.astype(jnp.int32)
    doc_ends = jnp.cumsum(lengths_group, dtype=jnp.int32).astype(jnp.int32)
    starts = (doc_ends - lengths_group).astype(jnp.int32)
    positions = jnp.arange(group_tok, dtype=jnp.int32)
    segment = lax.optimization_barrier(jnp.sum((positions[:, None] >= doc_ends[None, :]).astype(jnp.int32), axis=1, dtype=jnp.int32)).astype(jnp.int32)
    table_heads = bias_table.reshape(HEADS, BUCKETS)
    normed = low(rms_norm(tokens_group, gain_attn))
    queries = rounded_both(matmul_high(normed, query_weight)).reshape(group_tok, HEADS, HEAD)
    keys_all = rounded_both(matmul_high(normed, key_weight)).reshape(group_tok, HEADS, HEAD)
    values_all = rounded_both(matmul_high(normed, value_weight)).reshape(group_tok, HEADS, HEAD)

    def attend_block(row_start):
        rows_query = lax.dynamic_slice_in_dim(queries, row_start, block_rows, 0)
        row_pos = (row_start + jnp.arange(block_rows, dtype=jnp.int32)).astype(jnp.int32)
        relative = (positions[None, :] - row_pos[:, None]).astype(jnp.int32)
        scores = jnp.einsum('qhe,khe->hqk', rows_query, keys_all, precision=highest)
        scores = low_back(scores + jnp.take(table_heads, bucket_of(relative), axis=1))
        seg_rows = lax.dynamic_slice_in_dim(segment, row_start, block_rows, 0)
        same_doc = seg_rows[:, None] == segment[None, :]
        attn_probs = low(jax.nn.softmax(jnp.where(same_doc[None], scores, -1e+30), axis=-1))
        return jnp.einsum('hqk,khe->qhe', attn_probs, values_all, precision=highest)
    block_starts = jnp.arange(0, group_tok, block_rows, dtype=jnp.int32)
    context = lax.map(jax.checkpoint(attend_block), block_starts)
    context = rounded_both(context.reshape(group_tok, D))
    middle = tokens_group + low_back(matmul_high(context, out_weight))
    normed_ff = low(rms_norm(middle, gain_ff))
    hidden = low(smooth_gate(low_back(matmul_high(normed_ff, ff_in))))
    enc_hidden = middle + low_back(matmul_high(hidden, ff_out))
    memory = low(enc_hidden)
    mem_keys = rounded_both(matmul_high(memory, cross_key)).reshape(group_tok, HEADS, HEAD)
    mem_values = rounded_both(matmul_high(memory, cross_value)).reshape(group_tok, HEADS, HEAD)
    onehot = (starts[:, None] == positions[None, :]).astype(jnp.float32)
    first_rows = matmul_high(onehot, tokens_group)
    self_normed = low(rms_norm(first_rows, gain_self))
    self_vals = rounded_both(matmul_high(self_normed, self_value))
    state_one = first_rows + low_back(matmul_high(self_vals, self_out))
    cross_normed = low(rms_norm(state_one, gain_cross))
    cross_q = rounded_both(matmul_high(cross_normed, cross_query)).reshape(-1, HEADS, HEAD)
    cross_scores = low_back(jnp.einsum('rhe,khe->hrk', cross_q, mem_keys, precision=highest))
    doc_ids = jnp.arange(lengths_group.shape[0], dtype=jnp.int32)
    doc_mask = doc_ids[:, None] == segment[None, :]
    cross_probs = low(jax.nn.softmax(jnp.where(doc_mask[None], cross_scores, -1e+30), axis=-1))
    cross_ctx = rounded_both(jnp.einsum('hrk,khe->rhe', cross_probs, mem_values, precision=highest).reshape(-1, D))
    state_two = state_one + low_back(matmul_high(cross_ctx, cross_out))
    ffn_normed = low(rms_norm(state_two, gain_dff))
    dec_hid = low(smooth_gate(low_back(matmul_high(ffn_normed, dff_in))))
    dec_hidden = state_two + low_back(matmul_high(dec_hid, dff_out))
    return (enc_hidden, dec_hidden)

def reference(tokens, doc_lengths, gain_attn, query_weight, key_weight, value_weight, out_weight, bias_table, gain_ff, ff_in, ff_out, gain_self, self_value, self_out, gain_cross, cross_query, cross_key, cross_value, cross_out, gain_dff, dff_in, dff_out, enc_cot, dec_cot):
    params = (gain_attn.astype(jnp.float32), query_weight.astype(jnp.float32), key_weight.astype(jnp.float32), value_weight.astype(jnp.float32), out_weight.astype(jnp.float32), bias_table.astype(jnp.float32), gain_ff.astype(jnp.float32), ff_in.astype(jnp.float32), ff_out.astype(jnp.float32), gain_self.astype(jnp.float32), self_value.astype(jnp.float32), self_out.astype(jnp.float32), gain_cross.astype(jnp.float32), cross_query.astype(jnp.float32), cross_key.astype(jnp.float32), cross_value.astype(jnp.float32), cross_out.astype(jnp.float32), gain_dff.astype(jnp.float32), dff_in.astype(jnp.float32), dff_out.astype(jnp.float32))
    groups_count = doc_lengths.shape[0]
    group_tok = tokens.shape[0] // groups_count
    tokens_all = tokens.astype(jnp.float32).reshape(groups_count, group_tok, D)
    lengths_all = doc_lengths.astype(jnp.int32)

    def forward(tokens_in, weights_all):

        def one_group(carried, inputs):
            enc_group, dec_group = group_layers(inputs[0], inputs[1], weights_all)
            return (carried, (enc_group, dec_group))
        unused, (enc_all, dec_all) = lax.scan(jax.checkpoint(one_group), jnp.zeros((), jnp.float32), (tokens_in, lengths_all))
        return (enc_all.reshape(-1, D), dec_all.reshape(-1, D))
    outputs, pullback = jax.vjp(forward, tokens_all, params)
    tokens_back, all_grads = pullback((enc_cot.astype(jnp.float32), dec_cot.astype(jnp.float32)))
    grad_gain_attn, grad_query, grad_key, grad_value, grad_out, grad_table, grad_gain_ff, grad_ff_in, grad_ff_out, grad_gain_self, grad_self_value, grad_self_out, grad_gain_cross, grad_cross_query, grad_cross_key, grad_cross_value, grad_cross_out, grad_gain_dff, grad_dff_in, grad_dff_out = all_grads
    return (outputs[0], outputs[1], tokens_back.reshape(-1, D), grad_gain_attn, grad_query, grad_key, grad_value, grad_out, grad_table, grad_gain_ff, grad_ff_in, grad_ff_out, grad_gain_self, grad_self_value, grad_self_out, grad_gain_cross, grad_cross_query, grad_cross_key, grad_cross_value, grad_cross_out, grad_gain_dff, grad_dff_in, grad_dff_out)
```

```python
import functools, math
import jax, jax.numpy as jnp
from jax import lax
from jax.experimental import pallas as pl
from jax.experimental.pallas import tpu as pltpu
from jax.sharding import PartitionSpec as P

HEADS=12; HEAD=64; BUCKETS=32
LIMITS = (12, 16, 23, 32, 46, 64, 91)
BLK=256
SUB=128
BAND=512
NEG=-1e30

def bucket_of(relative):
    distance = jnp.abs(relative)
    bucket = jnp.minimum(distance, 8)
    for bound_value in LIMITS:
        bucket = bucket + (distance >= bound_value).astype(jnp.int32)
    return bucket + 16 * (relative > 0).astype(jnp.int32)

def nt(a,b):
    return lax.dot_general(a,b,(((1,),(1,)),((),())),preferred_element_type=jnp.float32)
def tn(a,b):
    return lax.dot_general(a,b,(((0,),(0,)),((),())),preferred_element_type=jnp.float32)
def nn(a,b):
    return lax.dot_general(a,b,(((1,),(0,)),((),())),preferred_element_type=jnp.float32)

def band_offsets(sign):
    c = jnp.arange(BAND, dtype=jnp.int32)
    t = jnp.where(c < 3*SUB, c, c - BAND) - SUB
    return sign * t

def seg_of(pos, e0, e1):
    return (pos >= e0).astype(jnp.int32) + (pos >= e1).astype(jnp.int32)

def build_tiles(band_ref, tiles, hh, flip):
    row = band_ref[hh:hh+1, :]
    x = jnp.broadcast_to(row, (SUB, BAND))
    x = pltpu.roll(x, 0, 1, stride=1, stride_axis=0)
    last, first = row[0:1, 3*SUB-1:3*SUB], row[0:1, 3*SUB:3*SUB+1]
    near = [x[:, n*SUB:(n+1)*SUB] for n in range(3)]
    if flip:
        near = near[::-1]
        last, first = first, last
    low = jnp.broadcast_to(first, (SUB, SUB))
    high = jnp.broadcast_to(last, (SUB, SUB))
    for d in range(5):
        for r in range(2):
            for c in range(2):
                off = ((r - c) if flip else (c - r)) + 2*(d-2)
                tiles[hh, d, r*SUB:(r+1)*SUB, c*SUB:(c+1)*SUB] = low if off < -1 else high if off > 1 else near[off+1]

def fwd_kernel(info, band_ref, q_ref, k_ref, v_ref, ctx_ref, lse_ref, tiles, s_scr):
    p0, e0, e1 = info[0], info[1], info[2]
    T = q_ref.shape[0]; G = k_ref.shape[0]
    lane = lax.broadcasted_iota(jnp.int32, (1,128), 1)
    left = lane < HEAD
    for hh in range(2):
        build_tiles(band_ref, tiles, hh, False)
    for i in range(T//BLK):
        a = p0 + i*BLK; b = a + BLK - 1
        lo = jnp.where(a >= e1, e1, jnp.where(a >= e0, e0, 0))
        hi = jnp.where(b >= e1, G, jnp.where(b >= e0, e1, e0))
        j0 = lo // BLK; j1 = (hi + BLK - 1)//BLK
        ib = a // BLK
        qb = q_ref[i*BLK:(i+1)*BLK, :]
        row_pos = a + lax.broadcasted_iota(jnp.int32, (BLK,1), 0)
        row_seg = jnp.broadcast_to(seg_of(row_pos, e0, e1),(BLK,128))
        zero = jnp.zeros_like(qb)
        qh = [jnp.where(left, qb, zero), jnp.where(left, zero, qb)]
        def score(j, carry):
            koff = pl.multiple_of(j*BLK, BLK)
            kb = k_ref[pl.ds(koff, BLK), :]
            kpos = koff + lax.broadcasted_iota(jnp.int32, (1,BLK), 1)
            kseg = seg_of(kpos, e0, e1)
            same = jnp.concatenate([row_seg == kseg[:, :128], row_seg == kseg[:,128:]],axis=1)
            d = jnp.clip(j - ib, -2, 2) + 2
            out = []
            for hh in range(2):
                s = nt(qh[hh], kb) + tiles[hh, d]
                s = jnp.where(same, s, NEG)
                s_scr[hh, j] = s
                out.append(jnp.maximum(carry[hh], jnp.maximum(s[:, :128], s[:, 128:])))
            return tuple(out)
        init = jnp.full((BLK,128), NEG, jnp.float32)
        mx = lax.fori_loop(j0, j1, score, (init, init))
        top = [jnp.max(m, axis=1, keepdims=True) for m in mx]
        def weigh(j, carry):
            koff = pl.multiple_of(j*BLK, BLK)
            vb = v_ref[pl.ds(koff, BLK), :]
            one = jnp.ones_like(vb)
            vh = [jnp.where(left, vb, one), jnp.where(left, one, vb)]
            out = []
            for hh in range(2):
                p = jnp.exp(s_scr[hh, j] - top[hh]).astype(jnp.bfloat16)
                out.append(carry[hh] + nn(p, vh[hh]))
            return tuple(out)
        zf = jnp.zeros((BLK,128), jnp.float32)
        acc = lax.fori_loop(j0, j1, weigh, (zf, zf))
        tot = [jnp.where(left, pltpu.roll(acc[0], HEAD, 1), pltpu.roll(acc[1], HEAD, 1))]
        num = jnp.where(left, acc[0], acc[1])
        total = tot[0]
        ctx_ref[i*BLK:(i+1)*BLK, :] = (num / total).astype(jnp.bfloat16)
        lse_ref[i*BLK:(i+1)*BLK, :] = jnp.where(left, top[0], top[1]) + jnp.log(total)

def attn_fwd(info, band, q, k, v):
    T=q.shape[0]; G=k.shape[0]; W=q.shape[1]
    pairs=W//128
    return pl.pallas_call(
        fwd_kernel,
        grid=(pairs,),
        in_specs=[pl.BlockSpec(memory_space=pltpu.SMEM),
                  pl.BlockSpec((None,2,BAND), lambda p:(p,0,0)),
                  pl.BlockSpec((T,128), lambda p:(0,p)),
                  pl.BlockSpec((G,128), lambda p:(0,p)),
                  pl.BlockSpec((G,128), lambda p:(0,p))],
        out_specs=[pl.BlockSpec((T,128), lambda p:(0,p)), pl.BlockSpec((T,128), lambda p:(0,p))],
        out_shape=[jax.ShapeDtypeStruct((T,W), jnp.bfloat16), jax.ShapeDtypeStruct((T,W), jnp.float32)],
        scratch_shapes=[pltpu.VMEM((2,5,BLK,BLK), jnp.float32), pltpu.VMEM((2,G//BLK,BLK,BLK), jnp.float32)],
        compiler_params=pltpu.CompilerParams(vmem_limit_bytes=50<<20),
        cost_estimate=pl.CostEstimate(flops=4*HEADS*T*1280*128, bytes_accessed=4*G*W+8*T*W, transcendentals=HEADS*T*1280),
    )(info, band, q, k, v)

def bwd_kernel(info, band_ref, q_ref, k_ref, v_ref, g_ref, ctx_ref, lse_ref, gq_ref, gk_ref, gv_ref, gb_ref, gf_ref, tiles, gt, gk_acc, gv_acc):
    p0, e0, e1 = info[0], info[1], info[2]
    T = q_ref.shape[0]; G = k_ref.shape[0]
    lane = lax.broadcasted_iota(jnp.int32, (1,128), 1)
    left = lane < HEAD
    sub_left = lax.broadcasted_iota(jnp.int32, (128,1), 0) < HEAD
    for hh in range(2):
        build_tiles(band_ref, tiles, hh, True)
    gt[...] = jnp.zeros_like(gt)
    gk_acc[...] = jnp.zeros_like(gk_acc)
    gv_acc[...] = jnp.zeros_like(gv_acc)
    for i in range(T//BLK):
        a = p0 + i*BLK; b = a + BLK - 1
        lo = jnp.where(a >= e1, e1, jnp.where(a >= e0, e0, 0))
        hi = jnp.where(b >= e1, G, jnp.where(b >= e0, e1, e0))
        j0 = lo // BLK; j1 = (hi + BLK - 1)//BLK
        ib = a // BLK
        rows = slice(i*BLK,(i+1)*BLK)
        qb = q_ref[rows, :]; gb = g_ref[rows, :]
        zero = jnp.zeros_like(qb)
        qh = [jnp.where(left, qb, zero), jnp.where(left, zero, qb)]
        gh = [jnp.where(left, gb, zero), jnp.where(left, zero, gb)]
        prod = (gb.astype(jnp.float32) * ctx_ref[rows,:].astype(jnp.float32)).T
        lse_t = lse_ref[rows,:].T
        dot = [jnp.sum(prod[hh*HEAD:(hh+1)*HEAD], axis=0, keepdims=True) for hh in range(2)]
        lse = [lse_t[hh*HEAD:hh*HEAD+1] for hh in range(2)]
        q_pos = a + lax.broadcasted_iota(jnp.int32, (1,BLK), 1)
        q_seg = seg_of(q_pos, e0, e1)
        def step(j, carry):
            koff = pl.multiple_of(j*BLK, BLK)
            kb = k_ref[pl.ds(koff, BLK), :]
            vb = v_ref[pl.ds(koff, BLK), :]
            kpos = koff + lax.broadcasted_iota(jnp.int32, (BLK,1), 0)
            same = jnp.broadcast_to(seg_of(kpos, e0, e1), (BLK,BLK)) == jnp.broadcast_to(q_seg, (BLK,BLK))
            d = jnp.clip(j - ib, -2, 2) + 2
            gqs=[]
            gk = None; gv=None
            for hh in range(2):
                s = nt(kb, qh[hh]) + tiles[hh, d]
                s = jnp.where(same, s, NEG)
                p = jnp.exp(s - lse[hh])
                gp = nt(vb, gh[hh])
                gs = p * (gp - dot[hh])
                gt[hh, d] += gs
                pb = p.astype(jnp.bfloat16); gsb = gs.astype(jnp.bfloat16)
                tk = nn(gsb, qh[hh]); tv = nn(pb, gh[hh])
                gk = tk if gk is None else gk + tk
                gv = tv if gv is None else gv + tv
                gqs.append(carry[hh] + tn(gsb, kb))
            gk_acc[pl.ds(koff,BLK), :] += gk
            gv_acc[pl.ds(koff,BLK), :] += gv
            return tuple(gqs)
        zf = jnp.zeros((BLK,128), jnp.float32)
        gq = lax.fori_loop(j0, j1, step, (zf, zf))
        gq_ref[rows,:] = jnp.where(left, gq[0], gq[1]).astype(jnp.bfloat16)
    gk_ref[...] = gk_acc[...].astype(jnp.bfloat16)
    gv_ref[...] = gv_acc[...].astype(jnp.bfloat16)
    for hh in range(2):
        near = [None]*3; low = None; high = None
        for d in range(5):
            for r in range(2):
                for c in range(2):
                    off = r - c + 2*(d-2)
                    x = gt[hh, d, r*SUB:(r+1)*SUB, c*SUB:(c+1)*SUB]
                    if off < -1: low = x if low is None else low + x
                    elif off > 1: high = x if high is None else high + x
                    else: near[off+1] = x if near[off+1] is None else near[off+1] + x
        x = jnp.concatenate([near[2], near[1], near[0], jnp.zeros((SUB,SUB),jnp.float32)], axis=1)
        rows_left = SUB
        while rows_left > 1:
            rows_left //= 2
            x = x[:rows_left] + pltpu.roll(x[rows_left:], BAND - rows_left, 1)
        gb_ref[hh:hh+1,:] = x
        gf_ref[hh:hh+1,:] = jnp.concatenate([jnp.sum(low, axis=0, keepdims=True), jnp.sum(high, axis=0, keepdims=True)], axis=1)

def attn_bwd(info, band, q, k, v, g, ctx, lse):
    T=q.shape[0]; G=k.shape[0]; W=q.shape[1]
    pairs=W//128
    tb = lambda: pl.BlockSpec((T,128), lambda p:(0,p))
    gb = lambda: pl.BlockSpec((G,128), lambda p:(0,p))
    return pl.pallas_call(
        bwd_kernel,
        grid=(pairs,),
        in_specs=[pl.BlockSpec(memory_space=pltpu.SMEM),
                  pl.BlockSpec((None,2,BAND), lambda p:(p,0,0)),
                  tb(), gb(), gb(), tb(), tb(), tb()],
        out_specs=[tb(), gb(), gb(), pl.BlockSpec((None,2,BAND), lambda p:(p,0,0)), pl.BlockSpec((None,2,2*SUB), lambda p:(p,0,0))],
        out_shape=[jax.ShapeDtypeStruct((T,W), jnp.bfloat16), jax.ShapeDtypeStruct((G,W), jnp.bfloat16), jax.ShapeDtypeStruct((G,W), jnp.bfloat16),
                   jax.ShapeDtypeStruct((pairs,2,BAND), jnp.float32), jax.ShapeDtypeStruct((pairs,2,2*SUB), jnp.float32)],
        scratch_shapes=[pltpu.VMEM((2,5,BLK,BLK), jnp.float32), pltpu.VMEM((2,5,BLK,BLK), jnp.float32),
                        pltpu.VMEM((G,128), jnp.float32), pltpu.VMEM((G,128), jnp.float32)],
        compiler_params=pltpu.CompilerParams(vmem_limit_bytes=50<<20),
        cost_estimate=pl.CostEstimate(flops=10*HEADS*T*1280*128, bytes_accessed=8*G*W+12*T*W, transcendentals=HEADS*T*1280),
    )(info, band, q, k, v, g, ctx, lse)

def make_band(table, sign):
    off = band_offsets(sign)
    oh = (bucket_of(off)[None,:] == jnp.arange(BUCKETS, dtype=jnp.int32)[:,None]).astype(jnp.bfloat16)
    return jnp.dot(table, oh, preferred_element_type=jnp.float32).reshape(HEADS//2, 2, BAND)

def table_grad(gb, gf):
    oh = (bucket_of(band_offsets(-1))[:,None] == jnp.arange(BUCKETS, dtype=jnp.int32)[None,:]).astype(jnp.float32)
    t = jnp.dot(gb.reshape(HEADS,BAND), oh, precision=lax.Precision.HIGHEST)
    f = gf.reshape(HEADS, 2, SUB).sum(axis=2)
    return t.at[:,15].add(f[:,0]).at[:,31].add(f[:,1])


eps = 1e-06
GELU_COEF = 0.044715
GELU_ROOT = math.sqrt(2.0 / math.pi)
bf16 = jnp.bfloat16
f32 = jnp.float32


def gelu_both(values):
    inner = GELU_ROOT * (values + GELU_COEF * values * values * values)
    tanh_val = jnp.tanh(inner)
    half = 0.5 * (1.0 + tanh_val)
    slope = half + 0.5 * values * (1.0 - tanh_val * tanh_val) * GELU_ROOT * (
        1.0 + 3.0 * GELU_COEF * values * values
    )
    return values * half, slope


def norm_forward(values, gain_vec):
    inverse = lax.rsqrt(jnp.mean(values * values, axis=-1, keepdims=True) + eps)
    return (values * inverse * gain_vec).astype(bf16), inverse


def norm_backward(values, inverse, gain_vec, grad_normed):
    scaled = grad_normed * gain_vec
    cubed = inverse * inverse * inverse
    grad_values = inverse * scaled - values * cubed * jnp.mean(
        scaled * values, axis=-1, keepdims=True
    )
    return grad_values, jnp.sum(grad_normed * values * inverse, axis=0)


def body(
    tokens, doc_lengths, gain_attn, query_weight, key_weight, value_weight, out_weight, bias_table,
    gain_ff, ff_in, ff_out, gain_self, self_value, self_out, gain_cross, cross_query, cross_key,
    cross_value, cross_out, gain_dff, dff_in, dff_out, enc_cot, dec_cot,
):
    seq_index = lax.axis_index("seq")
    seq_count = lax.axis_size("seq")
    own = lax.axis_index("fsdp")
    fsdp = lax.axis_size("fsdp")
    rows = tokens.shape[0]
    width = tokens.shape[1]
    group_tok = rows * seq_count
    part = query_weight.shape[0]
    buckets_part = bias_table.shape[0]
    docs = doc_lengths.shape[1]

    columns = [gain_attn, gain_ff, gain_self, gain_cross, gain_dff,
               jnp.pad(bias_table, (0, part - buckets_part))]
    small = jnp.pad(jnp.stack(columns, axis=1), ((0, 0), (0, 128 - len(columns))))
    over_fsdp = lambda piece: lax.all_gather(piece, "fsdp", axis=0, tiled=True)
    group = lax.all_gather(tokens, "seq", axis=0, tiled=True)
    first_weights = over_fsdp(jnp.concatenate([query_weight, key_weight, value_weight, small], axis=1))
    second_weights = over_fsdp(jnp.concatenate([out_weight, ff_in], axis=1))
    ff_out_full = over_fsdp(ff_out)
    dec_weights = over_fsdp(jnp.concatenate(
        [self_value, self_out, cross_query, cross_key, cross_value, cross_out, dff_in], axis=1))
    dff_out_full = over_fsdp(dff_out)

    query_full = first_weights[:, :width]
    kv_full = first_weights[:, width : 3 * width]
    vectors = first_weights[:, 3 * width : 3 * width + len(columns)].astype(f32)
    gain_attn_f, gain_ff_f, gain_self_f, gain_cross_f, gain_dff_f = (vectors[:, n] for n in range(5))
    table = vectors[:, 5].reshape(fsdp, part)[:, :buckets_part].reshape(HEADS, BUCKETS).astype(bf16)
    out_full = second_weights[:, :width]
    ff_in_full = second_weights[:, width:]
    self_value_full, self_out_full, cross_query_full, cross_key_full, cross_value_full, cross_out_full = (
        dec_weights[:, n * width : (n + 1) * width] for n in range(6))
    dff_in_full = dec_weights[:, 6 * width :]

    lengths = doc_lengths[0]
    end_zero = lengths[0]
    end_one = lengths[0] + lengths[1]
    here = seq_index * rows
    info = jnp.stack([here.astype(jnp.int32), end_zero, end_one])
    local_seg = seg_of(here + jnp.arange(rows, dtype=jnp.int32), end_zero, end_one)
    starts = jnp.stack([jnp.zeros_like(end_zero), end_zero, end_one])

    group_f = group.astype(f32)
    normed_all, inverse_all = norm_forward(group_f, gain_attn_f)
    normed = lax.dynamic_slice_in_dim(normed_all, here, rows, 0)
    inverse_attn = lax.dynamic_slice_in_dim(inverse_all, here, rows, 0)
    query = nn(normed, query_full).astype(bf16)
    key = nn(normed_all, kv_full[:, :width]).astype(bf16)
    value = nn(normed_all, kv_full[:, width:]).astype(bf16)
    context, lse = attn_fwd(info, make_band(table, 1), query, key, value)
    tokens_f = tokens.astype(f32)
    middle = tokens_f + nn(context, out_full)
    normed_ff, inverse_ff = norm_forward(middle, gain_ff_f)
    pre_act = nn(normed_ff, ff_in_full)
    hidden_f, slope = gelu_both(pre_act)
    hidden = hidden_f.astype(bf16)
    enc_hidden = middle + nn(hidden, ff_out_full)
    memory = enc_hidden.astype(bf16)

    pick = (starts[:, None] == jnp.arange(group_tok, dtype=jnp.int32)[None, :]).astype(bf16)
    first = nn(pick, group)
    self_low, self_inv = norm_forward(first, gain_self_f)
    self_vals = nn(self_low, self_value_full).astype(bf16)
    state_one = first + nn(self_vals, self_out_full)
    cross_low, cross_inv = norm_forward(state_one, gain_cross_f)
    cross_q = nn(cross_low, cross_query_full).astype(bf16)
    head_of = jnp.arange(width, dtype=jnp.int32) // HEAD
    head_mask = (jnp.arange(HEADS, dtype=jnp.int32)[:, None] == head_of[None, :])[:, None, :]

    def by_head(values):
        return jnp.where(head_mask, values[None], 0).reshape(HEADS * docs, width)

    def from_heads(values):
        return jnp.sum(jnp.where(head_mask, values.reshape(HEADS, docs, width), 0), axis=0)

    probe = nt(by_head(cross_q), cross_key_full).astype(bf16)
    doc_rows = jnp.tile(jnp.arange(docs, dtype=jnp.int32), HEADS)
    in_doc = doc_rows[:, None] == local_seg[None, :]
    scores = jnp.where(in_doc, nt(probe, memory), NEG)
    top = jnp.max(scores, axis=1, keepdims=True)
    powers = jnp.where(in_doc, jnp.exp(scores - top), 0.0)
    total = jnp.sum(powers, axis=1, keepdims=True)
    mixed = nn(powers.astype(bf16), memory)
    lanes = lambda column: jnp.broadcast_to(column, (HEADS * docs, 128))
    parts = lax.all_gather(jnp.concatenate([mixed, lanes(top), lanes(total)], axis=1), "seq", axis=0)
    tops = parts[:, :, width : width + 1]
    top_all = jnp.max(tops, axis=0)
    scale = jnp.exp(tops - top_all[None])
    total_all = jnp.sum(scale * parts[:, :, width + 128 : width + 129], axis=0)
    mixed_all = (jnp.sum(scale * parts[:, :, :width], axis=0) / total_all).astype(bf16)
    cross_ctx = from_heads(nn(mixed_all, cross_value_full)).astype(bf16)
    state_two = state_one + nn(cross_ctx, cross_out_full)
    ffn_low, ffn_inv = norm_forward(state_two, gain_dff_f)
    dec_hid_f, dec_slope = gelu_both(nn(ffn_low, dff_in_full))
    dec_hid = dec_hid_f.astype(bf16)
    dec_hidden = state_two + nn(dec_hid, dff_out_full)

    grad_dec_pre = (dec_slope * nt(dec_cot, dff_out_full)).astype(bf16)
    back_values, grad_gain_dff = norm_backward(state_two, ffn_inv, gain_dff_f, nt(grad_dec_pre, dff_in_full))
    grad_two = dec_cot.astype(f32) + back_values
    grad_two_low = grad_two.astype(bf16)
    grad_cross_ctx = nt(grad_two_low, cross_out_full).astype(bf16)
    pull = nt(by_head(grad_cross_ctx), cross_value_full).astype(bf16)
    probs = powers * (jnp.exp(top - top_all) / total_all)
    row_dot = jnp.sum(by_head(grad_cross_ctx.astype(f32) * cross_ctx.astype(f32)), axis=1, keepdims=True)
    grad_scores = (probs * (nt(pull, memory) - row_dot)).astype(bf16)
    grad_memory = tn(jnp.concatenate([grad_scores, probs.astype(bf16)], axis=0),
                     jnp.concatenate([probe, pull], axis=0))
    grad_mixed = lax.psum(nn(grad_scores, memory), "seq").astype(bf16)
    grad_cross_q = from_heads(nn(grad_mixed, cross_key_full)).astype(bf16)
    back_values, grad_gain_cross = norm_backward(state_one, cross_inv, gain_cross_f, nt(grad_cross_q, cross_query_full))
    grad_one = grad_two + back_values
    grad_one_low = grad_one.astype(bf16)
    grad_self_vals = nt(grad_one_low, self_out_full).astype(bf16)
    back_values, grad_gain_self = norm_backward(first, self_inv, gain_self_f, nt(grad_self_vals, self_value_full))
    grad_first = grad_one + back_values

    gains_rows = jnp.stack([grad_gain_self, grad_gain_cross, grad_gain_dff]).astype(bf16)
    pack = [self_low, grad_self_vals, self_vals, grad_one_low, cross_low, grad_cross_q, cross_q, grad_cross_ctx,
            cross_ctx, grad_two_low, ffn_low, dec_cot, gains_rows]
    wide = dec_hid.shape[1] // width
    pack += [dec_hid[:, n * width : (n + 1) * width] for n in range(wide)]
    pack += [grad_dec_pre[:, n * width : (n + 1) * width] for n in range(wide)]
    pack += [grad_mixed, mixed_all]
    pack = jnp.concatenate(pack, axis=0)
    pack = jnp.pad(pack, ((0, -pack.shape[0] % 16), (0, 0)))
    packs = lax.all_gather(pack, "fsdp", axis=0)
    rowset = lambda n: packs[:, n * docs : (n + 1) * docs].reshape(fsdp * docs, width)
    mine = lambda values: lax.dynamic_slice_in_dim(values, own * part, part, 1)
    shard_self_value = tn(mine(rowset(0)), rowset(1))
    shard_self_out = tn(mine(rowset(2)), rowset(3))
    shard_cross_query = tn(mine(rowset(4)), rowset(5))
    shard_cross_out = tn(mine(rowset(8)), rowset(9))
    at = 13
    hid_all = jnp.concatenate([rowset(at + n) for n in range(wide)], axis=1)
    pre_all = jnp.concatenate([rowset(at + wide + n) for n in range(wide)], axis=1)
    shard_dff_in = tn(mine(rowset(10)), pre_all)
    part_ff = dff_out.shape[0]
    shard_dff_out = tn(lax.dynamic_slice_in_dim(hid_all, own * part_ff, part_ff, 1), rowset(11))
    gains_all = jnp.sum(packs[:, 12 * docs : 13 * docs].astype(f32), axis=0)
    gains_own = mine(gains_all)
    at = (13 + 2 * wide) * docs
    heads_rows = HEADS * docs
    mixed_g = packs[:, at : at + heads_rows].reshape(fsdp * heads_rows, width)
    mixed_m = packs[:, at + heads_rows : at + 2 * heads_rows].reshape(fsdp * heads_rows, width)
    spread = lambda n: jnp.where(head_mask[None], packs[:, None, n * docs : (n + 1) * docs], 0).reshape(
        fsdp * heads_rows, width)
    shard_cross_key = tn(mine(mixed_g), spread(6))
    shard_cross_value = tn(mine(mixed_m), spread(7))

    grad_enc = enc_cot.astype(f32) + grad_memory
    grad_enc_low = grad_enc.astype(bf16)
    scatter = lambda values: lax.psum(
        lax.psum_scatter(values.astype(bf16), "fsdp", scatter_dimension=0, tiled=True), "seq").astype(f32)
    shard_ff_out = scatter(tn(hidden, grad_enc_low))
    grad_pre = (slope * nt(grad_enc_low, ff_out_full)).astype(bf16)
    shard_ff_in = scatter(tn(normed_ff, grad_pre))
    back_values, grad_gain_ff = norm_backward(middle, inverse_ff, gain_ff_f, nt(grad_pre, ff_in_full))
    grad_middle = grad_enc + back_values
    grad_middle_low = grad_middle.astype(bf16)
    grad_out = tn(context, grad_middle_low)
    grad_context = nt(grad_middle_low, out_full).astype(bf16)
    grad_query, grad_key, grad_value, grad_band, grad_far = attn_bwd(
        info, make_band(table, -1), query, key, value, grad_context, context, lse)
    grad_table = table_grad(grad_band, grad_far).reshape(fsdp, buckets_part)
    partial = nt(grad_key, kv_full[:, :width]) + nt(grad_value, kv_full[:, width:])
    grad_normed = nt(grad_query, query_full) + lax.psum_scatter(
        partial.astype(bf16), "seq", scatter_dimension=0, tiled=True).astype(f32)
    back_values, grad_gain_attn = norm_backward(tokens_f, inverse_attn, gain_attn_f, grad_normed)
    local_pick = lax.dynamic_slice_in_dim(pick, here, rows, 1).astype(f32)
    first_back = lax.dot_general(local_pick, grad_first, (((0,), (0,)), ((), ())),
                                 precision=lax.Precision.HIGHEST, preferred_element_type=f32)
    tokens_grad = grad_middle + back_values + first_back
    small_grads = [grad_gain_attn, grad_gain_ff,
                   jnp.pad(grad_table, ((0, 0), (0, part - buckets_part))).reshape(width)]
    small_grads = jnp.pad(jnp.stack(small_grads, axis=1), ((0, 0), (0, 125)))
    last = scatter(jnp.concatenate([
        tn(normed, grad_query).astype(bf16), tn(normed_all, grad_key).astype(bf16),
        tn(normed_all, grad_value).astype(bf16), grad_out.astype(bf16), small_grads.astype(bf16)], axis=1))
    shard_query, shard_key, shard_value, shard_out = (last[:, n * width : (n + 1) * width] for n in range(4))
    tail = last[:, 4 * width :]
    return (
        enc_hidden, dec_hidden, tokens_grad, tail[:, 0], shard_query, shard_key, shard_value, shard_out,
        tail[:buckets_part, 2], tail[:, 1], shard_ff_in, shard_ff_out, gains_own[0], shard_self_value, shard_self_out,
        gains_own[1], shard_cross_query, shard_cross_key, shard_cross_value, shard_cross_out, gains_own[2],
        shard_dff_in, shard_dff_out,
    )


def solution(mesh):
    tok, wide, one = P(("fsdp", "seq"), None), P("fsdp", None), P("fsdp")
    return jax.shard_map(
        body,
        mesh=mesh,
        in_specs=(tok, wide, one, wide, wide, wide, wide, one, one, wide, wide, one, wide, wide, one, wide, wide, wide,
                  wide, one, wide, wide, tok, wide),
        out_specs=(tok, wide, tok, one, wide, wide, wide, wide, one, one, wide, wide, one, wide, wide, one, wide, wide,
                   wide, wide, one, wide, wide),
        check_vma=False,
    )
```

```python
import functools, math
import jax, jax.numpy as jnp
from jax import lax
from jax.experimental import pallas as pl
from jax.experimental.pallas import tpu as pltpu
from jax.sharding import PartitionSpec as P

HEADS=12; HEAD=64; BUCKETS=32
LIMITS = (12, 16, 23, 32, 46, 64, 91)
BLK=256
SUB=128
BAND=512
NEG=-1e30

def bucket_of(relative):
    distance = jnp.abs(relative)
    bucket = jnp.minimum(distance, 8)
    for bound_value in LIMITS:
        bucket = bucket + (distance >= bound_value).astype(jnp.int32)
    return bucket + 16 * (relative > 0).astype(jnp.int32)

def nt(a,b):
    return lax.dot_general(a,b,(((1,),(1,)),((),())),preferred_element_type=jnp.float32)
def tn(a,b):
    return lax.dot_general(a,b,(((0,),(0,)),((),())),preferred_element_type=jnp.float32)
def nn(a,b):
    return lax.dot_general(a,b,(((1,),(0,)),((),())),preferred_element_type=jnp.float32)

def band_offsets(sign):
    c = jnp.arange(BAND, dtype=jnp.int32)
    t = jnp.where(c < 3*SUB, c, c - BAND) - SUB
    return sign * t

def seg_of(pos, e0, e1):
    return (pos >= e0).astype(jnp.int32) + (pos >= e1).astype(jnp.int32)

def build_tiles(band_ref, tiles, hh, flip):
    row = band_ref[hh:hh+1, :]
    x = jnp.broadcast_to(row, (SUB, BAND))
    x = pltpu.roll(x, 0, 1, stride=1, stride_axis=0)
    last, first = row[0:1, 3*SUB-1:3*SUB], row[0:1, 3*SUB:3*SUB+1]
    near = [x[:, n*SUB:(n+1)*SUB] for n in range(3)]
    if flip:
        near = near[::-1]
        last, first = first, last
    low = jnp.broadcast_to(first, (SUB, SUB))
    high = jnp.broadcast_to(last, (SUB, SUB))
    for d in range(5):
        for r in range(2):
            for c in range(2):
                off = ((r - c) if flip else (c - r)) + 2*(d-2)
                tiles[hh, d, r*SUB:(r+1)*SUB, c*SUB:(c+1)*SUB] = low if off < -1 else high if off > 1 else near[off+1]

def fwd_kernel(info, band_ref, q_ref, k_ref, v_ref, ctx_ref, lse_ref, tiles, s_scr):
    p0, e0, e1 = info[0], info[1], info[2]
    T = q_ref.shape[0]; G = k_ref.shape[0]
    lane = lax.broadcasted_iota(jnp.int32, (1,128), 1)
    left = lane < HEAD
    for hh in range(2):
        build_tiles(band_ref, tiles, hh, False)
    for i in range(T//BLK):
        a = p0 + i*BLK; b = a + BLK - 1
        lo = jnp.where(a >= e1, e1, jnp.where(a >= e0, e0, 0))
        hi = jnp.where(b >= e1, G, jnp.where(b >= e0, e1, e0))
        j0 = lo // BLK; j1 = (hi + BLK - 1)//BLK
        ib = a // BLK
        qb = q_ref[i*BLK:(i+1)*BLK, :]
        row_pos = a + lax.broadcasted_iota(jnp.int32, (BLK,1), 0)
        row_seg = jnp.broadcast_to(seg_of(row_pos, e0, e1),(BLK,128))
        zero = jnp.zeros_like(qb)
        qh = [jnp.where(left, qb, zero), jnp.where(left, zero, qb)]
        def score(j, carry):
            koff = pl.multiple_of(j*BLK, BLK)
            kb = k_ref[pl.ds(koff, BLK), :]
            kpos = koff + lax.broadcasted_iota(jnp.int32, (1,BLK), 1)
            kseg = seg_of(kpos, e0, e1)
            same = jnp.concatenate([row_seg == kseg[:, :128], row_seg == kseg[:,128:]],axis=1)
            d = jnp.clip(j - ib, -2, 2) + 2
            out = []
            for hh in range(2):
                s = nt(qh[hh], kb) + tiles[hh, d]
                s = jnp.where(same, s, NEG)
                s_scr[hh, j] = s
                out.append(jnp.maximum(carry[hh], jnp.maximum(s[:, :128], s[:, 128:])))
            return tuple(out)
        init = jnp.full((BLK,128), NEG, jnp.float32)
        mx = lax.fori_loop(j0, j1, score, (init, init))
        top = [jnp.max(m, axis=1, keepdims=True) for m in mx]
        def weigh(j, carry):
            koff = pl.multiple_of(j*BLK, BLK)
            vb = v_ref[pl.ds(koff, BLK), :]
            one = jnp.ones_like(vb)
            vh = [jnp.where(left, vb, one), jnp.where(left, one, vb)]
            out = []
            for hh in range(2):
                p = jnp.exp(s_scr[hh, j] - top[hh]).astype(jnp.bfloat16)
                out.append(carry[hh] + nn(p, vh[hh]))
            return tuple(out)
        zf = jnp.zeros((BLK,128), jnp.float32)
        acc = lax.fori_loop(j0, j1, weigh, (zf, zf))
        tot = [jnp.where(left, pltpu.roll(acc[0], HEAD, 1), pltpu.roll(acc[1], HEAD, 1))]
        num = jnp.where(left, acc[0], acc[1])
        total = tot[0]
        ctx_ref[i*BLK:(i+1)*BLK, :] = (num / total).astype(jnp.bfloat16)
        lse_ref[i*BLK:(i+1)*BLK, :] = jnp.where(left, top[0], top[1]) + jnp.log(total)

def attn_fwd(info, band, q, k, v):
    T=q.shape[0]; G=k.shape[0]; W=q.shape[1]
    pairs=W//128
    return pl.pallas_call(
        fwd_kernel,
        grid=(pairs,),
        in_specs=[pl.BlockSpec(memory_space=pltpu.SMEM),
                  pl.BlockSpec((None,2,BAND), lambda p:(p,0,0)),
                  pl.BlockSpec((T,128), lambda p:(0,p)),
                  pl.BlockSpec((G,128), lambda p:(0,p)),
                  pl.BlockSpec((G,128), lambda p:(0,p))],
        out_specs=[pl.BlockSpec((T,128), lambda p:(0,p)), pl.BlockSpec((T,128), lambda p:(0,p))],
        out_shape=[jax.ShapeDtypeStruct((T,W), jnp.bfloat16), jax.ShapeDtypeStruct((T,W), jnp.float32)],
        scratch_shapes=[pltpu.VMEM((2,5,BLK,BLK), jnp.float32), pltpu.VMEM((2,G//BLK,BLK,BLK), jnp.float32)],
        compiler_params=pltpu.CompilerParams(vmem_limit_bytes=24<<20),
        cost_estimate=pl.CostEstimate(flops=4*HEADS*T*1280*128, bytes_accessed=4*G*W+8*T*W, transcendentals=HEADS*T*1280),
    )(info, band, q, k, v)

def bwd_kernel(info, band_ref, q_ref, k_ref, v_ref, g_ref, ctx_ref, lse_ref, gq_ref, gk_ref, gv_ref, gb_ref, gf_ref, tiles, gt, gk_acc, gv_acc):
    p0, e0, e1 = info[0], info[1], info[2]
    T = q_ref.shape[0]; G = k_ref.shape[0]
    lane = lax.broadcasted_iota(jnp.int32, (1,128), 1)
    left = lane < HEAD
    sub_left = lax.broadcasted_iota(jnp.int32, (128,1), 0) < HEAD
    for hh in range(2):
        build_tiles(band_ref, tiles, hh, True)
    gt[...] = jnp.zeros_like(gt)
    gk_acc[...] = jnp.zeros_like(gk_acc)
    gv_acc[...] = jnp.zeros_like(gv_acc)
    for i in range(T//BLK):
        a = p0 + i*BLK; b = a + BLK - 1
        lo = jnp.where(a >= e1, e1, jnp.where(a >= e0, e0, 0))
        hi = jnp.where(b >= e1, G, jnp.where(b >= e0, e1, e0))
        j0 = lo // BLK; j1 = (hi + BLK - 1)//BLK
        ib = a // BLK
        rows = slice(i*BLK,(i+1)*BLK)
        qb = q_ref[rows, :]; gb = g_ref[rows, :]
        zero = jnp.zeros_like(qb)
        qh = [jnp.where(left, qb, zero), jnp.where(left, zero, qb)]
        gh = [jnp.where(left, gb, zero), jnp.where(left, zero, gb)]
        prod = (gb.astype(jnp.float32) * ctx_ref[rows,:].astype(jnp.float32)).T
        lse_t = lse_ref[rows,:].T
        dot = [jnp.sum(prod[hh*HEAD:(hh+1)*HEAD], axis=0, keepdims=True) for hh in range(2)]
        lse = [lse_t[hh*HEAD:hh*HEAD+1] for hh in range(2)]
        q_pos = a + lax.broadcasted_iota(jnp.int32, (1,BLK), 1)
        q_seg = seg_of(q_pos, e0, e1)
        def step(j, carry):
            koff = pl.multiple_of(j*BLK, BLK)
            kb = k_ref[pl.ds(koff, BLK), :]
            vb = v_ref[pl.ds(koff, BLK), :]
            kpos = koff + lax.broadcasted_iota(jnp.int32, (BLK,1), 0)
            same = jnp.broadcast_to(seg_of(kpos, e0, e1), (BLK,BLK)) == jnp.broadcast_to(q_seg, (BLK,BLK))
            d = jnp.clip(j - ib, -2, 2) + 2
            gqs=[]
            gk = None; gv=None
            for hh in range(2):
                s = nt(kb, qh[hh]) + tiles[hh, d]
                s = jnp.where(same, s, NEG)
                p = jnp.exp(s - lse[hh])
                gp = nt(vb, gh[hh])
                gs = p * (gp - dot[hh])
                gt[hh, d] += gs
                pb = p.astype(jnp.bfloat16); gsb = gs.astype(jnp.bfloat16)
                tk = nn(gsb, qh[hh]); tv = nn(pb, gh[hh])
                gk = tk if gk is None else gk + tk
                gv = tv if gv is None else gv + tv
                gqs.append(carry[hh] + tn(gsb, kb))
            gk_acc[pl.ds(koff,BLK), :] += gk
            gv_acc[pl.ds(koff,BLK), :] += gv
            return tuple(gqs)
        zf = jnp.zeros((BLK,128), jnp.float32)
        gq = lax.fori_loop(j0, j1, step, (zf, zf))
        gq_ref[rows,:] = jnp.where(left, gq[0], gq[1]).astype(jnp.bfloat16)
    gk_ref[...] = gk_acc[...].astype(jnp.bfloat16)
    gv_ref[...] = gv_acc[...].astype(jnp.bfloat16)
    for hh in range(2):
        near = [None]*3; low = None; high = None
        for d in range(5):
            for r in range(2):
                for c in range(2):
                    off = r - c + 2*(d-2)
                    x = gt[hh, d, r*SUB:(r+1)*SUB, c*SUB:(c+1)*SUB]
                    if off < -1: low = x if low is None else low + x
                    elif off > 1: high = x if high is None else high + x
                    else: near[off+1] = x if near[off+1] is None else near[off+1] + x
        x = jnp.concatenate([near[2], near[1], near[0], jnp.zeros((SUB,SUB),jnp.float32)], axis=1)
        rows_left = SUB
        while rows_left > 1:
            rows_left //= 2
            x = x[:rows_left] + pltpu.roll(x[rows_left:], BAND - rows_left, 1)
        gb_ref[hh:hh+1,:] = x
        gf_ref[hh:hh+1,:] = jnp.concatenate([jnp.sum(low, axis=0, keepdims=True), jnp.sum(high, axis=0, keepdims=True)], axis=1)

def attn_bwd(info, band, q, k, v, g, ctx, lse, first_pair, count, into):
    T=q.shape[0]; G=k.shape[0]; W=q.shape[1]
    at = lambda rows: pl.BlockSpec((rows,128), lambda p:(0,p+first_pair))
    kernel = bwd_kernel
    if into is not None:
        kernel = lambda *refs: bwd_kernel(*refs[:8], *refs[13:])
    extra = [] if into is None else list(into)
    small = lambda n: pl.BlockSpec((None,2,n), lambda p:(p+first_pair,0,0))
    pairs=W//128
    return pl.pallas_call(
        kernel,
        grid=(count,),
        in_specs=[pl.BlockSpec(memory_space=pltpu.SMEM), small(BAND),
                  at(T), at(G), at(G), at(T), at(T), at(T)] + [pl.BlockSpec(memory_space=pl.ANY)]*len(extra),
        out_specs=[at(T), at(G), at(G), small(BAND), small(2*SUB)],
        out_shape=[jax.ShapeDtypeStruct((T,W), jnp.bfloat16), jax.ShapeDtypeStruct((G,W), jnp.bfloat16), jax.ShapeDtypeStruct((G,W), jnp.bfloat16),
                   jax.ShapeDtypeStruct((pairs,2,BAND), jnp.float32), jax.ShapeDtypeStruct((pairs,2,2*SUB), jnp.float32)],
        scratch_shapes=[pltpu.VMEM((2,5,BLK,BLK), jnp.float32), pltpu.VMEM((2,5,BLK,BLK), jnp.float32),
                        pltpu.VMEM((G,128), jnp.float32), pltpu.VMEM((G,128), jnp.float32)],
        input_output_aliases={8+n: n for n in range(len(extra))},
        compiler_params=pltpu.CompilerParams(vmem_limit_bytes=24<<20),
        cost_estimate=pl.CostEstimate(flops=count*10*2*T*1280*128*4, bytes_accessed=(8*G*W+12*T*W)*count//pairs, transcendentals=2*count*T*1280),
    )(info, band, q, k, v, g, ctx, lse, *extra)

def make_band(table, sign):
    off = band_offsets(sign)
    oh = (bucket_of(off)[None,:] == jnp.arange(BUCKETS, dtype=jnp.int32)[:,None]).astype(jnp.bfloat16)
    return jnp.dot(table, oh, preferred_element_type=jnp.float32).reshape(HEADS//2, 2, BAND)

def table_grad(gb, gf):
    oh = (bucket_of(band_offsets(-1))[:,None] == jnp.arange(BUCKETS, dtype=jnp.int32)[None,:]).astype(jnp.float32)
    t = jnp.dot(gb.reshape(HEADS,BAND), oh, precision=lax.Precision.HIGHEST)
    f = gf.reshape(HEADS, 2, SUB).sum(axis=2)
    return t.at[:,15].add(f[:,0]).at[:,31].add(f[:,1])


DOC_MAX = 1024


def swap(values, axis, bit):
    count = lax.axis_size(axis)
    return lax.ppermute(values, axis, [(n, n ^ bit) for n in range(count)])


def shift(values, axis, step):
    count = lax.axis_size(axis)
    return lax.ppermute(values, axis, [(n, n + step) for n in range(count) if 0 <= n + step < count])


def bits_of(axis):
    bits = []
    while 1 << len(bits) < lax.axis_size(axis):
        bits.append(1 << len(bits))
    return bits


def pick_at(values, index, dim):
    return lax.dynamic_index_in_dim(values, index, dim, keepdims=False)


def add_low(left, right):
    return (left.astype(jnp.float32) + right.astype(jnp.float32)).astype(jnp.bfloat16)


def scatter_fsdp(values):
    index = lax.axis_index("fsdp")
    count = lax.axis_size("fsdp")
    bits = bits_of("fsdp")
    mine = lambda bit: (index // bit) % 2
    part = values.shape[0] // count
    columns = values.shape[1]
    values = values.reshape(count // 2, 2, part, columns)
    summed = add_low(pick_at(values, mine(1), 1), swap(pick_at(values, 1 - mine(1), 1), "fsdp", 1))
    cut = columns // 256 * 128
    done = []
    for piece, order in ((summed[:, :, :cut], bits[1:]), (summed[:, :, cut:], bits[:0:-1])):
        piece = piece.reshape((2,) * (len(bits) - 1) + piece.shape[1:])
        left = bits[:0:-1]
        for bit in order:
            dim = left.index(bit)
            piece = add_low(pick_at(piece, mine(bit), dim), swap(pick_at(piece, 1 - mine(bit), dim), "fsdp", bit))
            left = left[:dim] + left[dim + 1 :]
        done.append(piece)
    return done


def sum_seq(piece, dim):
    index = lax.axis_index("seq")
    bits = bits_of("seq")
    for bit in bits:
        mine = (index // bit) % 2
        low, high = jnp.split(piece, 2, axis=dim)
        keep = jnp.where(mine == 0, low, high)
        piece = add_low(keep, swap(jnp.where(mine == 0, high, low), "seq", bit))
    for bit in bits[::-1]:
        mine = (index // bit) % 2
        other = swap(piece, "seq", bit)
        piece = jnp.concatenate([jnp.where(mine == 0, piece, other), jnp.where(mine == 0, other, piece)], axis=dim)
    return piece


def gather_fsdp(values):
    index = lax.axis_index("fsdp")
    bits = bits_of("fsdp")
    mine = lambda bit: (index // bit) % 2
    part, columns = values.shape
    cut = columns // 256 * 128
    done = []
    for piece, order in ((values[:, :cut], bits[1:]), (values[:, cut:], bits[:0:-1])):
        piece = piece.reshape((1,) * (len(bits) - 1) + piece.shape)
        for bit in order:
            dim = bits[:0:-1].index(bit)
            other = swap(piece, "fsdp", bit)
            piece = jnp.concatenate([jnp.where(mine(bit) == 0, piece, other), jnp.where(mine(bit) == 0, other, piece)], axis=dim)
        piece = piece.reshape((-1,) + piece.shape[-2:])
        done.append(piece)
    both = []
    for piece in done:
        other = swap(piece, "fsdp", 1)
        both.append(jnp.stack([jnp.where(mine(1) == 0, piece, other), jnp.where(mine(1) == 0, other, piece)], axis=1))
    return jnp.concatenate(both, axis=3).reshape(-1, columns)


def gather_seq(values):
    index = lax.axis_index("seq")
    count = lax.axis_size("seq")
    turn = lambda step: lax.ppermute(values, "seq", [(n, (n + step) % count) for n in range(count)])
    found = jnp.stack([values] + [turn(step) for step in range(count - 1, 0, -1)])
    order = (jnp.arange(count) - index) % count
    return jnp.stack([pick_at(found, order[n], 0) for n in range(count)])


def window_blocks(rows):
    return min(lax.axis_size("seq") - 1, -(-(DOC_MAX - 1) // rows))


def gather_window(values):
    rows = values.shape[0]
    count, reach = lax.axis_size("seq"), window_blocks(values.shape[0])
    left, right = [values], [values]
    for _ in range(reach):
        left.append(shift(left[-1], "seq", 1))
        right.append(shift(right[-1], "seq", -1))
    pad = jnp.zeros(((count - 1 - reach) * rows, values.shape[1]), values.dtype)
    line = jnp.concatenate([pad] + left[:0:-1] + right + [pad], axis=0)
    return lax.dynamic_slice_in_dim(line, (count - 1 - lax.axis_index("seq")) * rows, count * rows, 0)


def scatter_window(block, reach):
    total = None
    for sign in (1, -1):
        carried = None
        for far in range(reach, 0, -1):
            term = block(sign * far)
            carried = term.astype(jnp.bfloat16) if carried is None else add_low(term, carried)
            carried = shift(carried, "seq", sign)
        total = carried.astype(jnp.float32) if total is None else total + carried.astype(jnp.float32)
    return total


CALLS = 3
eps = 1e-06
GELU_COEF = 0.044715
GELU_ROOT = math.sqrt(2.0 / math.pi)
bf16 = jnp.bfloat16
f32 = jnp.float32


def gelu_both(values):
    inner = GELU_ROOT * (values + GELU_COEF * values * values * values)
    tanh_val = jnp.tanh(inner)
    half = 0.5 * (1.0 + tanh_val)
    slope = half + 0.5 * values * (1.0 - tanh_val * tanh_val) * GELU_ROOT * (
        1.0 + 3.0 * GELU_COEF * values * values
    )
    return values * half, slope


def norm_forward(values, gain_vec):
    inverse = lax.rsqrt(jnp.mean(values * values, axis=-1, keepdims=True) + eps)
    return (values * inverse * gain_vec).astype(bf16), inverse


def norm_backward(values, inverse, gain_vec, grad_normed):
    scaled = grad_normed * gain_vec
    cubed = inverse * inverse * inverse
    grad_values = inverse * scaled - values * cubed * jnp.mean(
        scaled * values, axis=-1, keepdims=True
    )
    return grad_values, jnp.sum(grad_normed * values * inverse, axis=0)


def body(
    tokens, doc_lengths, gain_attn, query_weight, key_weight, value_weight, out_weight, bias_table,
    gain_ff, ff_in, ff_out, gain_self, self_value, self_out, gain_cross, cross_query, cross_key,
    cross_value, cross_out, gain_dff, dff_in, dff_out, enc_cot, dec_cot,
):
    seq_index = lax.axis_index("seq")
    seq_count = lax.axis_size("seq")
    own = lax.axis_index("fsdp")
    fsdp = lax.axis_size("fsdp")
    rows = tokens.shape[0]
    width = tokens.shape[1]
    group_tok = rows * seq_count
    part = query_weight.shape[0]
    buckets_part = bias_table.shape[0]
    docs = doc_lengths.shape[1]

    columns = [gain_attn, gain_ff, gain_self, gain_cross, gain_dff,
               jnp.pad(bias_table, (0, part - buckets_part))]
    small = jnp.pad(jnp.stack(columns, axis=1), ((0, 0), (0, 128 - len(columns))))
    over_fsdp = lambda piece: lax.all_gather(piece, "fsdp", axis=0, tiled=True)
    group = gather_window(tokens)
    first_weights = gather_fsdp(jnp.concatenate([query_weight, key_weight, value_weight, small], axis=1))
    second_weights = over_fsdp(jnp.concatenate([out_weight, ff_in], axis=1))
    ff_out_full = over_fsdp(ff_out)
    units = dff_out.shape[0] // seq_count
    dff_in_part = pick_at(dff_in.reshape(part, fsdp, seq_count, units), seq_index, 2).reshape(part, fsdp * units)
    dff_out_part = lax.dynamic_slice_in_dim(dff_out, seq_index * units, units, 0)
    dec_weights = over_fsdp(jnp.concatenate(
        [self_value, self_out, cross_query, cross_key, cross_value, cross_out, dff_in_part, dff_out_part], axis=1))

    query_full = first_weights[:, :width]
    kv_full = first_weights[:, width : 3 * width]
    vectors = first_weights[:, 3 * width : 3 * width + len(columns)].astype(f32)
    gain_attn_f, gain_ff_f, gain_self_f, gain_cross_f, gain_dff_f = (vectors[:, n] for n in range(5))
    table = vectors[:, 5].reshape(fsdp, part)[:, :buckets_part].reshape(HEADS, BUCKETS).astype(bf16)
    out_full = second_weights[:, :width]
    ff_in_full = second_weights[:, width:]
    self_value_full, self_out_full, cross_query_full, cross_key_full, cross_value_full, cross_out_full = (
        dec_weights[:, n * width : (n + 1) * width] for n in range(6))
    dff_in_full = dec_weights[:, 6 * width : 7 * width]
    dff_out_full = dec_weights[:, 7 * width :]

    lengths = doc_lengths[0]
    end_zero = lengths[0]
    end_one = lengths[0] + lengths[1]
    here = seq_index * rows
    info = jnp.stack([here.astype(jnp.int32), end_zero, end_one])
    local_seg = seg_of(here + jnp.arange(rows, dtype=jnp.int32), end_zero, end_one)
    starts = jnp.stack([jnp.zeros_like(end_zero), end_zero, end_one])

    group_f = group.astype(f32)
    normed_all, inverse_all = norm_forward(group_f, gain_attn_f)
    normed = lax.dynamic_slice_in_dim(normed_all, here, rows, 0)
    inverse_attn = lax.dynamic_slice_in_dim(inverse_all, here, rows, 0)
    query = nn(normed, query_full).astype(bf16)
    key = nn(normed_all, kv_full[:, :width]).astype(bf16)
    value = nn(normed_all, kv_full[:, width:]).astype(bf16)
    context, lse = attn_fwd(info, make_band(table, 1), query, key, value)
    tokens_f = tokens.astype(f32)
    middle = tokens_f + nn(context, out_full)
    normed_ff, inverse_ff = norm_forward(middle, gain_ff_f)
    pre_act = nn(normed_ff, ff_in_full)
    hidden_f, slope = gelu_both(pre_act)
    hidden = hidden_f.astype(bf16)
    enc_hidden = middle + nn(hidden, ff_out_full)
    memory = enc_hidden.astype(bf16)

    local_pick = starts[:, None] == here + jnp.arange(rows, dtype=jnp.int32)[None, :]
    first = jnp.sum(gather_seq(nn(local_pick.astype(bf16), tokens).astype(bf16)).astype(f32), axis=0)
    self_low, self_inv = norm_forward(first, gain_self_f)
    self_vals = nn(self_low, self_value_full).astype(bf16)
    state_one = first + nn(self_vals, self_out_full)
    cross_low, cross_inv = norm_forward(state_one, gain_cross_f)
    cross_q = nn(cross_low, cross_query_full).astype(bf16)
    head_of = jnp.arange(width, dtype=jnp.int32) // HEAD
    head_mask = (jnp.arange(HEADS, dtype=jnp.int32)[:, None] == head_of[None, :])[:, None, :]

    def by_head(values):
        return jnp.where(head_mask, values[None], 0).reshape(HEADS * docs, width)

    def from_heads(values):
        return jnp.sum(jnp.where(head_mask, values.reshape(HEADS, docs, width), 0), axis=0)

    probe = nt(by_head(cross_q), cross_key_full).astype(bf16)
    doc_rows = jnp.tile(jnp.arange(docs, dtype=jnp.int32), HEADS)
    in_doc = doc_rows[:, None] == local_seg[None, :]
    scores = jnp.where(in_doc, nt(probe, memory), NEG)
    top = jnp.max(scores, axis=1, keepdims=True)
    powers = jnp.where(in_doc, jnp.exp(scores - top), 0.0)
    total = jnp.sum(powers, axis=1, keepdims=True)
    mixed = nn(powers.astype(bf16), memory)
    lanes = lambda column: jnp.pad(column[:, 0], (0, 128 - HEADS * docs))
    stats = gather_seq(jnp.stack([lanes(top), lanes(total)]))
    parts = gather_seq(mixed.astype(bf16)).astype(f32)
    tops = stats[:, 0, : HEADS * docs, None]
    top_all = jnp.max(tops, axis=0)
    scale = jnp.exp(tops - top_all[None])
    total_all = jnp.sum(scale * stats[:, 1, : HEADS * docs, None], axis=0)
    mixed_f = jnp.sum(scale * parts, axis=0) / total_all
    mixed_all = mixed_f.astype(bf16)
    cross_ctx = from_heads(nn(mixed_all, cross_value_full)).astype(bf16)
    state_two = state_one + nn(cross_ctx, cross_out_full)
    ffn_low, ffn_inv = norm_forward(state_two, gain_dff_f)
    dec_hid_f, dec_slope = gelu_both(nn(ffn_low, dff_in_full))
    dec_hid = dec_hid_f.astype(bf16)

    grad_dec_pre = (dec_slope * nt(dec_cot, dff_out_full)).astype(bf16)
    halves = jnp.sum(gather_seq(jnp.concatenate([nn(dec_hid, dff_out_full), nt(grad_dec_pre, dff_in_full)])), axis=0)
    dec_hidden = state_two + halves[:docs]
    back_values, grad_gain_dff = norm_backward(state_two, ffn_inv, gain_dff_f, halves[docs:])
    grad_two = dec_cot.astype(f32) + back_values
    grad_two_low = grad_two.astype(bf16)
    grad_cross_ctx = nt(grad_two_low, cross_out_full).astype(bf16)
    pull = nt(by_head(grad_cross_ctx), cross_value_full).astype(bf16)
    probs = powers * (jnp.exp(top - top_all) / total_all)
    row_dot = jnp.sum(mixed_f * pull.astype(f32), axis=1, keepdims=True)
    grad_scores = (probs * (nt(pull, memory) - row_dot)).astype(bf16)
    grad_memory = tn(jnp.concatenate([grad_scores, probs.astype(bf16)], axis=0),
                     jnp.concatenate([probe, pull], axis=0))
    grad_mixed = jnp.sum(gather_seq(nn(grad_scores, memory).astype(bf16)).astype(f32), axis=0).astype(bf16)
    grad_cross_q = from_heads(nn(grad_mixed, cross_key_full)).astype(bf16)
    back_values, grad_gain_cross = norm_backward(state_one, cross_inv, gain_cross_f, nt(grad_cross_q, cross_query_full))
    grad_one = grad_two + back_values
    grad_one_low = grad_one.astype(bf16)
    grad_self_vals = nt(grad_one_low, self_out_full).astype(bf16)
    back_values, grad_gain_self = norm_backward(first, self_inv, gain_self_f, nt(grad_self_vals, self_value_full))
    grad_first = grad_one + back_values

    gains_rows = jnp.stack([grad_gain_self, grad_gain_cross, grad_gain_dff]).astype(bf16)
    pack = [self_low, grad_self_vals, self_vals, grad_one_low, cross_low, grad_cross_q, cross_q, grad_cross_ctx,
            cross_ctx, grad_two_low, ffn_low, dec_cot, gains_rows]
    both = gather_seq(jnp.concatenate([dec_hid, grad_dec_pre])).reshape(seq_count, 2, docs, fsdp, units)
    both = both.transpose(1, 2, 3, 0, 4).reshape(2, docs, fsdp * seq_count * units)
    wide = both.shape[2] // width
    pack += [both[0, :, n * width : (n + 1) * width] for n in range(wide)]
    pack += [both[1, :, n * width : (n + 1) * width] for n in range(wide)]
    pack += [grad_mixed, mixed_all]
    pack = jnp.concatenate(pack, axis=0)
    pack = jnp.pad(pack, ((0, -pack.shape[0] % 16), (0, 0)))
    packs = lax.all_gather(pack, "fsdp", axis=0)
    rowset = lambda n: packs[:, n * docs : (n + 1) * docs].reshape(fsdp * docs, width)
    mine = lambda values: lax.dynamic_slice_in_dim(values, own * part, part, 1)
    shard_self_value = tn(mine(rowset(0)), rowset(1))
    shard_self_out = tn(mine(rowset(2)), rowset(3))
    shard_cross_query = tn(mine(rowset(4)), rowset(5))
    shard_cross_out = tn(mine(rowset(8)), rowset(9))
    at = 13
    hid_all = jnp.concatenate([rowset(at + n) for n in range(wide)], axis=1)
    pre_all = jnp.concatenate([rowset(at + wide + n) for n in range(wide)], axis=1)
    shard_dff_in = tn(mine(rowset(10)), pre_all)
    part_ff = dff_out.shape[0]
    shard_dff_out = tn(lax.dynamic_slice_in_dim(hid_all, own * part_ff, part_ff, 1), rowset(11))
    gains_all = jnp.sum(packs[:, 12 * docs : 13 * docs].astype(f32), axis=0)
    gains_own = mine(gains_all)
    at = (13 + 2 * wide) * docs
    heads_rows = HEADS * docs
    mixed_g = packs[:, at : at + heads_rows].reshape(fsdp * heads_rows, width)
    mixed_m = packs[:, at + heads_rows : at + 2 * heads_rows].reshape(fsdp * heads_rows, width)
    spread = lambda n: jnp.where(head_mask[None], packs[:, None, n * docs : (n + 1) * docs], 0).reshape(
        fsdp * heads_rows, width)
    shard_cross_key = tn(mine(mixed_g), spread(6))
    shard_cross_value = tn(mine(mixed_m), spread(7))

    grad_enc = enc_cot.astype(f32) + grad_memory
    grad_enc_low = grad_enc.astype(bf16)
    ff_out_pieces = scatter_fsdp(tn(hidden, grad_enc_low).astype(bf16))
    shard_ff_out = jnp.concatenate([sum_seq(piece, 0) for piece in ff_out_pieces], axis=1).astype(f32)
    grad_pre = (slope * nt(grad_enc_low, ff_out_full)).astype(bf16)
    ff_in_pieces = scatter_fsdp(tn(normed_ff, grad_pre).astype(bf16))
    shard_ff_in = jnp.concatenate([sum_seq(piece, 1) for piece in ff_in_pieces], axis=1).astype(f32)
    back_values, grad_gain_ff = norm_backward(middle, inverse_ff, gain_ff_f, nt(grad_pre, ff_in_full))
    grad_middle = grad_enc + back_values
    grad_middle_low = grad_middle.astype(bf16)
    grad_out = tn(context, grad_middle_low)
    grad_context = nt(grad_middle_low, out_full).astype(bf16)
    band = make_band(table, -1)
    grads = None
    pairs = HEADS // 2
    for call in range(CALLS):
        grads = attn_bwd(info, band, query, key, value, grad_context, context, lse,
                         call * pairs // CALLS, pairs // CALLS, grads)
    grad_query, grad_key, grad_value, grad_band, grad_far = grads
    grad_table = table_grad(grad_band, grad_far).reshape(fsdp, buckets_part)
    reach = window_blocks(rows)
    terms = {}

    def term(step):
        at = (seq_index + step) * rows
        block = lambda values: lax.dynamic_slice_in_dim(values, at, rows, 0)
        here_term = nt(block(grad_key), kv_full[:, :width]) + nt(block(grad_value), kv_full[:, width:])
        if step == 0:
            here_term = here_term + nt(grad_query, query_full)
        inside = (seq_index + step >= 0) & (seq_index + step < seq_count)
        gain_part = jnp.sum(here_term * block(group_f) * block(inverse_all), axis=0)
        terms[step] = jnp.where(inside, gain_part, 0.0)
        return here_term

    far_terms = scatter_window(term, reach)
    grad_normed = term(0) + far_terms
    back_values, _ = norm_backward(tokens_f, inverse_attn, gain_attn_f, grad_normed)
    grad_gain_attn = sum(terms.values())
    first_back = lax.dot_general(local_pick.astype(f32), grad_first, (((0,), (0,)), ((), ())),
                                 precision=lax.Precision.HIGHEST, preferred_element_type=f32)
    tokens_grad = grad_middle + back_values + first_back
    small_grads = [grad_gain_attn, grad_gain_ff,
                   jnp.pad(grad_table, ((0, 0), (0, part - buckets_part))).reshape(width)]
    small_grads = jnp.pad(jnp.stack(small_grads, axis=1), ((0, 0), (0, 125)))
    last = scatter_fsdp(jnp.concatenate([
        tn(normed, grad_query).astype(bf16), tn(normed_all, grad_key).astype(bf16),
        tn(normed_all, grad_value).astype(bf16), grad_out.astype(bf16), small_grads.astype(bf16)], axis=1))
    last = jnp.concatenate([sum_seq(piece, 1) for piece in last], axis=1).astype(f32)
    shard_query, shard_key, shard_value, shard_out = (last[:, n * width : (n + 1) * width] for n in range(4))
    tail = last[:, 4 * width :]
    return (
        enc_hidden, dec_hidden, tokens_grad, tail[:, 0], shard_query, shard_key, shard_value, shard_out,
        tail[:buckets_part, 2], tail[:, 1], shard_ff_in, shard_ff_out, gains_own[0], shard_self_value, shard_self_out,
        gains_own[1], shard_cross_query, shard_cross_key, shard_cross_value, shard_cross_out, gains_own[2],
        shard_dff_in, shard_dff_out,
    )


def solution(mesh):
    tok, wide, one = P(("fsdp", "seq"), None), P("fsdp", None), P("fsdp")
    return jax.shard_map(
        body,
        mesh=mesh,
        in_specs=(tok, wide, one, wide, wide, wide, wide, one, one, wide, wide, one, wide, wide, one, wide, wide, wide,
                  wide, one, wide, wide, tok, wide),
        out_specs=(tok, wide, tok, one, wide, wide, wide, wide, one, one, wide, wide, one, wide, wide, one, wide, wide,
                   wide, wide, one, wide, wide),
        check_vma=False,
    )
```

```python
import functools, math
import jax, jax.numpy as jnp
from jax import lax
from jax.experimental import pallas as pl
from jax.experimental.pallas import tpu as pltpu
from jax.sharding import PartitionSpec as P

HEADS=12; HEAD=64; BUCKETS=32
LIMITS = (12, 16, 23, 32, 46, 64, 91)
BLK=256
SUB=128
BAND=512
NEG=-1e30

def bucket_of(relative):
    distance = jnp.abs(relative)
    bucket = jnp.minimum(distance, 8)
    for bound_value in LIMITS:
        bucket = bucket + (distance >= bound_value).astype(jnp.int32)
    return bucket + 16 * (relative > 0).astype(jnp.int32)

def nt(a,b):
    return lax.dot_general(a,b,(((1,),(1,)),((),())),preferred_element_type=jnp.float32)
def tn(a,b):
    return lax.dot_general(a,b,(((0,),(0,)),((),())),preferred_element_type=jnp.float32)
def nn(a,b):
    return lax.dot_general(a,b,(((1,),(0,)),((),())),preferred_element_type=jnp.float32)

def band_offsets(sign):
    c = jnp.arange(BAND, dtype=jnp.int32)
    t = jnp.where(c < 3*SUB, c, c - BAND) - SUB
    return sign * t

def seg_of(pos, e0, e1):
    return (pos >= e0).astype(jnp.int32) + (pos >= e1).astype(jnp.int32)

def build_tiles(band_ref, tiles, hh, flip):
    row = band_ref[hh:hh+1, :]
    x = jnp.broadcast_to(row, (SUB, BAND))
    x = pltpu.roll(x, 0, 1, stride=1, stride_axis=0)
    last, first = row[0:1, 3*SUB-1:3*SUB], row[0:1, 3*SUB:3*SUB+1]
    near = [x[:, n*SUB:(n+1)*SUB] for n in range(3)]
    if flip:
        near = near[::-1]
        last, first = first, last
    low = jnp.broadcast_to(first, (SUB, SUB))
    high = jnp.broadcast_to(last, (SUB, SUB))
    for d in range(5):
        for r in range(2):
            for c in range(2):
                off = ((r - c) if flip else (c - r)) + 2*(d-2)
                tiles[hh, d, r*SUB:(r+1)*SUB, c*SUB:(c+1)*SUB] = low if off < -1 else high if off > 1 else near[off+1]

def fwd_kernel(info, band_ref, q_ref, k_ref, v_ref, ctx_ref, lse_ref, tiles, s_scr):
    p0, e0, e1 = info[0], info[1], info[2]
    T = q_ref.shape[0]; G = k_ref.shape[0]
    lane = lax.broadcasted_iota(jnp.int32, (1,128), 1)
    left = lane < HEAD
    for hh in range(2):
        build_tiles(band_ref, tiles, hh, False)
    for i in range(T//BLK):
        a = p0 + i*BLK; b = a + BLK - 1
        lo = jnp.where(a >= e1, e1, jnp.where(a >= e0, e0, 0))
        hi = jnp.where(b >= e1, G, jnp.where(b >= e0, e1, e0))
        j0 = lo // BLK; j1 = (hi + BLK - 1)//BLK
        ib = a // BLK
        qb = q_ref[i*BLK:(i+1)*BLK, :]
        row_pos = a + lax.broadcasted_iota(jnp.int32, (BLK,1), 0)
        row_seg = jnp.broadcast_to(seg_of(row_pos, e0, e1),(BLK,128))
        zero = jnp.zeros_like(qb)
        qh = [jnp.where(left, qb, zero), jnp.where(left, zero, qb)]
        def score(j, carry):
            koff = pl.multiple_of(lax.rem(j*BLK + G - p0, G), BLK)
            kb = k_ref[pl.ds(koff, BLK), :]
            kpos = j*BLK + lax.broadcasted_iota(jnp.int32, (1,BLK), 1)
            kseg = seg_of(kpos, e0, e1)
            same = jnp.concatenate([row_seg == kseg[:, :128], row_seg == kseg[:,128:]],axis=1)
            d = jnp.clip(j - ib, -2, 2) + 2
            out = []
            for hh in range(2):
                s = nt(qh[hh], kb) + tiles[hh, d]
                s = jnp.where(same, s, NEG)
                s_scr[hh, j] = s
                out.append(jnp.maximum(carry[hh], jnp.maximum(s[:, :128], s[:, 128:])))
            return tuple(out)
        init = jnp.full((BLK,128), NEG, jnp.float32)
        mx = lax.fori_loop(j0, j1, score, (init, init))
        top = [jnp.max(m, axis=1, keepdims=True) for m in mx]
        def weigh(j, carry):
            koff = pl.multiple_of(lax.rem(j*BLK + G - p0, G), BLK)
            vb = v_ref[pl.ds(koff, BLK), :]
            one = jnp.ones_like(vb)
            vh = [jnp.where(left, vb, one), jnp.where(left, one, vb)]
            out = []
            for hh in range(2):
                p = jnp.exp(s_scr[hh, j] - top[hh]).astype(jnp.bfloat16)
                out.append(carry[hh] + nn(p, vh[hh]))
            return tuple(out)
        zf = jnp.zeros((BLK,128), jnp.float32)
        acc = lax.fori_loop(j0, j1, weigh, (zf, zf))
        tot = [jnp.where(left, pltpu.roll(acc[0], HEAD, 1), pltpu.roll(acc[1], HEAD, 1))]
        num = jnp.where(left, acc[0], acc[1])
        total = tot[0]
        ctx_ref[i*BLK:(i+1)*BLK, :] = (num / total).astype(jnp.bfloat16)
        lse_ref[i*BLK:(i+1)*BLK, :] = jnp.where(left, top[0], top[1]) + jnp.log(total)

def attn_fwd(info, band, q, k, v):
    T=q.shape[0]; G=k.shape[0]; W=q.shape[1]
    pairs=W//128
    return pl.pallas_call(
        fwd_kernel,
        grid=(pairs,),
        in_specs=[pl.BlockSpec(memory_space=pltpu.SMEM),
                  pl.BlockSpec((None,2,BAND), lambda p:(p,0,0)),
                  pl.BlockSpec((T,128), lambda p:(0,p)),
                  pl.BlockSpec((G,128), lambda p:(0,p)),
                  pl.BlockSpec((G,128), lambda p:(0,p))],
        out_specs=[pl.BlockSpec((T,128), lambda p:(0,p)), pl.BlockSpec((T,128), lambda p:(0,p))],
        out_shape=[jax.ShapeDtypeStruct((T,W), jnp.bfloat16), jax.ShapeDtypeStruct((T,W), jnp.float32)],
        scratch_shapes=[pltpu.VMEM((2,5,BLK,BLK), jnp.float32), pltpu.VMEM((2,G//BLK,BLK,BLK), jnp.float32)],
        compiler_params=pltpu.CompilerParams(vmem_limit_bytes=24<<20),
        cost_estimate=pl.CostEstimate(flops=4*HEADS*T*1280*128, bytes_accessed=4*G*W+8*T*W, transcendentals=HEADS*T*1280),
    )(info, band, q, k, v)

def bwd_kernel(info, band_ref, q_ref, k_ref, v_ref, g_ref, ctx_ref, lse_ref, gq_ref, gk_ref, gv_ref, gb_ref, gf_ref, tiles, gt, gk_acc, gv_acc):
    p0, e0, e1 = info[0], info[1], info[2]
    T = q_ref.shape[0]; G = k_ref.shape[0]
    lane = lax.broadcasted_iota(jnp.int32, (1,128), 1)
    left = lane < HEAD
    sub_left = lax.broadcasted_iota(jnp.int32, (128,1), 0) < HEAD
    for hh in range(2):
        build_tiles(band_ref, tiles, hh, True)
    gt[...] = jnp.zeros_like(gt)
    gk_acc[...] = jnp.zeros_like(gk_acc)
    gv_acc[...] = jnp.zeros_like(gv_acc)
    for i in range(T//BLK):
        a = p0 + i*BLK; b = a + BLK - 1
        lo = jnp.where(a >= e1, e1, jnp.where(a >= e0, e0, 0))
        hi = jnp.where(b >= e1, G, jnp.where(b >= e0, e1, e0))
        j0 = lo // BLK; j1 = (hi + BLK - 1)//BLK
        ib = a // BLK
        rows = slice(i*BLK,(i+1)*BLK)
        qb = q_ref[rows, :]; gb = g_ref[rows, :]
        zero = jnp.zeros_like(qb)
        qh = [jnp.where(left, qb, zero), jnp.where(left, zero, qb)]
        gh = [jnp.where(left, gb, zero), jnp.where(left, zero, gb)]
        prod = (gb.astype(jnp.float32) * ctx_ref[rows,:].astype(jnp.float32)).T
        lse_t = lse_ref[rows,:].T
        dot = [jnp.sum(prod[hh*HEAD:(hh+1)*HEAD], axis=0, keepdims=True) for hh in range(2)]
        lse = [lse_t[hh*HEAD:hh*HEAD+1] for hh in range(2)]
        q_pos = a + lax.broadcasted_iota(jnp.int32, (1,BLK), 1)
        q_seg = seg_of(q_pos, e0, e1)
        def step(j, carry):
            koff = pl.multiple_of(lax.rem(j*BLK + G - p0, G), BLK)
            kb = k_ref[pl.ds(koff, BLK), :]
            vb = v_ref[pl.ds(koff, BLK), :]
            kpos = j*BLK + lax.broadcasted_iota(jnp.int32, (BLK,1), 0)
            same = jnp.broadcast_to(seg_of(kpos, e0, e1), (BLK,BLK)) == jnp.broadcast_to(q_seg, (BLK,BLK))
            d = jnp.clip(j - ib, -2, 2) + 2
            gqs=[]
            gk = None; gv=None
            for hh in range(2):
                s = nt(kb, qh[hh]) + tiles[hh, d]
                s = jnp.where(same, s, NEG)
                p = jnp.exp(s - lse[hh])
                gp = nt(vb, gh[hh])
                gs = p * (gp - dot[hh])
                gt[hh, d] += gs
                pb = p.astype(jnp.bfloat16); gsb = gs.astype(jnp.bfloat16)
                tk = nn(gsb, qh[hh]); tv = nn(pb, gh[hh])
                gk = tk if gk is None else gk + tk
                gv = tv if gv is None else gv + tv
                gqs.append(carry[hh] + tn(gsb, kb))
            gk_acc[pl.ds(koff,BLK), :] += gk
            gv_acc[pl.ds(koff,BLK), :] += gv
            return tuple(gqs)
        zf = jnp.zeros((BLK,128), jnp.float32)
        gq = lax.fori_loop(j0, j1, step, (zf, zf))
        gq_ref[rows,:] = jnp.where(left, gq[0], gq[1]).astype(jnp.bfloat16)
    gk_ref[...] = gk_acc[...].astype(jnp.bfloat16)
    gv_ref[...] = gv_acc[...].astype(jnp.bfloat16)
    for hh in range(2):
        near = [None]*3; low = None; high = None
        for d in range(5):
            for r in range(2):
                for c in range(2):
                    off = r - c + 2*(d-2)
                    x = gt[hh, d, r*SUB:(r+1)*SUB, c*SUB:(c+1)*SUB]
                    if off < -1: low = x if low is None else low + x
                    elif off > 1: high = x if high is None else high + x
                    else: near[off+1] = x if near[off+1] is None else near[off+1] + x
        x = jnp.concatenate([near[2], near[1], near[0], jnp.zeros((SUB,SUB),jnp.float32)], axis=1)
        rows_left = SUB
        while rows_left > 1:
            rows_left //= 2
            x = x[:rows_left] + pltpu.roll(x[rows_left:], BAND - rows_left, 1)
        gb_ref[hh:hh+1,:] = x
        gf_ref[hh:hh+1,:] = jnp.concatenate([jnp.sum(low, axis=0, keepdims=True), jnp.sum(high, axis=0, keepdims=True)], axis=1)

def attn_bwd(info, band, q, k, v, g, ctx, lse, first_pair, count, into):
    T=q.shape[0]; G=k.shape[0]; W=q.shape[1]
    at = lambda rows: pl.BlockSpec((rows,128), lambda p:(0,p+first_pair))
    kernel = bwd_kernel
    if into is not None:
        kernel = lambda *refs: bwd_kernel(*refs[:8], *refs[13:])
    extra = [] if into is None else list(into)
    small = lambda n: pl.BlockSpec((None,2,n), lambda p:(p+first_pair,0,0))
    pairs=W//128
    return pl.pallas_call(
        kernel,
        grid=(count,),
        in_specs=[pl.BlockSpec(memory_space=pltpu.SMEM), small(BAND),
                  at(T), at(G), at(G), at(T), at(T), at(T)] + [pl.BlockSpec(memory_space=pl.ANY)]*len(extra),
        out_specs=[at(T), at(G), at(G), small(BAND), small(2*SUB)],
        out_shape=[jax.ShapeDtypeStruct((T,W), jnp.bfloat16), jax.ShapeDtypeStruct((G,W), jnp.bfloat16), jax.ShapeDtypeStruct((G,W), jnp.bfloat16),
                   jax.ShapeDtypeStruct((pairs,2,BAND), jnp.float32), jax.ShapeDtypeStruct((pairs,2,2*SUB), jnp.float32)],
        scratch_shapes=[pltpu.VMEM((2,5,BLK,BLK), jnp.float32), pltpu.VMEM((2,5,BLK,BLK), jnp.float32),
                        pltpu.VMEM((G,128), jnp.float32), pltpu.VMEM((G,128), jnp.float32)],
        input_output_aliases={8+n: n for n in range(len(extra))},
        compiler_params=pltpu.CompilerParams(vmem_limit_bytes=24<<20),
        cost_estimate=pl.CostEstimate(flops=count*10*2*T*1280*128*4, bytes_accessed=(8*G*W+12*T*W)*count//pairs, transcendentals=2*count*T*1280),
    )(info, band, q, k, v, g, ctx, lse, *extra)

def make_band(table, sign):
    off = band_offsets(sign)
    oh = (bucket_of(off)[None,:] == jnp.arange(BUCKETS, dtype=jnp.int32)[:,None]).astype(jnp.bfloat16)
    return jnp.dot(table, oh, preferred_element_type=jnp.float32).reshape(HEADS//2, 2, BAND)

def table_grad(gb, gf):
    oh = (bucket_of(band_offsets(-1))[:,None] == jnp.arange(BUCKETS, dtype=jnp.int32)[None,:]).astype(jnp.float32)
    t = jnp.dot(gb.reshape(HEADS,BAND), oh, precision=lax.Precision.HIGHEST)
    f = gf.reshape(HEADS, 2, SUB).sum(axis=2)
    return t.at[:,15].add(f[:,0]).at[:,31].add(f[:,1])


DOC_MAX = 1024


def swap(values, axis, bit):
    count = lax.axis_size(axis)
    return lax.ppermute(values, axis, [(n, n ^ bit) for n in range(count)])


def shift(values, axis, step):
    count = lax.axis_size(axis)
    return lax.ppermute(values, axis, [(n, n + step) for n in range(count) if 0 <= n + step < count])


def bits_of(axis):
    bits = []
    while 1 << len(bits) < lax.axis_size(axis):
        bits.append(1 << len(bits))
    return bits


def pick_at(values, index, dim):
    return lax.dynamic_index_in_dim(values, index, dim, keepdims=False)


def add_low(left, right):
    return (left.astype(jnp.float32) + right.astype(jnp.float32)).astype(jnp.bfloat16)


def scatter_core(pieces):
    index = lax.axis_index("fsdp")
    core = index % 2
    halves = [piece.reshape((piece.shape[0] // 2, 2) + piece.shape[1:]) for piece in pieces]
    send = jnp.concatenate([pick_at(half, 1 - core, 1) for half in halves], axis=2)
    keep = jnp.concatenate([pick_at(half, core, 1) for half in halves], axis=2)
    return add_low(keep, swap(send, "fsdp", 1))


def scatter_chips(piece):
    index = lax.axis_index("fsdp") // 2
    done = 2
    while piece.shape[0] > 1:
        step = min(4, piece.shape[0])
        piece = piece.reshape((piece.shape[0] // step, step) + piece.shape[1:])
        place = index % step
        total = pick_at(piece, place, 1).astype(jnp.float32)
        for other in range(1, step):
            total = total + swap(pick_at(piece, place ^ other, 1), "fsdp", other * done).astype(jnp.float32)
        piece = total.astype(jnp.bfloat16)
        index = index // step
        done = done * step
    return piece[0]


def halve_seq(piece, bit, dim):
    mine = lax.axis_index("seq") // bit % 2
    low, high = jnp.split(piece, 2, axis=dim)
    return add_low(jnp.where(mine == 0, low, high), swap(jnp.where(mine == 0, high, low), "seq", bit))


def whole_seq(pieces, dims, width):
    index = lax.axis_index("seq")
    for bit in bits_of("seq")[::-1]:
        mine = index // bit % 2
        shapes = [piece.shape for piece in pieces]
        flat = [jnp.concatenate(jnp.split(piece, piece.shape[1] // width, axis=1), axis=0) for piece in pieces]
        come = swap(jnp.concatenate(flat, axis=0), "seq", bit)
        at = 0
        for n, (shape, dim) in enumerate(zip(shapes, dims)):
            rows = flat[n].shape[0]
            other = come[at : at + rows]
            at += rows
            other = jnp.concatenate(jnp.split(other, shape[1] // width, axis=0), axis=1)
            pieces[n] = jnp.concatenate([jnp.where(mine == 0, pieces[n], other), jnp.where(mine == 0, other, pieces[n])], axis=dim)
    return pieces


def sum_seq(piece, dim):
    for bit in bits_of("seq"):
        piece = halve_seq(piece, bit, dim)
    return whole_seq([piece], [dim], piece.shape[1])[0]


def gather_seq(values):
    index = lax.axis_index("seq")
    count = lax.axis_size("seq")
    turn = lambda step: lax.ppermute(values, "seq", [(n, (n + step) % count) for n in range(count)])
    found = jnp.stack([values] + [turn(step) for step in range(count - 1, 0, -1)])
    order = (jnp.arange(count) - index) % count
    return jnp.stack([pick_at(found, order[n], 0) for n in range(count)])


def window_blocks(rows):
    return min(lax.axis_size("seq") - 1, -(-(DOC_MAX - 1) // rows))


def gather_window(values, beside):
    rows = values.shape[0]
    count, reach = lax.axis_size("seq"), window_blocks(rows)
    left, right = [values], [values]
    for far in range(reach):
        left.append(shift(left[-1], "seq", 1))
        right.append(shift(right[-1], "seq", -1))
        if far == 0:
            left[1], right[1], beside = lax.optimization_barrier((left[1], right[1], beside))
    slots = [values]
    for place in range(1, count):
        found = [right[place]] if place <= reach else []
        found += [left[count - place]] if count - place <= reach else []
        slots.append(sum(found[1:], found[0]) if found else jnp.zeros_like(values))
    return jnp.concatenate(slots, axis=0), beside


def scatter_window(block, reach):
    total = None
    carried = {}
    for far in range(reach, 0, -1):
        for sign in (1, -1):
            term = block(sign * far)
            moving = term.astype(jnp.bfloat16) if far == reach else add_low(term, carried[sign])
            carried[sign] = shift(moving, "seq", sign)
    return carried[1].astype(jnp.float32) + carried[-1].astype(jnp.float32)


eps = 1e-06
GELU_COEF = 0.044715
GELU_ROOT = math.sqrt(2.0 / math.pi)
bf16 = jnp.bfloat16
f32 = jnp.float32


def gelu_both(values):
    inner = GELU_ROOT * (values + GELU_COEF * values * values * values)
    tanh_val = jnp.tanh(inner)
    half = 0.5 * (1.0 + tanh_val)
    slope = half + 0.5 * values * (1.0 - tanh_val * tanh_val) * GELU_ROOT * (
        1.0 + 3.0 * GELU_COEF * values * values
    )
    return values * half, slope


def norm_forward(values, gain_vec):
    inverse = lax.rsqrt(jnp.mean(values * values, axis=-1, keepdims=True) + eps)
    return (values * inverse * gain_vec).astype(bf16), inverse


def norm_backward(values, inverse, gain_vec, grad_normed):
    scaled = grad_normed * gain_vec
    cubed = inverse * inverse * inverse
    grad_values = inverse * scaled - values * cubed * jnp.mean(
        scaled * values, axis=-1, keepdims=True
    )
    return grad_values


def body(
    tokens, doc_lengths, gain_attn, query_weight, key_weight, value_weight, out_weight, bias_table,
    gain_ff, ff_in, ff_out, gain_self, self_value, self_out, gain_cross, cross_query, cross_key,
    cross_value, cross_out, gain_dff, dff_in, dff_out, enc_cot, dec_cot,
):
    seq_index = lax.axis_index("seq")
    seq_count = lax.axis_size("seq")
    own = lax.axis_index("fsdp")
    fsdp = lax.axis_size("fsdp")
    rows = tokens.shape[0]
    width = tokens.shape[1]
    group_tok = rows * seq_count
    part = query_weight.shape[0]
    buckets_part = bias_table.shape[0]
    docs = doc_lengths.shape[1]

    columns = [gain_attn, gain_ff, gain_self, gain_cross, gain_dff,
               jnp.pad(bias_table, (0, part - buckets_part))]
    small = jnp.pad(jnp.stack(columns, axis=1), ((0, 0), (0, 128 - len(columns))))
    over_fsdp = lambda pieces: lax.all_gather(jnp.concatenate(pieces, axis=1), "fsdp", axis=0, tiled=True)
    held = (out_weight, ff_in, self_value, self_out, cross_query, cross_key, cross_value, cross_out, dff_in)
    group, held = gather_window(tokens, held)
    first_weights = over_fsdp([query_weight, key_weight, value_weight, small])
    out_weight_b, ff_in_b, self_value_b, self_out_b, cross_query_b, cross_key_b, cross_value_b, cross_out_b, dff_in_b = held
    wide = dff_out.shape[0] // part
    units = dff_out.shape[0] // seq_count
    dff_in_part = pick_at(dff_in_b.reshape(part, fsdp, seq_count, units), seq_index, 2).reshape(part, fsdp * units)
    dff_out_part = lax.dynamic_slice_in_dim(dff_out, seq_index * units, units, 0)
    second_weights = over_fsdp([out_weight_b, ff_in_b, self_value_b, self_out_b, cross_query_b, cross_key_b])
    ff_out_full = over_fsdp([ff_out])
    third_weights = over_fsdp([cross_value_b, cross_out_b, dff_in_part, dff_out_part])

    query_full = first_weights[:, :width]
    kv_full = first_weights[:, width : 3 * width]
    vectors = first_weights[:, 3 * width : 3 * width + len(columns)].astype(f32)
    gain_attn_f, gain_ff_f, gain_self_f, gain_cross_f, gain_dff_f = (vectors[:, n] for n in range(5))
    table = vectors[:, 5].reshape(fsdp, part)[:, :buckets_part].reshape(HEADS, BUCKETS).astype(bf16)
    span = lambda start, count: second_weights[:, start * width : (start + count) * width]
    out_full = span(0, 1)
    ff_in_full = span(1, wide)
    self_value_full, self_out_full, cross_query_full, cross_key_full = (span(1 + wide + n, 1) for n in range(4))
    cross_value_full, cross_out_full, dff_in_full, dff_out_full = (
        third_weights[:, n * width : (n + 1) * width] for n in range(4))
    lengths = doc_lengths[0]
    end_zero = lengths[0]
    end_one = lengths[0] + lengths[1]
    here = seq_index * rows
    info = jnp.stack([here.astype(jnp.int32), end_zero, end_one])
    local_seg = seg_of(here + jnp.arange(rows, dtype=jnp.int32), end_zero, end_one)
    starts = jnp.stack([jnp.zeros_like(end_zero), end_zero, end_one])

    tokens_f = tokens.astype(f32)
    normed_all, inverse_all = norm_forward(group.astype(f32), gain_attn_f)
    normed, inverse_attn = normed_all[:rows], inverse_all[:rows]
    query = nn(normed, query_full).astype(bf16)
    key = nn(normed_all, kv_full[:, :width]).astype(bf16)
    value = nn(normed_all, kv_full[:, width:]).astype(bf16)
    context, lse = attn_fwd(info, make_band(table, 1), query, key, value)
    middle = tokens_f + nn(context, out_full)
    normed_ff, inverse_ff = norm_forward(middle, gain_ff_f)
    pre_act = nn(normed_ff, ff_in_full)
    hidden_f, slope = gelu_both(pre_act)
    hidden = hidden_f.astype(bf16)
    enc_hidden = middle + nn(hidden, ff_out_full)
    memory = enc_hidden.astype(bf16)

    local_pick = starts[:, None] == here + jnp.arange(rows, dtype=jnp.int32)[None, :]
    first = jnp.sum(gather_seq(nn(local_pick.astype(bf16), tokens).astype(bf16)).astype(f32), axis=0)
    self_low, self_inv = norm_forward(first, gain_self_f)
    self_vals = nn(self_low, self_value_full).astype(bf16)
    state_one = first + nn(self_vals, self_out_full)
    cross_low, cross_inv = norm_forward(state_one, gain_cross_f)
    cross_q = nn(cross_low, cross_query_full).astype(bf16)
    head_of = jnp.arange(width, dtype=jnp.int32) // HEAD
    head_rows = -(-HEADS // 8) * 8
    head_mask = (jnp.arange(head_rows, dtype=jnp.int32)[:, None] == head_of[None, :])[None]

    def by_head(values):
        return jnp.where(head_mask, values[:, None, :], 0).reshape(-1, width)

    def from_heads(values):
        return jnp.sum(jnp.where(head_mask, values.reshape(docs, head_rows, width), 0), axis=1)

    probe = nt(by_head(cross_q), cross_key_full).astype(bf16)
    doc_rows = jnp.repeat(jnp.arange(docs, dtype=jnp.int32), head_rows)
    in_doc = doc_rows[:, None] == local_seg[None, :]
    scores = jnp.where(in_doc, nt(probe, memory), NEG)
    top = jnp.max(scores, axis=1, keepdims=True)
    powers = jnp.where(in_doc, jnp.exp(scores - top), 0.0)
    total = jnp.sum(powers, axis=1, keepdims=True)
    mixed = nn(powers.astype(bf16), memory)
    stat_lanes = jnp.where(jnp.arange(128, dtype=jnp.int32)[None, :] == 0, top, total)
    parts = gather_seq(jnp.concatenate([mixed, stat_lanes], axis=1))
    tops = parts[:, :, width : width + 1]
    top_all = jnp.max(tops, axis=0)
    scale = jnp.exp(tops - top_all[None])
    total_all = jnp.sum(scale * parts[:, :, width + 1 : width + 2], axis=0)
    mixed_f = jnp.sum(scale * parts[:, :, :width], axis=0) / total_all
    mixed_all = mixed_f.astype(bf16)
    cross_ctx = from_heads(nn(mixed_all, cross_value_full)).astype(bf16)
    state_two = state_one + nn(cross_ctx, cross_out_full)
    ffn_low, ffn_inv = norm_forward(state_two, gain_dff_f)
    dec_hid_f, dec_slope = gelu_both(nn(ffn_low, dff_in_full))
    dec_hid = dec_hid_f.astype(bf16)

    grad_dec_pre = (dec_slope * nt(dec_cot, dff_out_full)).astype(bf16)
    halves = jnp.sum(gather_seq(jnp.concatenate([nn(dec_hid, dff_out_full), nt(grad_dec_pre, dff_in_full)])), axis=0)
    dec_hidden = state_two + halves[:docs]
    back_values = norm_backward(state_two, ffn_inv, gain_dff_f, halves[docs:])
    grad_two = dec_cot.astype(f32) + back_values
    grad_two_low = grad_two.astype(bf16)
    grad_cross_ctx = nt(grad_two_low, cross_out_full).astype(bf16)
    pull = nt(by_head(grad_cross_ctx), cross_value_full).astype(bf16)
    probs = powers * (jnp.exp(top - top_all) / total_all)
    row_dot = jnp.sum(mixed_f * pull.astype(f32), axis=1, keepdims=True)
    grad_scores = (probs * (nt(pull, memory) - row_dot)).astype(bf16)
    grad_memory = tn(jnp.concatenate([grad_scores, probs.astype(bf16)], axis=0),
                     jnp.concatenate([probe, pull], axis=0))
    grad_mixed = jnp.sum(gather_seq(nn(grad_scores, memory).astype(bf16)).astype(f32), axis=0).astype(bf16)
    grad_cross_q = from_heads(nn(grad_mixed, cross_key_full)).astype(bf16)
    back_values = norm_backward(state_one, cross_inv, gain_cross_f, nt(grad_cross_q, cross_query_full))
    grad_one = grad_two + back_values
    grad_one_low = grad_one.astype(bf16)
    grad_self_vals = nt(grad_one_low, self_out_full).astype(bf16)
    back_values = norm_backward(first, self_inv, gain_self_f, nt(grad_self_vals, self_value_full))
    grad_first = grad_one + back_values

    both = gather_seq(jnp.concatenate([dec_hid, grad_dec_pre])).reshape(seq_count, 2, docs, fsdp, units)
    both = both.transpose(1, 2, 3, 0, 4).reshape(2, docs, fsdp * seq_count * units)
    pack = [self_low, grad_self_vals, self_vals, grad_one_low, cross_low, grad_cross_q, cross_q, grad_cross_ctx,
            cross_ctx, grad_two_low, ffn_low, dec_cot]
    pack += [both[0, :, n * width : (n + 1) * width] for n in range(wide)]
    pack += [both[1, :, n * width : (n + 1) * width] for n in range(wide)]
    tile = 8
    pack = [jnp.pad(rows_of, ((0, tile - docs), (0, 0))) for rows_of in pack] + [grad_mixed, mixed_all]
    pack = jnp.concatenate(pack, axis=0)

    grad_enc = enc_cot.astype(f32) + grad_memory
    grad_enc_low = grad_enc.astype(bf16)
    blocks = tn(hidden, grad_enc_low).astype(bf16).reshape(fsdp, wide, part, width)
    grad_pre = (slope * nt(grad_enc_low, ff_out_full)).astype(bf16)
    back_values = norm_backward(middle, inverse_ff, gain_ff_f, nt(grad_pre, ff_in_full))
    grad_middle = grad_enc + back_values
    grad_middle_low = grad_middle.astype(bf16)
    early = [blocks[:, n] for n in range(wide)] + [tn(context, grad_middle_low).astype(bf16).reshape(fsdp, part, width)]
    across = [tn(normed_ff, grad_pre).astype(bf16).reshape(fsdp, part, wide * width)]
    early, across = scatter_core(early), scatter_core(across)
    grad_context = nt(grad_middle_low, out_full).astype(bf16)
    band, early, across, pack = lax.optimization_barrier((make_band(table, -1), early, across, pack))
    early = scatter_chips(early)
    seq_bits = bits_of("seq")
    grads = None
    pairs = HEADS // 2
    for call, bit in enumerate(seq_bits):
        across_next = halve_seq(across, bit, 2)
        first, count = call * pairs // len(seq_bits), (call + 1) * pairs // len(seq_bits) - call * pairs // len(seq_bits)
        grads = attn_bwd(info, band, query, key, value, grad_context, context, lse, first, count, grads)
        band, across, grads = lax.optimization_barrier((band, across_next, grads))
    grads, early, pack = lax.optimization_barrier((grads, early, pack))
    packs = lax.all_gather(pack, "fsdp", axis=0)
    stack = lambda shard: jnp.concatenate(
        [shard[:, n * width : (n + 1) * width] for n in range(shard.shape[1] // width)], axis=0)
    unstack = lambda rows_of: jnp.concatenate(
        [rows_of[n * part : (n + 1) * part] for n in range(rows_of.shape[0] // part)], axis=1)
    across = scatter_chips(across)
    early = stack(early)
    for bit in seq_bits:
        early = halve_seq(early, bit, 0)
    across, early = whole_seq([across, early], [1, 0], width)
    shard_ff_out = early[: wide * part].astype(f32)
    shard_ff_in = across.astype(f32)
    shard_out = early[wide * part :].astype(f32)
    grad_query, grad_key, grad_value, grad_band, grad_far = grads
    reach = window_blocks(rows)

    def term(step):
        place = step % seq_count * rows
        block = lambda values: values[place : place + rows]
        return nt(block(grad_key), kv_full[:, :width]) + nt(block(grad_value), kv_full[:, width:])

    grad_normed = scatter_window(term, reach) + (term(0) + nt(grad_query, query_full))
    late = [tn(normed, grad_query), tn(normed_all, grad_key), tn(normed_all, grad_value)]
    late = [piece.astype(bf16).reshape(fsdp, part, width) for piece in late]
    grad_table = table_grad(grad_band, grad_far).reshape(fsdp, 1, buckets_part).astype(bf16)
    late += [jnp.pad(grad_table, ((0, 0), (0, part - 1), (0, 128 - buckets_part)))]
    late = scatter_core(late)
    rowset = lambda n: packs[:, n * tile : (n + 1) * tile].reshape(fsdp * tile, width)
    mine = lambda values: lax.dynamic_slice_in_dim(values, own * part, part, 1)
    at = 12
    hid_all = jnp.concatenate([rowset(at + n) for n in range(wide)], axis=1)
    pre_all = jnp.concatenate([rowset(at + wide + n) for n in range(wide)], axis=1)
    part_ff = dff_out.shape[0]
    at = (12 + 2 * wide) * tile
    heads_rows = head_rows * docs
    mixed_g = packs[:, at : at + heads_rows].reshape(fsdp * heads_rows, width)
    mixed_m = packs[:, at + heads_rows : at + 2 * heads_rows].reshape(fsdp * heads_rows, width)
    spread = lambda n: jnp.where(head_mask[None], packs[:, n * tile : n * tile + docs, None], 0).reshape(
        fsdp * heads_rows, width)
    dec_shards = [
        tn(mine(rowset(0)), rowset(1)), tn(mine(rowset(2)), rowset(3)), tn(mine(rowset(4)), rowset(5)),
        tn(mine(mixed_g), spread(6)), tn(mine(mixed_m), spread(7)), tn(mine(rowset(8)), rowset(9)),
        tn(mine(rowset(10)), pre_all),
        tn(lax.dynamic_slice_in_dim(hid_all, own * part_ff, part_ff, 1), rowset(11)),
    ]
    late = scatter_chips(late)
    late, dec_shards = lax.optimization_barrier((late, dec_shards))
    shard_self_value, shard_self_out, shard_cross_query, shard_cross_key = dec_shards[:4]
    shard_cross_value, shard_cross_out, shard_dff_in, shard_dff_out = dec_shards[4:]
    table_rows = jnp.pad(late[:1, 3 * width :], ((0, 31), (0, width - 128)))
    late = sum_seq(jnp.concatenate([stack(late[:, : 3 * width]), table_rows], axis=0), 0).astype(f32)
    shard_query, shard_key, shard_value = (late[n * part : (n + 1) * part] for n in range(3))
    shard_table = late[3 * part, :buckets_part]
    back_values = norm_backward(tokens_f, inverse_attn, gain_attn_f, grad_normed)
    first_back = lax.dot_general(local_pick.astype(f32), grad_first, (((0,), (0,)), ((), ())),
                                 precision=lax.Precision.HIGHEST, preferred_element_type=f32)
    tokens_grad = grad_middle + back_values + first_back

    def gain_grad(gain_vec, *pairs_of):
        return sum(jnp.sum(grad * weight.astype(f32), axis=1) for grad, weight in pairs_of) / gain_vec.astype(f32)

    grad_gain_attn = gain_grad(gain_attn, (shard_query, query_weight), (shard_key, key_weight), (shard_value, value_weight))
    grad_gain_ff = gain_grad(gain_ff, (shard_ff_in, ff_in))
    grad_gain_self = gain_grad(gain_self, (shard_self_value, self_value))
    grad_gain_cross = gain_grad(gain_cross, (shard_cross_query, cross_query))
    grad_gain_dff = gain_grad(gain_dff, (shard_dff_in, dff_in))
    return (
        enc_hidden, dec_hidden, tokens_grad, grad_gain_attn, shard_query, shard_key, shard_value, shard_out,
        shard_table, grad_gain_ff, shard_ff_in, shard_ff_out, grad_gain_self, shard_self_value, shard_self_out,
        grad_gain_cross, shard_cross_query, shard_cross_key, shard_cross_value, shard_cross_out, grad_gain_dff,
        shard_dff_in, shard_dff_out,
    )


def solution(mesh):
    tok, wide, one = P(("fsdp", "seq"), None), P("fsdp", None), P("fsdp")
    return jax.shard_map(
        body,
        mesh=mesh,
        in_specs=(tok, wide, one, wide, wide, wide, wide, one, one, wide, wide, one, wide, wide, one, wide, wide, wide,
                  wide, one, wide, wide, tok, wide),
        out_specs=(tok, wide, tok, one, wide, wide, wide, wide, one, one, wide, wide, one, wide, wide, one, wide, wide,
                   wide, wide, one, wide, wide),
        check_vma=False,
    )
```

```python
import functools, math
import jax, jax.numpy as jnp
from jax import lax
from jax.experimental import pallas as pl
from jax.experimental.pallas import tpu as pltpu
from jax.sharding import PartitionSpec as P

HEADS=12; HEAD=64; BUCKETS=32
LIMITS = (12, 16, 23, 32, 46, 64, 91)
BLK=256
SUB=128
BAND=512
NEG=-1e30

def bucket_of(relative):
    distance = jnp.abs(relative)
    bucket = jnp.minimum(distance, 8)
    for bound_value in LIMITS:
        bucket = bucket + (distance >= bound_value).astype(jnp.int32)
    return bucket + 16 * (relative > 0).astype(jnp.int32)

def nt(a,b):
    return lax.dot_general(a,b,(((1,),(1,)),((),())),preferred_element_type=jnp.float32)
def tn(a,b):
    return lax.dot_general(a,b,(((0,),(0,)),((),())),preferred_element_type=jnp.float32)
def nn(a,b):
    return lax.dot_general(a,b,(((1,),(0,)),((),())),preferred_element_type=jnp.float32)

def band_offsets(sign):
    c = jnp.arange(BAND, dtype=jnp.int32)
    t = jnp.where(c < 3*SUB, c, c - BAND) - SUB
    return sign * t

def seg_of(pos, e0, e1):
    return (pos >= e0).astype(jnp.int32) + (pos >= e1).astype(jnp.int32)

def build_tiles(band_ref, tiles, hh, flip):
    row = band_ref[hh:hh+1, :]
    x = jnp.broadcast_to(row, (SUB, BAND))
    x = pltpu.roll(x, 0, 1, stride=1, stride_axis=0)
    last, first = row[0:1, 3*SUB-1:3*SUB], row[0:1, 3*SUB:3*SUB+1]
    near = [x[:, n*SUB:(n+1)*SUB] for n in range(3)]
    if flip:
        near = near[::-1]
        last, first = first, last
    low = jnp.broadcast_to(first, (SUB, SUB))
    high = jnp.broadcast_to(last, (SUB, SUB))
    for d in range(5):
        for r in range(2):
            for c in range(2):
                off = ((r - c) if flip else (c - r)) + 2*(d-2)
                tiles[hh, d, r*SUB:(r+1)*SUB, c*SUB:(c+1)*SUB] = low if off < -1 else high if off > 1 else near[off+1]

def fwd_kernel(info, band_ref, q_ref, k_ref, v_ref, ctx_ref, lse_ref, tiles, s_scr, kt_scr):
    p0, e0, e1 = info[0], info[1], info[2]
    T = q_ref.shape[0]; G = k_ref.shape[0]
    lane = lax.broadcasted_iota(jnp.int32, (1,128), 1)
    left = lane < HEAD
    for hh in range(2):
        build_tiles(band_ref, tiles, hh, False)
    for c in range(G//BLK):
        kt_scr[c] = k_ref[c*BLK:(c+1)*BLK, :].T
    for i in range(T//BLK):
        a = p0 + i*BLK; b = a + BLK - 1
        lo = jnp.where(a >= e1, e1, jnp.where(a >= e0, e0, 0))
        hi = jnp.where(b >= e1, G, jnp.where(b >= e0, e1, e0))
        j0 = lo // BLK; j1 = (hi + BLK - 1)//BLK
        ib = a // BLK
        qb = q_ref[i*BLK:(i+1)*BLK, :]
        row_pos = a + lax.broadcasted_iota(jnp.int32, (BLK,1), 0)
        row_seg = jnp.broadcast_to(seg_of(row_pos, e0, e1),(BLK,128))
        zero = jnp.zeros_like(qb)
        qh = [jnp.where(left, qb, zero), jnp.where(left, zero, qb)]
        def score(j, carry):
            kt = kt_scr[lax.rem(j*BLK + G - p0, G) // BLK]
            kpos = j*BLK + lax.broadcasted_iota(jnp.int32, (1,BLK), 1)
            kseg = seg_of(kpos, e0, e1)
            same = jnp.concatenate([row_seg == kseg[:, :128], row_seg == kseg[:,128:]],axis=1)
            d = jnp.clip(j - ib, -2, 2) + 2
            out = []
            for hh in range(2):
                s = nn(qh[hh], kt) + tiles[hh, d]
                s = jnp.where(same, s, NEG)
                s_scr[hh, j] = s
                out.append(jnp.maximum(carry[hh], jnp.maximum(s[:, :128], s[:, 128:])))
            return tuple(out)
        init = jnp.full((BLK,128), NEG, jnp.float32)
        mx = lax.fori_loop(j0, j1, score, (init, init))
        top = [jnp.max(m, axis=1, keepdims=True) for m in mx]
        def weigh(j, carry):
            koff = pl.multiple_of(lax.rem(j*BLK + G - p0, G), BLK)
            vb = v_ref[pl.ds(koff, BLK), :]
            one = jnp.ones_like(vb)
            vh = [jnp.where(left, vb, one), jnp.where(left, one, vb)]
            out = []
            for hh in range(2):
                p = jnp.exp(s_scr[hh, j] - top[hh]).astype(jnp.bfloat16)
                out.append(carry[hh] + nn(p, vh[hh]))
            return tuple(out)
        zf = jnp.zeros((BLK,128), jnp.float32)
        acc = lax.fori_loop(j0, j1, weigh, (zf, zf))
        tot = [jnp.where(left, pltpu.roll(acc[0], HEAD, 1), pltpu.roll(acc[1], HEAD, 1))]
        num = jnp.where(left, acc[0], acc[1])
        total = tot[0]
        ctx_ref[i*BLK:(i+1)*BLK, :] = (num / total).astype(jnp.bfloat16)
        lse_ref[i*BLK:(i+1)*BLK, :] = jnp.where(left, top[0], top[1]) + jnp.log(total)

def attn_fwd(info, band, q, k, v):
    T=q.shape[0]; G=k.shape[0]; W=q.shape[1]
    pairs=W//128
    return pl.pallas_call(
        fwd_kernel,
        grid=(pairs,),
        in_specs=[pl.BlockSpec(memory_space=pltpu.SMEM),
                  pl.BlockSpec((None,2,BAND), lambda p:(p,0,0)),
                  pl.BlockSpec((T,128), lambda p:(0,p)),
                  pl.BlockSpec((G,128), lambda p:(0,p)),
                  pl.BlockSpec((G,128), lambda p:(0,p))],
        out_specs=[pl.BlockSpec((T,128), lambda p:(0,p)), pl.BlockSpec((T,128), lambda p:(0,p))],
        out_shape=[jax.ShapeDtypeStruct((T,W), jnp.bfloat16), jax.ShapeDtypeStruct((T,W), jnp.float32)],
        scratch_shapes=[pltpu.VMEM((2,5,BLK,BLK), jnp.float32), pltpu.VMEM((2,G//BLK,BLK,BLK), jnp.float32),
                        pltpu.VMEM((G//BLK,128,BLK), jnp.bfloat16)],
        compiler_params=pltpu.CompilerParams(vmem_limit_bytes=24<<20),
        cost_estimate=pl.CostEstimate(flops=4*HEADS*T*1280*128, bytes_accessed=4*G*W+8*T*W, transcendentals=HEADS*T*1280),
    )(info, band, q, k, v)

def bwd_kernel(info, band_ref, q_ref, k_ref, v_ref, g_ref, ctx_ref, lse_ref, gq_ref, gk_ref, gv_ref, gb_ref, gf_ref, tiles, gt, gk_acc, gv_acc, kt_scr):
    p0, e0, e1 = info[0], info[1], info[2]
    T = q_ref.shape[0]; G = k_ref.shape[0]
    lane = lax.broadcasted_iota(jnp.int32, (1,128), 1)
    left = lane < HEAD
    sub_left = lax.broadcasted_iota(jnp.int32, (128,1), 0) < HEAD
    for hh in range(2):
        build_tiles(band_ref, tiles, hh, True)
    for c in range(G//BLK//2):
        kt_scr[c] = k_ref[c*2*BLK:(c+1)*2*BLK, :].T
    gt[...] = jnp.zeros_like(gt)
    gk_acc[...] = jnp.zeros_like(gk_acc)
    gv_acc[...] = jnp.zeros_like(gv_acc)
    for i in range(T//BLK):
        a = p0 + i*BLK; b = a + BLK - 1
        lo = jnp.where(a >= e1, e1, jnp.where(a >= e0, e0, 0))
        hi = jnp.where(b >= e1, G, jnp.where(b >= e0, e1, e0))
        j0 = lo // BLK; j1 = (hi + BLK - 1)//BLK
        ib = a // BLK
        rows = slice(i*BLK,(i+1)*BLK)
        qb = q_ref[rows, :]; gb = g_ref[rows, :]
        zero = jnp.zeros_like(qb)
        qh = [jnp.where(left, qb, zero), jnp.where(left, zero, qb)]
        gh = [jnp.where(left, gb, zero), jnp.where(left, zero, gb)]
        qt = [x.T for x in qh]; gth = [x.T for x in gh]
        prod = (gb.astype(jnp.float32) * ctx_ref[rows,:].astype(jnp.float32)).T
        lse_t = lse_ref[rows,:].T
        dot = [jnp.sum(prod[hh*HEAD:(hh+1)*HEAD], axis=0, keepdims=True) for hh in range(2)]
        lse = [lse_t[hh*HEAD:hh*HEAD+1] for hh in range(2)]
        q_pos = a + lax.broadcasted_iota(jnp.int32, (1,BLK), 1)
        q_seg = seg_of(q_pos, e0, e1)
        def step(jj, carry):
            koff = pl.multiple_of(lax.rem(jj*2*BLK + G - p0, G), 2*BLK)
            kb = k_ref[pl.ds(koff, 2*BLK), :]
            vb = v_ref[pl.ds(koff, 2*BLK), :]
            kt = kt_scr[koff // (2*BLK)]
            same = []
            for half in range(2):
                kpos = (jj*2+half)*BLK + lax.broadcasted_iota(jnp.int32, (BLK,1), 0)
                same.append(jnp.broadcast_to(seg_of(kpos, e0, e1), (BLK,BLK)) == jnp.broadcast_to(q_seg, (BLK,BLK)))
            gqs=[]
            gk = None; gv=None
            for hh in range(2):
                s_all = nn(kb, qt[hh]); gp_all = nn(vb, gth[hh])
                ps = []; gss = []
                for half in range(2):
                    d = jnp.clip(jj*2 + half - ib, -2, 2) + 2
                    s = s_all[half*BLK:(half+1)*BLK] + tiles[hh, d]
                    s = jnp.where(same[half], s, NEG)
                    p = jnp.exp(s - lse[hh])
                    gs = p * (gp_all[half*BLK:(half+1)*BLK] - dot[hh])
                    gt[hh, d] += gs
                    ps.append(p.astype(jnp.bfloat16)); gss.append(gs.astype(jnp.bfloat16))
                pb = jnp.concatenate(ps, axis=0); gsb = jnp.concatenate(gss, axis=0)
                tk = nn(gsb, qh[hh]); tv = nn(pb, gh[hh])
                gk = tk if gk is None else gk + tk
                gv = tv if gv is None else gv + tv
                gqs.append(carry[hh] + nn(kt[hh*HEAD:(hh+1)*HEAD], gsb))
            gk_acc[pl.ds(koff,2*BLK), :] += gk
            gv_acc[pl.ds(koff,2*BLK), :] += gv
            return tuple(gqs)
        zf = jnp.zeros((HEAD,BLK), jnp.float32)
        gq = lax.fori_loop(j0 // 2, (j1 + 1) // 2, step, (zf, zf))
        gq_ref[rows,:] = jnp.concatenate(gq, axis=0).T.astype(jnp.bfloat16)
    gk_ref[...] = gk_acc[...].astype(jnp.bfloat16)
    gv_ref[...] = gv_acc[...].astype(jnp.bfloat16)
    for hh in range(2):
        near = [None]*3; low = None; high = None
        for d in range(5):
            for r in range(2):
                for c in range(2):
                    off = r - c + 2*(d-2)
                    x = gt[hh, d, r*SUB:(r+1)*SUB, c*SUB:(c+1)*SUB]
                    if off < -1: low = x if low is None else low + x
                    elif off > 1: high = x if high is None else high + x
                    else: near[off+1] = x if near[off+1] is None else near[off+1] + x
        x = jnp.concatenate([near[2], near[1], near[0], jnp.zeros((SUB,SUB),jnp.float32)], axis=1)
        rows_left = SUB
        while rows_left > 1:
            rows_left //= 2
            x = x[:rows_left] + pltpu.roll(x[rows_left:], BAND - rows_left, 1)
        gb_ref[hh:hh+1,:] = x
        gf_ref[hh:hh+1,:] = jnp.concatenate([jnp.sum(low, axis=0, keepdims=True), jnp.sum(high, axis=0, keepdims=True)], axis=1)

def attn_bwd(info, band, q, k, v, g, ctx, lse, first_pair, count, into):
    T=q.shape[0]; G=k.shape[0]; W=q.shape[1]
    at = lambda rows: pl.BlockSpec((rows,128), lambda p:(0,p+first_pair))
    kernel = bwd_kernel
    if into is not None:
        kernel = lambda *refs: bwd_kernel(*refs[:8], *refs[13:])
    extra = [] if into is None else list(into)
    small = lambda n: pl.BlockSpec((None,2,n), lambda p:(p+first_pair,0,0))
    pairs=W//128
    return pl.pallas_call(
        kernel,
        grid=(count,),
        in_specs=[pl.BlockSpec(memory_space=pltpu.SMEM), small(BAND),
                  at(T), at(G), at(G), at(T), at(T), at(T)] + [pl.BlockSpec(memory_space=pl.ANY)]*len(extra),
        out_specs=[at(T), at(G), at(G), small(BAND), small(2*SUB)],
        out_shape=[jax.ShapeDtypeStruct((T,W), jnp.bfloat16), jax.ShapeDtypeStruct((G,W), jnp.bfloat16), jax.ShapeDtypeStruct((G,W), jnp.bfloat16),
                   jax.ShapeDtypeStruct((pairs,2,BAND), jnp.float32), jax.ShapeDtypeStruct((pairs,2,2*SUB), jnp.float32)],
        scratch_shapes=[pltpu.VMEM((2,5,BLK,BLK), jnp.float32), pltpu.VMEM((2,5,BLK,BLK), jnp.float32),
                        pltpu.VMEM((G,128), jnp.float32), pltpu.VMEM((G,128), jnp.float32),
                        pltpu.VMEM((G//BLK//2,128,2*BLK), jnp.bfloat16)],
        input_output_aliases={8+n: n for n in range(len(extra))},
        compiler_params=pltpu.CompilerParams(vmem_limit_bytes=24<<20),
        cost_estimate=pl.CostEstimate(flops=count*10*2*T*1280*128*4, bytes_accessed=(8*G*W+12*T*W)*count//pairs, transcendentals=2*count*T*1280),
    )(info, band, q, k, v, g, ctx, lse, *extra)

def make_band(table, sign):
    off = band_offsets(sign)
    oh = (bucket_of(off)[None,:] == jnp.arange(BUCKETS, dtype=jnp.int32)[:,None]).astype(jnp.bfloat16)
    return jnp.dot(table, oh, preferred_element_type=jnp.float32).reshape(HEADS//2, 2, BAND)

def table_grad(gb, gf):
    oh = (bucket_of(band_offsets(-1))[:,None] == jnp.arange(BUCKETS, dtype=jnp.int32)[None,:]).astype(jnp.float32)
    t = jnp.dot(gb.reshape(HEADS,BAND), oh, precision=lax.Precision.HIGHEST)
    f = gf.reshape(HEADS, 2, SUB).sum(axis=2)
    return t.at[:,15].add(f[:,0]).at[:,31].add(f[:,1])


DOC_MAX = 1024


def swap(values, axis, bit):
    count = lax.axis_size(axis)
    return lax.ppermute(values, axis, [(n, n ^ bit) for n in range(count)])


def shift(values, axis, step):
    count = lax.axis_size(axis)
    return lax.ppermute(values, axis, [(n, n + step) for n in range(count) if 0 <= n + step < count])


def bits_of(axis):
    bits = []
    while 1 << len(bits) < lax.axis_size(axis):
        bits.append(1 << len(bits))
    return bits


def pick_at(values, index, dim):
    return lax.dynamic_index_in_dim(values, index, dim, keepdims=False)


def add_low(left, right):
    return (left.astype(jnp.float32) + right.astype(jnp.float32)).astype(jnp.bfloat16)


def scatter_core(pieces):
    index = lax.axis_index("fsdp")
    core = index % 2
    halves = [piece.reshape((piece.shape[0] // 2, 2) + piece.shape[1:]) for piece in pieces]
    send = jnp.concatenate([pick_at(half, 1 - core, 1) for half in halves], axis=2)
    keep = jnp.concatenate([pick_at(half, core, 1) for half in halves], axis=2)
    return add_low(keep, swap(send, "fsdp", 1))


def scatter_chips(piece):
    index = lax.axis_index("fsdp") // 2
    done = 2
    while piece.shape[0] > 1:
        step = min(4, piece.shape[0])
        piece = piece.reshape((piece.shape[0] // step, step) + piece.shape[1:])
        place = index % step
        total = pick_at(piece, place, 1).astype(jnp.float32)
        for other in range(1, step):
            total = total + swap(pick_at(piece, place ^ other, 1), "fsdp", other * done).astype(jnp.float32)
        piece = total.astype(jnp.bfloat16)
        index = index // step
        done = done * step
    return piece[0]


def halve_seq(piece, bit, dim):
    mine = lax.axis_index("seq") // bit % 2
    low, high = jnp.split(piece, 2, axis=dim)
    return add_low(jnp.where(mine == 0, low, high), swap(jnp.where(mine == 0, high, low), "seq", bit))


def join_seq(pieces, dims, bit, width):
    mine = lax.axis_index("seq") // bit % 2
    flat = [jnp.concatenate(jnp.split(piece, piece.shape[1] // width, axis=1), axis=0) for piece in pieces]
    come = swap(jnp.concatenate(flat, axis=0), "seq", bit)
    at = 0
    joined = []
    for piece, rows_of, dim in zip(pieces, flat, dims):
        other = come[at : at + rows_of.shape[0]]
        at += rows_of.shape[0]
        other = jnp.concatenate(jnp.split(other, piece.shape[1] // width, axis=0), axis=1)
        low, high = jnp.where(mine == 0, piece, other), jnp.where(mine == 0, other, piece)
        joined.append(jnp.concatenate([low, high], axis=dim))
    return joined


def gather_seq(values):
    index = lax.axis_index("seq")
    count = lax.axis_size("seq")
    turn = lambda step: lax.ppermute(values, "seq", [(n, (n + step) % count) for n in range(count)])
    found = jnp.stack([values] + [turn(step) for step in range(count - 1, 0, -1)])
    order = (jnp.arange(count) - index) % count
    return jnp.stack([pick_at(found, order[n], 0) for n in range(count)])


def window_blocks(rows):
    return min(lax.axis_size("seq") - 1, -(-(DOC_MAX - 1) // rows))


def gather_window(values, beside):
    rows = values.shape[0]
    count, reach = lax.axis_size("seq"), window_blocks(rows)
    left, right = [values], [values]
    for far in range(reach):
        left.append(shift(left[-1], "seq", 1))
        right.append(shift(right[-1], "seq", -1))
        if far == 0:
            left[1], right[1], beside = lax.optimization_barrier((left[1], right[1], beside))
    slots = [values]
    for place in range(1, count):
        found = [right[place]] if place <= reach else []
        found += [left[count - place]] if count - place <= reach else []
        slots.append(sum(found[1:], found[0]) if found else jnp.zeros_like(values))
    return jnp.concatenate(slots, axis=0), beside


eps = 1e-06
GELU_COEF = 0.044715
GELU_ROOT = math.sqrt(2.0 / math.pi)
bf16 = jnp.bfloat16
f32 = jnp.float32


def gelu_both(values):
    inner = GELU_ROOT * (values + GELU_COEF * values * values * values)
    tanh_val = jnp.tanh(inner)
    half = 0.5 * (1.0 + tanh_val)
    slope = half + 0.5 * values * (1.0 - tanh_val * tanh_val) * GELU_ROOT * (
        1.0 + 3.0 * GELU_COEF * values * values
    )
    return values * half, slope


def norm_forward(values, gain_vec):
    inverse = lax.rsqrt(jnp.mean(values * values, axis=-1, keepdims=True) + eps)
    return (values * inverse * gain_vec).astype(bf16), inverse


def norm_backward(values, inverse, gain_vec, grad_normed):
    scaled = grad_normed * gain_vec
    cubed = inverse * inverse * inverse
    grad_values = inverse * scaled - values * cubed * jnp.mean(
        scaled * values, axis=-1, keepdims=True
    )
    return grad_values


def body(
    tokens, doc_lengths, gain_attn, query_weight, key_weight, value_weight, out_weight, bias_table,
    gain_ff, ff_in, ff_out, gain_self, self_value, self_out, gain_cross, cross_query, cross_key,
    cross_value, cross_out, gain_dff, dff_in, dff_out, enc_cot, dec_cot,
):
    seq_index = lax.axis_index("seq")
    seq_count = lax.axis_size("seq")
    own = lax.axis_index("fsdp")
    fsdp = lax.axis_size("fsdp")
    rows = tokens.shape[0]
    width = tokens.shape[1]
    group_tok = rows * seq_count
    part = query_weight.shape[0]
    buckets_part = bias_table.shape[0]
    docs = doc_lengths.shape[1]

    columns = [gain_attn, gain_ff, gain_self, gain_cross, gain_dff,
               jnp.pad(bias_table, (0, part - buckets_part))]
    small = jnp.pad(jnp.stack(columns, axis=1), ((0, 0), (0, 128 - len(columns))))
    over_fsdp = lambda pieces: lax.all_gather(jnp.concatenate(pieces, axis=1), "fsdp", axis=0, tiled=True)
    held = (out_weight, ff_in, self_value, self_out, cross_query, cross_key, cross_value, cross_out, dff_in)
    group, held = gather_window(tokens, held)
    first_weights = over_fsdp([query_weight, key_weight, value_weight, small])
    out_weight_b, ff_in_b, self_value_b, self_out_b, cross_query_b, cross_key_b, cross_value_b, cross_out_b, dff_in_b = held
    wide = dff_out.shape[0] // part
    units = dff_out.shape[0] // seq_count
    dff_in_part = pick_at(dff_in_b.reshape(part, fsdp, seq_count, units), seq_index, 2).reshape(part, fsdp * units)
    dff_out_part = lax.dynamic_slice_in_dim(dff_out, seq_index * units, units, 0)
    second_weights = over_fsdp([out_weight_b, ff_in_b, self_value_b, self_out_b, cross_query_b, cross_key_b])
    ff_out_full = over_fsdp([ff_out])
    third_weights = over_fsdp([cross_value_b, cross_out_b, dff_in_part, dff_out_part])

    query_full = first_weights[:, :width]
    kv_full = first_weights[:, width : 3 * width]
    vectors = first_weights[:, 3 * width : 3 * width + len(columns)].astype(f32)
    gain_attn_f, gain_ff_f, gain_self_f, gain_cross_f, gain_dff_f = (vectors[:, n] for n in range(5))
    table = vectors[:, 5].reshape(fsdp, part)[:, :buckets_part].reshape(HEADS, BUCKETS).astype(bf16)
    span = lambda start, count: second_weights[:, start * width : (start + count) * width]
    out_full = span(0, 1)
    ff_in_full = span(1, wide)
    self_value_full, self_out_full, cross_query_full, cross_key_full = (span(1 + wide + n, 1) for n in range(4))
    cross_value_full, cross_out_full, dff_in_full, dff_out_full = (
        third_weights[:, n * width : (n + 1) * width] for n in range(4))
    lengths = doc_lengths[0]
    end_zero = lengths[0]
    end_one = lengths[0] + lengths[1]
    here = seq_index * rows
    info = jnp.stack([here.astype(jnp.int32), end_zero, end_one])
    local_seg = seg_of(here + jnp.arange(rows, dtype=jnp.int32), end_zero, end_one)
    starts = jnp.stack([jnp.zeros_like(end_zero), end_zero, end_one])

    tokens_f = tokens.astype(f32)
    normed_all, inverse_all = norm_forward(group.astype(f32), gain_attn_f)
    normed, inverse_attn = normed_all[:rows], inverse_all[:rows]
    query = nn(normed, query_full).astype(bf16)
    key = nn(normed_all, kv_full[:, :width]).astype(bf16)
    value = nn(normed_all, kv_full[:, width:]).astype(bf16)
    context, lse = attn_fwd(info, make_band(table, 1), query, key, value)
    middle = tokens_f + nn(context, out_full)
    normed_ff, inverse_ff = norm_forward(middle, gain_ff_f)
    pre_act = nn(normed_ff, ff_in_full)
    hidden_f, slope = gelu_both(pre_act)
    hidden = hidden_f.astype(bf16)
    enc_hidden = middle + nn(hidden, ff_out_full)
    memory = enc_hidden.astype(bf16)

    local_pick = starts[:, None] == here + jnp.arange(rows, dtype=jnp.int32)[None, :]
    first = jnp.sum(gather_seq(nn(local_pick.astype(bf16), tokens).astype(bf16)).astype(f32), axis=0)
    self_low, self_inv = norm_forward(first, gain_self_f)
    self_vals = nn(self_low, self_value_full).astype(bf16)
    state_one = first + nn(self_vals, self_out_full)
    cross_low, cross_inv = norm_forward(state_one, gain_cross_f)
    cross_q = nn(cross_low, cross_query_full).astype(bf16)
    head_of = jnp.arange(width, dtype=jnp.int32) // HEAD
    head_rows = -(-HEADS // 8) * 8
    head_mask = (jnp.arange(head_rows, dtype=jnp.int32)[:, None] == head_of[None, :])[None]

    def by_head(values):
        return jnp.where(head_mask, values[:, None, :], 0).reshape(-1, width)

    def from_heads(values):
        return jnp.sum(jnp.where(head_mask, values.reshape(docs, head_rows, width), 0), axis=1)

    probe = nt(by_head(cross_q), cross_key_full).astype(bf16)
    doc_rows = jnp.repeat(jnp.arange(docs, dtype=jnp.int32), head_rows)
    in_doc = doc_rows[:, None] == local_seg[None, :]
    scores = jnp.where(in_doc, nt(probe, memory), NEG)
    top = jnp.max(scores, axis=1, keepdims=True)
    powers = jnp.where(in_doc, jnp.exp(scores - top), 0.0)
    total = jnp.sum(powers, axis=1, keepdims=True)
    mixed = nn(powers.astype(bf16), memory)
    stat_lanes = jnp.where(jnp.arange(128, dtype=jnp.int32)[None, :] == 0, top, total)
    parts = gather_seq(jnp.concatenate([mixed, stat_lanes], axis=1))
    tops = parts[:, :, width : width + 1]
    top_all = jnp.max(tops, axis=0)
    scale = jnp.exp(tops - top_all[None])
    total_all = jnp.sum(scale * parts[:, :, width + 1 : width + 2], axis=0)
    mixed_f = jnp.sum(scale * parts[:, :, :width], axis=0) / total_all
    mixed_all = mixed_f.astype(bf16)
    cross_ctx = from_heads(nn(mixed_all, cross_value_full)).astype(bf16)
    state_two = state_one + nn(cross_ctx, cross_out_full)
    ffn_low, ffn_inv = norm_forward(state_two, gain_dff_f)
    dec_hid_f, dec_slope = gelu_both(nn(ffn_low, dff_in_full))
    dec_hid = dec_hid_f.astype(bf16)

    grad_dec_pre = (dec_slope * nt(dec_cot, dff_out_full)).astype(bf16)
    halves = jnp.sum(gather_seq(jnp.concatenate([nn(dec_hid, dff_out_full), nt(grad_dec_pre, dff_in_full)])), axis=0)
    dec_hidden = state_two + halves[:docs]
    back_values = norm_backward(state_two, ffn_inv, gain_dff_f, halves[docs:])
    grad_two = dec_cot.astype(f32) + back_values
    grad_two_low = grad_two.astype(bf16)
    grad_cross_ctx = nt(grad_two_low, cross_out_full).astype(bf16)
    pull = nt(by_head(grad_cross_ctx), cross_value_full).astype(bf16)
    probs = powers * (jnp.exp(top - top_all) / total_all)
    row_dot = jnp.sum(mixed_f * pull.astype(f32), axis=1, keepdims=True)
    grad_scores = (probs * (nt(pull, memory) - row_dot)).astype(bf16)
    grad_memory = tn(jnp.concatenate([grad_scores, probs.astype(bf16)], axis=0),
                     jnp.concatenate([probe, pull], axis=0))
    grad_mixed = jnp.sum(gather_seq(nn(grad_scores, memory).astype(bf16)).astype(f32), axis=0).astype(bf16)
    grad_cross_q = from_heads(nn(grad_mixed, cross_key_full)).astype(bf16)
    back_values = norm_backward(state_one, cross_inv, gain_cross_f, nt(grad_cross_q, cross_query_full))
    grad_one = grad_two + back_values
    grad_one_low = grad_one.astype(bf16)
    grad_self_vals = nt(grad_one_low, self_out_full).astype(bf16)
    back_values = norm_backward(first, self_inv, gain_self_f, nt(grad_self_vals, self_value_full))
    grad_first = grad_one + back_values

    both = gather_seq(jnp.concatenate([dec_hid, grad_dec_pre])).reshape(seq_count, 2, docs, fsdp, units)
    both = both.transpose(1, 2, 3, 0, 4).reshape(2, docs, fsdp * seq_count * units)
    pack = [self_low, grad_self_vals, self_vals, grad_one_low, cross_low, grad_cross_q, cross_q, grad_cross_ctx,
            cross_ctx, grad_two_low, ffn_low, dec_cot]
    pack += [both[0, :, n * width : (n + 1) * width] for n in range(wide)]
    pack += [both[1, :, n * width : (n + 1) * width] for n in range(wide)]
    tile = 8
    pack = [jnp.pad(rows_of, ((0, tile - docs), (0, 0))) for rows_of in pack] + [grad_mixed, mixed_all]
    pack = jnp.concatenate(pack, axis=0)

    grad_enc = enc_cot.astype(f32) + grad_memory
    grad_enc_low = grad_enc.astype(bf16)
    blocks = tn(hidden, grad_enc_low).astype(bf16).reshape(fsdp, wide, part, width)
    grad_pre = (slope * nt(grad_enc_low, ff_out_full)).astype(bf16)
    back_values = norm_backward(middle, inverse_ff, gain_ff_f, nt(grad_pre, ff_in_full))
    grad_middle = grad_enc + back_values
    grad_middle_low = grad_middle.astype(bf16)
    early = [blocks[:, n] for n in range(wide)] + [tn(context, grad_middle_low).astype(bf16).reshape(fsdp, part, width)]
    across = [tn(normed_ff, grad_pre).astype(bf16).reshape(fsdp, part, wide * width)]
    early, across = scatter_core(early), scatter_core(across)
    grad_context = nt(grad_middle_low, out_full).astype(bf16)
    band, early, across, pack = lax.optimization_barrier((make_band(table, -1), early, across, pack))
    early = scatter_chips(early)
    seq_bits = bits_of("seq")
    grads = None
    pairs = HEADS // 2
    for call, bit in enumerate(seq_bits):
        across_next = halve_seq(across, bit, 2)
        first, count = call * pairs // len(seq_bits), (call + 1) * pairs // len(seq_bits) - call * pairs // len(seq_bits)
        grads = attn_bwd(info, band, query, key, value, grad_context, context, lse, first, count, grads)
        band, across, grads = lax.optimization_barrier((band, across_next, grads))
    grads, early, pack = lax.optimization_barrier((grads, early, pack))
    packs = lax.all_gather(pack, "fsdp", axis=0)
    stack = lambda shard: jnp.concatenate(
        [shard[:, n * width : (n + 1) * width] for n in range(shard.shape[1] // width)], axis=0)
    unstack = lambda rows_of: jnp.concatenate(
        [rows_of[n * part : (n + 1) * part] for n in range(rows_of.shape[0] // part)], axis=1)
    grad_query, grad_key, grad_value, grad_band, grad_far = grads
    reach = window_blocks(rows)

    def term(step):
        place = step % seq_count * rows
        block = lambda values: values[place : place + rows]
        return nt(block(grad_key), kv_full[:, :width]) + nt(block(grad_value), kv_full[:, width:])

    signs = (1, -1)
    moving = [shift(term(sign * reach).astype(bf16), "seq", sign) for sign in signs]
    early = halve_seq(stack(early), seq_bits[0], 0)
    across = scatter_chips(across)
    late = [tn(normed, grad_query), tn(normed_all, grad_key), tn(normed_all, grad_value)]
    late = [piece.astype(bf16).reshape(fsdp, part, width) for piece in late]
    grad_table = table_grad(grad_band, grad_far).reshape(fsdp, 1, buckets_part).astype(bf16)
    late += [jnp.pad(grad_table, ((0, 0), (0, part - 1), (0, 128 - buckets_part)))]
    late = scatter_core(late)
    near = [[term(sign * far) for sign in signs] for far in range(reach - 1, 0, -1)]
    moving, early, across, late, near = lax.optimization_barrier((moving, early, across, late, near))
    for terms in near:
        moving = [shift(add_low(one, come), "seq", sign) for one, come, sign in zip(terms, moving, signs)]
    for bit in seq_bits[1:]:
        early = halve_seq(early, bit, 0)
    late = scatter_chips(late)
    rowset = lambda n: packs[:, n * tile : (n + 1) * tile].reshape(fsdp * tile, width)
    mine = lambda values: lax.dynamic_slice_in_dim(values, own * part, part, 1)
    at = 12
    hid_all = jnp.concatenate([rowset(at + n) for n in range(wide)], axis=1)
    pre_all = jnp.concatenate([rowset(at + wide + n) for n in range(wide)], axis=1)
    part_ff = dff_out.shape[0]
    at = (12 + 2 * wide) * tile
    heads_rows = head_rows * docs
    mixed_g = packs[:, at : at + heads_rows].reshape(fsdp * heads_rows, width)
    mixed_m = packs[:, at + heads_rows : at + 2 * heads_rows].reshape(fsdp * heads_rows, width)
    spread = lambda n: jnp.where(head_mask[None], packs[:, n * tile : n * tile + docs, None], 0).reshape(
        fsdp * heads_rows, width)
    dec_shards = [
        tn(mine(rowset(0)), rowset(1)), tn(mine(rowset(2)), rowset(3)), tn(mine(rowset(4)), rowset(5)),
        tn(mine(mixed_g), spread(6)), tn(mine(mixed_m), spread(7)), tn(mine(rowset(8)), rowset(9)),
        tn(mine(rowset(10)), pre_all),
        tn(lax.dynamic_slice_in_dim(hid_all, own * part_ff, part_ff, 1), rowset(11)),
    ]
    moving, early, late, dec_shards = lax.optimization_barrier((moving, early, late, dec_shards))
    shard_self_value, shard_self_out, shard_cross_query, shard_cross_key = dec_shards[:4]
    shard_cross_value, shard_cross_out, shard_dff_in, shard_dff_out = dec_shards[4:]
    table_rows = jnp.pad(late[:1, 3 * width :], ((0, 31), (0, width - 128)))
    late = jnp.concatenate([stack(late[:, : 3 * width]), table_rows], axis=0)
    for back, bit in zip(seq_bits[::-1], seq_bits):
        across, early = join_seq([across, early], [1, 0], back, width)
        late = halve_seq(late, bit, 0)
        across, early, late = lax.optimization_barrier((across, early, late))
    for back in seq_bits[::-1]:
        (late,) = join_seq([late], [0], back, width)
    shard_ff_out = early[: wide * part].astype(f32)
    shard_ff_in = across.astype(f32)
    shard_out = early[wide * part :].astype(f32)
    late = late.astype(f32)
    shard_query, shard_key, shard_value = (late[n * part : (n + 1) * part] for n in range(3))
    shard_table = late[3 * part, :buckets_part]
    grad_normed = term(0) + nt(grad_query, query_full)
    grad_normed = grad_normed + (moving[0].astype(f32) + moving[1].astype(f32))
    back_values = norm_backward(tokens_f, inverse_attn, gain_attn_f, grad_normed)
    first_back = lax.dot_general(local_pick.astype(f32), grad_first, (((0,), (0,)), ((), ())),
                                 precision=lax.Precision.HIGHEST, preferred_element_type=f32)
    tokens_grad = grad_middle + back_values + first_back

    def gain_grad(gain_vec, *pairs_of):
        return sum(jnp.sum(grad * weight.astype(f32), axis=1) for grad, weight in pairs_of) / gain_vec.astype(f32)

    grad_gain_attn = gain_grad(gain_attn, (shard_query, query_weight), (shard_key, key_weight), (shard_value, value_weight))
    grad_gain_ff = gain_grad(gain_ff, (shard_ff_in, ff_in))
    grad_gain_self = gain_grad(gain_self, (shard_self_value, self_value))
    grad_gain_cross = gain_grad(gain_cross, (shard_cross_query, cross_query))
    grad_gain_dff = gain_grad(gain_dff, (shard_dff_in, dff_in))
    return (
        enc_hidden, dec_hidden, tokens_grad, grad_gain_attn, shard_query, shard_key, shard_value, shard_out,
        shard_table, grad_gain_ff, shard_ff_in, shard_ff_out, grad_gain_self, shard_self_value, shard_self_out,
        grad_gain_cross, shard_cross_query, shard_cross_key, shard_cross_value, shard_cross_out, grad_gain_dff,
        shard_dff_in, shard_dff_out,
    )


def solution(mesh):
    tok, wide, one = P(("fsdp", "seq"), None), P("fsdp", None), P("fsdp")
    return jax.shard_map(
        body,
        mesh=mesh,
        in_specs=(tok, wide, one, wide, wide, wide, wide, one, one, wide, wide, one, wide, wide, one, wide, wide, wide,
                  wide, one, wide, wide, tok, wide),
        out_specs=(tok, wide, tok, one, wide, wide, wide, wide, one, one, wide, wide, one, wide, wide, one, wide, wide,
                   wide, wide, one, wide, wide),
        check_vma=False,
    )
```

```python
import functools, math
import jax, jax.numpy as jnp
from jax import lax
from jax.experimental import pallas as pl
from jax.experimental.pallas import tpu as pltpu
from jax.sharding import PartitionSpec as P

HEADS=12; HEAD=64; BUCKETS=32
LIMITS = (12, 16, 23, 32, 46, 64, 91)
BLK=256
SUB=128
BAND=512
NEG=-1e30

def bucket_of(relative):
    distance = jnp.abs(relative)
    bucket = jnp.minimum(distance, 8)
    for bound_value in LIMITS:
        bucket = bucket + (distance >= bound_value).astype(jnp.int32)
    return bucket + 16 * (relative > 0).astype(jnp.int32)

def nt(a,b):
    return lax.dot_general(a,b,(((1,),(1,)),((),())),preferred_element_type=jnp.float32)
def tn(a,b):
    return lax.dot_general(a,b,(((0,),(0,)),((),())),preferred_element_type=jnp.float32)
def nn(a,b):
    return lax.dot_general(a,b,(((1,),(0,)),((),())),preferred_element_type=jnp.float32)

def band_offsets(sign):
    c = jnp.arange(BAND, dtype=jnp.int32)
    t = jnp.where(c < 3*SUB, c, c - BAND) - SUB
    return sign * t

def seg_of(pos, e0, e1):
    return (pos >= e0).astype(jnp.int32) + (pos >= e1).astype(jnp.int32)

def build_tiles(band_ref, tiles, hh, flip):
    row = band_ref[hh:hh+1, :]
    x = jnp.broadcast_to(row, (SUB, BAND))
    x = pltpu.roll(x, 0, 1, stride=1, stride_axis=0)
    last, first = row[0:1, 3*SUB-1:3*SUB], row[0:1, 3*SUB:3*SUB+1]
    near = [x[:, n*SUB:(n+1)*SUB] for n in range(3)]
    if flip:
        near = near[::-1]
        last, first = first, last
    low = jnp.broadcast_to(first, (SUB, SUB))
    high = jnp.broadcast_to(last, (SUB, SUB))
    for d in range(5):
        for r in range(2):
            for c in range(2):
                off = ((r - c) if flip else (c - r)) + 2*(d-2)
                tiles[hh, d, r*SUB:(r+1)*SUB, c*SUB:(c+1)*SUB] = low if off < -1 else high if off > 1 else near[off+1]

def fwd_kernel(info, band_ref, q_ref, k_ref, v_ref, ctx_ref, lse_ref, tiles, s_scr, kt_scr):
    p0, e0, e1 = info[0], info[1], info[2]
    T = q_ref.shape[0]; G = k_ref.shape[0]
    lane = lax.broadcasted_iota(jnp.int32, (1,128), 1)
    left = lane < HEAD
    for hh in range(2):
        build_tiles(band_ref, tiles, hh, False)
    for c in range(G//BLK):
        kt_scr[c] = k_ref[c*BLK:(c+1)*BLK, :].T
    for i in range(T//BLK):
        a = p0 + i*BLK; b = a + BLK - 1
        lo = jnp.where(a >= e1, e1, jnp.where(a >= e0, e0, 0))
        hi = jnp.where(b >= e1, G, jnp.where(b >= e0, e1, e0))
        j0 = lo // BLK; j1 = (hi + BLK - 1)//BLK
        ib = a // BLK
        qb = q_ref[i*BLK:(i+1)*BLK, :]
        row_pos = a + lax.broadcasted_iota(jnp.int32, (BLK,1), 0)
        row_seg = jnp.broadcast_to(seg_of(row_pos, e0, e1),(BLK,128))
        zero = jnp.zeros_like(qb)
        qh = [jnp.where(left, qb, zero), jnp.where(left, zero, qb)]
        def score(j, carry):
            kt = kt_scr[lax.rem(j*BLK + G - p0, G) // BLK]
            kpos = j*BLK + lax.broadcasted_iota(jnp.int32, (1,BLK), 1)
            kseg = seg_of(kpos, e0, e1)
            same = jnp.concatenate([row_seg == kseg[:, :128], row_seg == kseg[:,128:]],axis=1)
            d = jnp.clip(j - ib, -2, 2) + 2
            out = []
            for hh in range(2):
                s = nn(qh[hh], kt) + tiles[hh, d]
                s = jnp.where(same, s, NEG)
                s_scr[hh, j] = s
                out.append(jnp.maximum(carry[hh], jnp.maximum(s[:, :128], s[:, 128:])))
            return tuple(out)
        init = jnp.full((BLK,128), NEG, jnp.float32)
        mx = lax.fori_loop(j0, j1, score, (init, init))
        top = [jnp.max(m, axis=1, keepdims=True) for m in mx]
        def weigh(j, carry):
            koff = pl.multiple_of(lax.rem(j*BLK + G - p0, G), BLK)
            vb = v_ref[pl.ds(koff, BLK), :]
            one = jnp.ones_like(vb)
            vh = [jnp.where(left, vb, one), jnp.where(left, one, vb)]
            out = []
            for hh in range(2):
                p = jnp.exp(s_scr[hh, j] - top[hh]).astype(jnp.bfloat16)
                out.append(carry[hh] + nn(p, vh[hh]))
            return tuple(out)
        zf = jnp.zeros((BLK,128), jnp.float32)
        acc = lax.fori_loop(j0, j1, weigh, (zf, zf))
        tot = [jnp.where(left, pltpu.roll(acc[0], HEAD, 1), pltpu.roll(acc[1], HEAD, 1))]
        num = jnp.where(left, acc[0], acc[1])
        total = tot[0]
        ctx_ref[i*BLK:(i+1)*BLK, :] = (num / total).astype(jnp.bfloat16)
        lse_ref[i*BLK:(i+1)*BLK, :] = jnp.where(left, top[0], top[1]) + jnp.log(total)

def attn_fwd(info, band, q, k, v):
    T=q.shape[0]; G=k.shape[0]; W=q.shape[1]
    pairs=W//128
    return pl.pallas_call(
        fwd_kernel,
        grid=(pairs,),
        in_specs=[pl.BlockSpec(memory_space=pltpu.SMEM),
                  pl.BlockSpec((None,2,BAND), lambda p:(p,0,0)),
                  pl.BlockSpec((T,128), lambda p:(0,p)),
                  pl.BlockSpec((G,128), lambda p:(0,p)),
                  pl.BlockSpec((G,128), lambda p:(0,p))],
        out_specs=[pl.BlockSpec((T,128), lambda p:(0,p)), pl.BlockSpec((T,128), lambda p:(0,p))],
        out_shape=[jax.ShapeDtypeStruct((T,W), jnp.bfloat16), jax.ShapeDtypeStruct((T,W), jnp.float32)],
        scratch_shapes=[pltpu.VMEM((2,5,BLK,BLK), jnp.float32), pltpu.VMEM((2,G//BLK,BLK,BLK), jnp.float32),
                        pltpu.VMEM((G//BLK,128,BLK), jnp.bfloat16)],
        compiler_params=pltpu.CompilerParams(vmem_limit_bytes=24<<20),
        cost_estimate=pl.CostEstimate(flops=4*HEADS*T*1280*128, bytes_accessed=4*G*W+8*T*W, transcendentals=HEADS*T*1280),
    )(info, band, q, k, v)

def bwd_kernel(info, band_ref, q_ref, k_ref, v_ref, g_ref, ctx_ref, lse_ref, gq_ref, gk_ref, gv_ref, gb_ref, gf_ref, tiles, gt, gk_acc, gv_acc, kt_scr):
    p0, e0, e1 = info[0], info[1], info[2]
    T = q_ref.shape[0]; G = k_ref.shape[0]
    lane = lax.broadcasted_iota(jnp.int32, (1,128), 1)
    left = lane < HEAD
    sub_left = lax.broadcasted_iota(jnp.int32, (128,1), 0) < HEAD
    for hh in range(2):
        build_tiles(band_ref, tiles, hh, True)
    for c in range(G//BLK//2):
        kt_scr[c] = k_ref[c*2*BLK:(c+1)*2*BLK, :].T
    gt[...] = jnp.zeros_like(gt)
    gk_acc[...] = jnp.zeros_like(gk_acc)
    gv_acc[...] = jnp.zeros_like(gv_acc)
    for i in range(T//BLK):
        a = p0 + i*BLK; b = a + BLK - 1
        lo = jnp.where(a >= e1, e1, jnp.where(a >= e0, e0, 0))
        hi = jnp.where(b >= e1, G, jnp.where(b >= e0, e1, e0))
        j0 = lo // BLK; j1 = (hi + BLK - 1)//BLK
        ib = a // BLK
        rows = slice(i*BLK,(i+1)*BLK)
        qb = q_ref[rows, :]; gb = g_ref[rows, :]
        zero = jnp.zeros_like(qb)
        qh = [jnp.where(left, qb, zero), jnp.where(left, zero, qb)]
        gh = [jnp.where(left, gb, zero), jnp.where(left, zero, gb)]
        qt = [x.T for x in qh]; gth = [x.T for x in gh]
        prod = (gb.astype(jnp.float32) * ctx_ref[rows,:].astype(jnp.float32)).T
        lse_t = lse_ref[rows,:].T
        dot = [jnp.sum(prod[hh*HEAD:(hh+1)*HEAD], axis=0, keepdims=True) for hh in range(2)]
        lse = [lse_t[hh*HEAD:hh*HEAD+1] for hh in range(2)]
        q_pos = a + lax.broadcasted_iota(jnp.int32, (1,BLK), 1)
        q_seg = seg_of(q_pos, e0, e1)
        def step(jj, carry):
            koff = pl.multiple_of(lax.rem(jj*2*BLK + G - p0, G), 2*BLK)
            kb = k_ref[pl.ds(koff, 2*BLK), :]
            vb = v_ref[pl.ds(koff, 2*BLK), :]
            kt = kt_scr[koff // (2*BLK)]
            same = []
            for half in range(2):
                kpos = (jj*2+half)*BLK + lax.broadcasted_iota(jnp.int32, (BLK,1), 0)
                same.append(jnp.broadcast_to(seg_of(kpos, e0, e1), (BLK,BLK)) == jnp.broadcast_to(q_seg, (BLK,BLK)))
            gqs=[]
            gk = None; gv=None
            for hh in range(2):
                s_all = nn(kb, qt[hh]); gp_all = nn(vb, gth[hh])
                ps = []; gss = []
                for half in range(2):
                    d = jnp.clip(jj*2 + half - ib, -2, 2) + 2
                    s = s_all[half*BLK:(half+1)*BLK] + tiles[hh, d]
                    s = jnp.where(same[half], s, NEG)
                    p = jnp.exp(s - lse[hh])
                    gs = p * (gp_all[half*BLK:(half+1)*BLK] - dot[hh])
                    gt[hh, d] += gs
                    ps.append(p.astype(jnp.bfloat16)); gss.append(gs.astype(jnp.bfloat16))
                pb = jnp.concatenate(ps, axis=0); gsb = jnp.concatenate(gss, axis=0)
                tk = nn(gsb, qh[hh]); tv = nn(pb, gh[hh])
                gk = tk if gk is None else gk + tk
                gv = tv if gv is None else gv + tv
                gqs.append(carry[hh] + nn(kt[hh*HEAD:(hh+1)*HEAD], gsb))
            gk_acc[pl.ds(koff,2*BLK), :] += gk
            gv_acc[pl.ds(koff,2*BLK), :] += gv
            return tuple(gqs)
        zf = jnp.zeros((HEAD,BLK), jnp.float32)
        gq = lax.fori_loop(j0 // 2, (j1 + 1) // 2, step, (zf, zf))
        gq_ref[rows,:] = jnp.concatenate(gq, axis=0).T.astype(jnp.bfloat16)
    gk_ref[...] = gk_acc[...].astype(jnp.bfloat16)
    gv_ref[...] = gv_acc[...].astype(jnp.bfloat16)
    for hh in range(2):
        near = [None]*3; low = None; high = None
        for d in range(5):
            for r in range(2):
                for c in range(2):
                    off = r - c + 2*(d-2)
                    x = gt[hh, d, r*SUB:(r+1)*SUB, c*SUB:(c+1)*SUB]
                    if off < -1: low = x if low is None else low + x
                    elif off > 1: high = x if high is None else high + x
                    else: near[off+1] = x if near[off+1] is None else near[off+1] + x
        x = jnp.concatenate([near[2], near[1], near[0], jnp.zeros((SUB,SUB),jnp.float32)], axis=1)
        rows_left = SUB
        while rows_left > 1:
            rows_left //= 2
            x = x[:rows_left] + pltpu.roll(x[rows_left:], BAND - rows_left, 1)
        gb_ref[hh:hh+1,:] = x
        gf_ref[hh:hh+1,:] = jnp.concatenate([jnp.sum(low, axis=0, keepdims=True), jnp.sum(high, axis=0, keepdims=True)], axis=1)

def attn_bwd(info, band, q, k, v, g, ctx, lse, first_pair, count, into):
    T=q.shape[0]; G=k.shape[0]; W=q.shape[1]
    at = lambda rows: pl.BlockSpec((rows,128), lambda p:(0,p+first_pair))
    kernel = bwd_kernel
    if into is not None:
        kernel = lambda *refs: bwd_kernel(*refs[:8], *refs[13:])
    extra = [] if into is None else list(into)
    small = lambda n: pl.BlockSpec((None,2,n), lambda p:(p+first_pair,0,0))
    pairs=W//128
    return pl.pallas_call(
        kernel,
        grid=(count,),
        in_specs=[pl.BlockSpec(memory_space=pltpu.SMEM), small(BAND),
                  at(T), at(G), at(G), at(T), at(T), at(T)] + [pl.BlockSpec(memory_space=pl.ANY)]*len(extra),
        out_specs=[at(T), at(G), at(G), small(BAND), small(2*SUB)],
        out_shape=[jax.ShapeDtypeStruct((T,W), jnp.bfloat16), jax.ShapeDtypeStruct((G,W), jnp.bfloat16), jax.ShapeDtypeStruct((G,W), jnp.bfloat16),
                   jax.ShapeDtypeStruct((pairs,2,BAND), jnp.float32), jax.ShapeDtypeStruct((pairs,2,2*SUB), jnp.float32)],
        scratch_shapes=[pltpu.VMEM((2,5,BLK,BLK), jnp.float32), pltpu.VMEM((2,5,BLK,BLK), jnp.float32),
                        pltpu.VMEM((G,128), jnp.float32), pltpu.VMEM((G,128), jnp.float32),
                        pltpu.VMEM((G//BLK//2,128,2*BLK), jnp.bfloat16)],
        input_output_aliases={8+n: n for n in range(len(extra))},
        compiler_params=pltpu.CompilerParams(vmem_limit_bytes=24<<20),
        cost_estimate=pl.CostEstimate(flops=count*10*2*T*1280*128*4, bytes_accessed=(8*G*W+12*T*W)*count//pairs, transcendentals=2*count*T*1280),
    )(info, band, q, k, v, g, ctx, lse, *extra)

def make_band(table, sign):
    off = band_offsets(sign)
    oh = (bucket_of(off)[None,:] == jnp.arange(BUCKETS, dtype=jnp.int32)[:,None]).astype(jnp.bfloat16)
    return jnp.dot(table, oh, preferred_element_type=jnp.float32).reshape(HEADS//2, 2, BAND)

def table_grad(gb, gf):
    oh = (bucket_of(band_offsets(-1))[:,None] == jnp.arange(BUCKETS, dtype=jnp.int32)[None,:]).astype(jnp.float32)
    t = jnp.dot(gb.reshape(HEADS,BAND), oh, precision=lax.Precision.HIGHEST)
    f = gf.reshape(HEADS, 2, SUB).sum(axis=2)
    return t.at[:,15].add(f[:,0]).at[:,31].add(f[:,1])


DOC_MAX = 1024


def swap(values, axis, bit):
    count = lax.axis_size(axis)
    return lax.ppermute(values, axis, [(n, n ^ bit) for n in range(count)])


def shift(values, axis, step):
    count = lax.axis_size(axis)
    return lax.ppermute(values, axis, [(n, n + step) for n in range(count) if 0 <= n + step < count])


def bits_of(axis):
    bits = []
    while 1 << len(bits) < lax.axis_size(axis):
        bits.append(1 << len(bits))
    return bits


def pick_at(values, index, dim):
    return lax.dynamic_index_in_dim(values, index, dim, keepdims=False)


def add_low(left, right):
    return (left.astype(jnp.float32) + right.astype(jnp.float32)).astype(jnp.bfloat16)


def scatter_core(pieces):
    index = lax.axis_index("fsdp")
    core = index % 2
    halves = [piece.reshape((piece.shape[0] // 2, 2) + piece.shape[1:]) for piece in pieces]
    send = jnp.concatenate([pick_at(half, 1 - core, 1) for half in halves], axis=2)
    keep = jnp.concatenate([pick_at(half, core, 1) for half in halves], axis=2)
    return add_low(keep, swap(send, "fsdp", 1))


def scatter_chips(piece):
    index = lax.axis_index("fsdp") // 2
    done = 2
    while piece.shape[0] > 1:
        step = min(4, piece.shape[0])
        piece = piece.reshape((piece.shape[0] // step, step) + piece.shape[1:])
        place = index % step
        total = pick_at(piece, place, 1).astype(jnp.float32)
        for other in range(1, step):
            total = total + swap(pick_at(piece, place ^ other, 1), "fsdp", other * done).astype(jnp.float32)
        piece = total.astype(jnp.bfloat16)
        index = index // step
        done = done * step
    return piece[0]


def halve_seq(piece, bit, dim):
    mine = lax.axis_index("seq") // bit % 2
    low, high = jnp.split(piece, 2, axis=dim)
    return add_low(jnp.where(mine == 0, low, high), swap(jnp.where(mine == 0, high, low), "seq", bit))


def join_seq(pieces, dims, bit, width):
    mine = lax.axis_index("seq") // bit % 2
    flat = [jnp.concatenate(jnp.split(piece, piece.shape[1] // width, axis=1), axis=0) for piece in pieces]
    come = swap(jnp.concatenate(flat, axis=0), "seq", bit)
    at = 0
    joined = []
    for piece, rows_of, dim in zip(pieces, flat, dims):
        other = come[at : at + rows_of.shape[0]]
        at += rows_of.shape[0]
        other = jnp.concatenate(jnp.split(other, piece.shape[1] // width, axis=0), axis=1)
        low, high = jnp.where(mine == 0, piece, other), jnp.where(mine == 0, other, piece)
        joined.append(jnp.concatenate([low, high], axis=dim))
    return joined


def gather_seq(values):
    index = lax.axis_index("seq")
    count = lax.axis_size("seq")
    turn = lambda step: lax.ppermute(values, "seq", [(n, (n + step) % count) for n in range(count)])
    found = jnp.stack([values] + [turn(step) for step in range(count - 1, 0, -1)])
    order = (jnp.arange(count) - index) % count
    return jnp.stack([pick_at(found, order[n], 0) for n in range(count)])


def window_blocks(rows):
    return min(lax.axis_size("seq") - 1, -(-(DOC_MAX - 1) // rows))


def gather_window(values, beside):
    rows = values.shape[0]
    count, reach = lax.axis_size("seq"), window_blocks(rows)
    left, right = [values], [values]
    for far in range(reach):
        left.append(shift(left[-1], "seq", 1))
        right.append(shift(right[-1], "seq", -1))
        if far == 0:
            left[1], right[1], beside = lax.optimization_barrier((left[1], right[1], beside))
    slots = [values]
    for place in range(1, count):
        found = [right[place]] if place <= reach else []
        found += [left[count - place]] if count - place <= reach else []
        slots.append(sum(found[1:], found[0]) if found else jnp.zeros_like(values))
    return jnp.concatenate(slots, axis=0), beside


eps = 1e-06
GELU_COEF = 0.044715
GELU_ROOT = math.sqrt(2.0 / math.pi)
bf16 = jnp.bfloat16
f32 = jnp.float32


def gelu_both(values):
    inner = GELU_ROOT * (values + GELU_COEF * values * values * values)
    tanh_val = jnp.tanh(inner)
    half = 0.5 * (1.0 + tanh_val)
    slope = half + 0.5 * values * (1.0 - tanh_val * tanh_val) * GELU_ROOT * (
        1.0 + 3.0 * GELU_COEF * values * values
    )
    return values * half, slope


def norm_forward(values, gain_vec):
    inverse = lax.rsqrt(jnp.mean(values * values, axis=-1, keepdims=True) + eps)
    return (values * inverse * gain_vec).astype(bf16), inverse


def norm_backward(values, inverse, gain_vec, grad_normed):
    scaled = grad_normed * gain_vec
    cubed = inverse * inverse * inverse
    grad_values = inverse * scaled - values * cubed * jnp.mean(
        scaled * values, axis=-1, keepdims=True
    )
    return grad_values


def body(
    tokens, doc_lengths, gain_attn, query_weight, key_weight, value_weight, out_weight, bias_table,
    gain_ff, ff_in, ff_out, gain_self, self_value, self_out, gain_cross, cross_query, cross_key,
    cross_value, cross_out, gain_dff, dff_in, dff_out, enc_cot, dec_cot,
):
    seq_index = lax.axis_index("seq")
    seq_count = lax.axis_size("seq")
    own = lax.axis_index("fsdp")
    fsdp = lax.axis_size("fsdp")
    rows = tokens.shape[0]
    width = tokens.shape[1]
    group_tok = rows * seq_count
    part = query_weight.shape[0]
    buckets_part = bias_table.shape[0]
    docs = doc_lengths.shape[1]

    columns = [gain_attn, gain_ff, gain_self, gain_cross, gain_dff,
               jnp.pad(bias_table, (0, part - buckets_part))]
    small = jnp.pad(jnp.stack(columns, axis=1), ((0, 0), (0, 128 - len(columns))))
    over_fsdp = lambda pieces: lax.all_gather(jnp.concatenate(pieces, axis=1), "fsdp", axis=0, tiled=True)
    held = (out_weight, ff_in, self_value, self_out, cross_query, cross_key, cross_value, cross_out, dff_in)
    group, held = gather_window(tokens, held)
    first_weights = over_fsdp([query_weight, key_weight, value_weight, small])
    out_weight_b, ff_in_b, self_value_b, self_out_b, cross_query_b, cross_key_b, cross_value_b, cross_out_b, dff_in_b = held
    wide = dff_out.shape[0] // part
    units = dff_out.shape[0] // seq_count
    dff_in_part = pick_at(dff_in_b.reshape(part, fsdp, seq_count, units), seq_index, 2).reshape(part, fsdp * units)
    dff_out_part = lax.dynamic_slice_in_dim(dff_out, seq_index * units, units, 0)
    second_weights = over_fsdp([out_weight_b, ff_in_b, self_value_b, self_out_b, cross_query_b, cross_key_b])
    ff_out_full = over_fsdp([ff_out])
    third_weights = over_fsdp([cross_value_b, cross_out_b, dff_in_part, dff_out_part])

    query_full = first_weights[:, :width]
    kv_full = first_weights[:, width : 3 * width]
    vectors = first_weights[:, 3 * width : 3 * width + len(columns)].astype(f32)
    gain_attn_f, gain_ff_f, gain_self_f, gain_cross_f, gain_dff_f = (vectors[:, n] for n in range(5))
    table = vectors[:, 5].reshape(fsdp, part)[:, :buckets_part].reshape(HEADS, BUCKETS).astype(bf16)
    span = lambda start, count: second_weights[:, start * width : (start + count) * width]
    out_full = span(0, 1)
    ff_in_full = span(1, wide)
    self_value_full, self_out_full, cross_query_full, cross_key_full = (span(1 + wide + n, 1) for n in range(4))
    cross_value_full, cross_out_full, dff_in_full, dff_out_full = (
        third_weights[:, n * width : (n + 1) * width] for n in range(4))
    lengths = doc_lengths[0]
    end_zero = lengths[0]
    end_one = lengths[0] + lengths[1]
    here = seq_index * rows
    info = jnp.stack([here.astype(jnp.int32), end_zero, end_one])
    local_seg = seg_of(here + jnp.arange(rows, dtype=jnp.int32), end_zero, end_one)
    starts = jnp.stack([jnp.zeros_like(end_zero), end_zero, end_one])

    tokens_f = tokens.astype(f32)
    normed_all, inverse_all = norm_forward(group.astype(f32), gain_attn_f)
    normed, inverse_attn = normed_all[:rows], inverse_all[:rows]
    query = nn(normed, query_full).astype(bf16)
    key = nn(normed_all, kv_full[:, :width]).astype(bf16)
    value = nn(normed_all, kv_full[:, width:]).astype(bf16)
    context, lse = attn_fwd(info, make_band(table, 1), query, key, value)
    middle = tokens_f + nn(context, out_full)
    normed_ff, inverse_ff = norm_forward(middle, gain_ff_f)
    pre_act = nn(normed_ff, ff_in_full)
    hidden_f, slope = gelu_both(pre_act)
    hidden = hidden_f.astype(bf16)
    enc_hidden = middle + nn(hidden, ff_out_full)
    memory = enc_hidden.astype(bf16)

    local_pick = starts[:, None] == here + jnp.arange(rows, dtype=jnp.int32)[None, :]
    first = jnp.sum(gather_seq(nn(local_pick.astype(bf16), tokens).astype(bf16)).astype(f32), axis=0)
    self_low, self_inv = norm_forward(first, gain_self_f)
    self_vals = nn(self_low, self_value_full).astype(bf16)
    state_one = first + nn(self_vals, self_out_full)
    cross_low, cross_inv = norm_forward(state_one, gain_cross_f)
    cross_q = nn(cross_low, cross_query_full).astype(bf16)
    head_of = jnp.arange(width, dtype=jnp.int32) // HEAD
    head_rows = -(-HEADS // 8) * 8
    head_mask = (jnp.arange(head_rows, dtype=jnp.int32)[:, None] == head_of[None, :])[None]

    def by_head(values):
        return jnp.where(head_mask, values[:, None, :], 0).reshape(-1, width)

    def from_heads(values):
        return jnp.sum(jnp.where(head_mask, values.reshape(docs, head_rows, width), 0), axis=1)

    probe = nt(by_head(cross_q), cross_key_full).astype(bf16)
    doc_rows = jnp.repeat(jnp.arange(docs, dtype=jnp.int32), head_rows)
    in_doc = doc_rows[:, None] == local_seg[None, :]
    scores = jnp.where(in_doc, nt(probe, memory), NEG)
    top = jnp.max(scores, axis=1, keepdims=True)
    powers = jnp.where(in_doc, jnp.exp(scores - top), 0.0)
    total = jnp.sum(powers, axis=1, keepdims=True)
    mixed = nn(powers.astype(bf16), memory)
    stat_lanes = jnp.where(jnp.arange(128, dtype=jnp.int32)[None, :] == 0, top, total)
    parts = gather_seq(jnp.concatenate([mixed, stat_lanes], axis=1))
    tops = parts[:, :, width : width + 1]
    top_all = jnp.max(tops, axis=0)
    scale = jnp.exp(tops - top_all[None])
    total_all = jnp.sum(scale * parts[:, :, width + 1 : width + 2], axis=0)
    mixed_f = jnp.sum(scale * parts[:, :, :width], axis=0) / total_all
    mixed_all = mixed_f.astype(bf16)
    cross_ctx = from_heads(nn(mixed_all, cross_value_full)).astype(bf16)
    state_two = state_one + nn(cross_ctx, cross_out_full)
    ffn_low, ffn_inv = norm_forward(state_two, gain_dff_f)
    dec_hid_f, dec_slope = gelu_both(nn(ffn_low, dff_in_full))
    dec_hid = dec_hid_f.astype(bf16)

    grad_dec_pre = (dec_slope * nt(dec_cot, dff_out_full)).astype(bf16)
    halves = jnp.sum(gather_seq(jnp.concatenate([nn(dec_hid, dff_out_full), nt(grad_dec_pre, dff_in_full)])), axis=0)
    dec_hidden = state_two + halves[:docs]
    back_values = norm_backward(state_two, ffn_inv, gain_dff_f, halves[docs:])
    grad_two = dec_cot.astype(f32) + back_values
    grad_two_low = grad_two.astype(bf16)
    grad_cross_ctx = nt(grad_two_low, cross_out_full).astype(bf16)
    pull = nt(by_head(grad_cross_ctx), cross_value_full).astype(bf16)
    probs = powers * (jnp.exp(top - top_all) / total_all)
    row_dot = jnp.sum(mixed_f * pull.astype(f32), axis=1, keepdims=True)
    grad_scores = (probs * (nt(pull, memory) - row_dot)).astype(bf16)
    grad_memory = tn(jnp.concatenate([grad_scores, probs.astype(bf16)], axis=0),
                     jnp.concatenate([probe, pull], axis=0))
    joint = gather_seq(jnp.concatenate([nn(grad_scores, memory).astype(bf16), dec_hid, grad_dec_pre], axis=0))
    heads_rows = head_rows * docs
    grad_mixed = jnp.sum(joint[:, :heads_rows].astype(f32), axis=0).astype(bf16)
    grad_cross_q = from_heads(nn(grad_mixed, cross_key_full)).astype(bf16)
    back_values = norm_backward(state_one, cross_inv, gain_cross_f, nt(grad_cross_q, cross_query_full))
    grad_one = grad_two + back_values
    grad_one_low = grad_one.astype(bf16)
    grad_self_vals = nt(grad_one_low, self_out_full).astype(bf16)
    back_values = norm_backward(first, self_inv, gain_self_f, nt(grad_self_vals, self_value_full))
    grad_first = grad_one + back_values

    both = joint[:, heads_rows:].reshape(seq_count, 2, docs, fsdp, units)
    both = both.transpose(1, 2, 3, 0, 4).reshape(2, docs, fsdp * seq_count * units)
    pack = [self_low, grad_self_vals, self_vals, grad_one_low, cross_low, grad_cross_q, cross_q, grad_cross_ctx,
            cross_ctx, grad_two_low, ffn_low, dec_cot]
    pack += [both[0, :, n * width : (n + 1) * width] for n in range(wide)]
    pack += [both[1, :, n * width : (n + 1) * width] for n in range(wide)]
    tile = 8
    pack = [jnp.pad(rows_of, ((0, tile - docs), (0, 0))) for rows_of in pack] + [grad_mixed, mixed_all]
    pack = jnp.concatenate(pack, axis=0)

    grad_enc = enc_cot.astype(f32) + grad_memory
    grad_enc_low = grad_enc.astype(bf16)
    blocks = tn(hidden, grad_enc_low).astype(bf16).reshape(fsdp, wide, part, width)
    grad_pre = (slope * nt(grad_enc_low, ff_out_full)).astype(bf16)
    back_values = norm_backward(middle, inverse_ff, gain_ff_f, nt(grad_pre, ff_in_full))
    grad_middle = grad_enc + back_values
    grad_middle_low = grad_middle.astype(bf16)
    early = [blocks[:, n] for n in range(wide)] + [tn(context, grad_middle_low).astype(bf16).reshape(fsdp, part, width)]
    across = [tn(normed_ff, grad_pre).astype(bf16).reshape(fsdp, part, wide * width)]
    early, across = scatter_core(early), scatter_core(across)
    grad_context = nt(grad_middle_low, out_full).astype(bf16)
    band, early, across, pack = lax.optimization_barrier((make_band(table, -1), early, across, pack))
    early = scatter_chips(early)
    seq_bits = bits_of("seq")
    grads = None
    pairs = HEADS // 2
    for call, bit in enumerate(seq_bits):
        across_next = halve_seq(across, bit, 2)
        first, count = call * pairs // len(seq_bits), (call + 1) * pairs // len(seq_bits) - call * pairs // len(seq_bits)
        grads = attn_bwd(info, band, query, key, value, grad_context, context, lse, first, count, grads)
        band, across, grads = lax.optimization_barrier((band, across_next, grads))
    grads, early, pack = lax.optimization_barrier((grads, early, pack))
    packs = lax.all_gather(pack, "fsdp", axis=0)
    stack = lambda shard: jnp.concatenate(
        [shard[:, n * width : (n + 1) * width] for n in range(shard.shape[1] // width)], axis=0)
    unstack = lambda rows_of: jnp.concatenate(
        [rows_of[n * part : (n + 1) * part] for n in range(rows_of.shape[0] // part)], axis=1)
    grad_query, grad_key, grad_value, grad_band, grad_far = grads
    reach = window_blocks(rows)

    def term(step):
        place = step % seq_count * rows
        block = lambda values: values[place : place + rows]
        return nt(block(grad_key), kv_full[:, :width]) + nt(block(grad_value), kv_full[:, width:])

    signs = (1, -1)
    moving = [shift(term(sign * reach).astype(bf16), "seq", sign) for sign in signs]
    early = halve_seq(stack(early), seq_bits[0], 0)
    across = scatter_chips(across)
    late = [tn(normed, grad_query), tn(normed_all, grad_key), tn(normed_all, grad_value)]
    late = [piece.astype(bf16).reshape(fsdp, part, width) for piece in late]
    grad_table = table_grad(grad_band, grad_far).reshape(fsdp, 1, buckets_part).astype(bf16)
    late += [jnp.pad(grad_table, ((0, 0), (0, part - 1), (0, 128 - buckets_part)))]
    late = scatter_core(late)
    near = [[term(sign * far) for sign in signs] for far in range(reach - 1, 0, -1)]
    moving, early, across, late, near = lax.optimization_barrier((moving, early, across, late, near))
    for terms in near:
        moving = [shift(add_low(one, come), "seq", sign) for one, come, sign in zip(terms, moving, signs)]
    for bit in seq_bits[1:]:
        early = halve_seq(early, bit, 0)
    late = scatter_chips(late)
    rowset = lambda n: packs[:, n * tile : (n + 1) * tile].reshape(fsdp * tile, width)
    mine = lambda values: lax.dynamic_slice_in_dim(values, own * part, part, 1)
    at = 12
    hid_all = jnp.concatenate([rowset(at + n) for n in range(wide)], axis=1)
    pre_all = jnp.concatenate([rowset(at + wide + n) for n in range(wide)], axis=1)
    part_ff = dff_out.shape[0]
    at = (12 + 2 * wide) * tile
    heads_rows = head_rows * docs
    mixed_g = packs[:, at : at + heads_rows].reshape(fsdp * heads_rows, width)
    mixed_m = packs[:, at + heads_rows : at + 2 * heads_rows].reshape(fsdp * heads_rows, width)
    spread = lambda n: jnp.where(head_mask[None], packs[:, n * tile : n * tile + docs, None], 0).reshape(
        fsdp * heads_rows, width)
    dec_shards = [
        tn(mine(rowset(0)), rowset(1)), tn(mine(rowset(2)), rowset(3)), tn(mine(rowset(4)), rowset(5)),
        tn(mine(mixed_g), spread(6)), tn(mine(mixed_m), spread(7)), tn(mine(rowset(8)), rowset(9)),
        tn(mine(rowset(10)), pre_all),
        tn(lax.dynamic_slice_in_dim(hid_all, own * part_ff, part_ff, 1), rowset(11)),
    ]
    moving, early, late, dec_shards = lax.optimization_barrier((moving, early, late, dec_shards))
    shard_self_value, shard_self_out, shard_cross_query, shard_cross_key = dec_shards[:4]
    shard_cross_value, shard_cross_out, shard_dff_in, shard_dff_out = dec_shards[4:]
    table_rows = jnp.pad(late[:1, 3 * width :], ((0, 31), (0, width - 128)))
    late = jnp.concatenate([stack(late[:, : 3 * width]), table_rows], axis=0)
    for back, bit in zip(seq_bits[::-1], seq_bits):
        across, early = join_seq([across, early], [1, 0], back, width)
        late = halve_seq(late, bit, 0)
        across, early, late = lax.optimization_barrier((across, early, late))
    for back in seq_bits[::-1]:
        (late,) = join_seq([late], [0], back, width)
    shard_ff_out = early[: wide * part].astype(f32)
    shard_ff_in = across.astype(f32)
    shard_out = early[wide * part :].astype(f32)
    late = late.astype(f32)
    shard_query, shard_key, shard_value = (late[n * part : (n + 1) * part] for n in range(3))
    shard_table = late[3 * part, :buckets_part]
    grad_normed = term(0) + nt(grad_query, query_full)
    grad_normed = grad_normed + (moving[0].astype(f32) + moving[1].astype(f32))
    back_values = norm_backward(tokens_f, inverse_attn, gain_attn_f, grad_normed)
    first_back = lax.dot_general(local_pick.astype(f32), grad_first, (((0,), (0,)), ((), ())),
                                 precision=lax.Precision.HIGHEST, preferred_element_type=f32)
    tokens_grad = grad_middle + back_values + first_back

    def gain_grad(gain_vec, *pairs_of):
        return sum(jnp.sum(grad * weight.astype(f32), axis=1) for grad, weight in pairs_of) / gain_vec.astype(f32)

    grad_gain_attn = gain_grad(gain_attn, (shard_query, query_weight), (shard_key, key_weight), (shard_value, value_weight))
    grad_gain_ff = gain_grad(gain_ff, (shard_ff_in, ff_in))
    grad_gain_self = gain_grad(gain_self, (shard_self_value, self_value))
    grad_gain_cross = gain_grad(gain_cross, (shard_cross_query, cross_query))
    grad_gain_dff = gain_grad(gain_dff, (shard_dff_in, dff_in))
    return (
        enc_hidden, dec_hidden, tokens_grad, grad_gain_attn, shard_query, shard_key, shard_value, shard_out,
        shard_table, grad_gain_ff, shard_ff_in, shard_ff_out, grad_gain_self, shard_self_value, shard_self_out,
        grad_gain_cross, shard_cross_query, shard_cross_key, shard_cross_value, shard_cross_out, grad_gain_dff,
        shard_dff_in, shard_dff_out,
    )


def solution(mesh):
    tok, wide, one = P(("fsdp", "seq"), None), P("fsdp", None), P("fsdp")
    return jax.shard_map(
        body,
        mesh=mesh,
        in_specs=(tok, wide, one, wide, wide, wide, wide, one, one, wide, wide, one, wide, wide, one, wide, wide, wide,
                  wide, one, wide, wide, tok, wide),
        out_specs=(tok, wide, tok, one, wide, wide, wide, wide, one, one, wide, wide, one, wide, wide, one, wide, wide,
                   wide, wide, one, wide, wide),
        check_vma=False,
    )
```

```python
import functools, math
import jax, jax.numpy as jnp
from jax import lax
from jax.experimental import pallas as pl
from jax.experimental.pallas import tpu as pltpu
from jax.sharding import PartitionSpec as P

HEADS=12; HEAD=64; BUCKETS=32
LIMITS = (12, 16, 23, 32, 46, 64, 91)
BLK=256
SUB=128
BAND=512
NEG=-1e30

def bucket_of(relative):
    distance = jnp.abs(relative)
    bucket = jnp.minimum(distance, 8)
    for bound_value in LIMITS:
        bucket = bucket + (distance >= bound_value).astype(jnp.int32)
    return bucket + 16 * (relative > 0).astype(jnp.int32)

def nt(a,b):
    return lax.dot_general(a,b,(((1,),(1,)),((),())),preferred_element_type=jnp.float32)
def tn(a,b):
    return lax.dot_general(a,b,(((0,),(0,)),((),())),preferred_element_type=jnp.float32)
def nn(a,b):
    return lax.dot_general(a,b,(((1,),(0,)),((),())),preferred_element_type=jnp.float32)

def band_offsets(sign):
    c = jnp.arange(BAND, dtype=jnp.int32)
    t = jnp.where(c < 3*SUB, c, c - BAND) - SUB
    return sign * t

def seg_of(pos, e0, e1):
    return (pos >= e0).astype(jnp.int32) + (pos >= e1).astype(jnp.int32)

def build_tiles(band_ref, tiles, hh, flip):
    row = band_ref[hh:hh+1, :]
    x = jnp.broadcast_to(row, (SUB, BAND))
    x = pltpu.roll(x, 0, 1, stride=1, stride_axis=0)
    last, first = row[0:1, 3*SUB-1:3*SUB], row[0:1, 3*SUB:3*SUB+1]
    near = [x[:, n*SUB:(n+1)*SUB] for n in range(3)]
    if flip:
        near = near[::-1]
        last, first = first, last
    low = jnp.broadcast_to(first, (SUB, SUB))
    high = jnp.broadcast_to(last, (SUB, SUB))
    for d in range(5):
        for r in range(2):
            for c in range(2):
                off = ((r - c) if flip else (c - r)) + 2*(d-2)
                tiles[hh, d, r*SUB:(r+1)*SUB, c*SUB:(c+1)*SUB] = low if off < -1 else high if off > 1 else near[off+1]

def fwd_kernel(info, band_ref, q_ref, k_ref, v_ref, ctx_ref, lse_ref, tiles, s_scr, kt_scr):
    p0, e0, e1 = info[0], info[1], info[2]
    T = q_ref.shape[0]; G = k_ref.shape[0]
    lane = lax.broadcasted_iota(jnp.int32, (1,128), 1)
    left = lane < HEAD
    for hh in range(2):
        build_tiles(band_ref, tiles, hh, False)
    for c in range(G//BLK):
        kt_scr[c] = k_ref[c*BLK:(c+1)*BLK, :].T
    for i in range(T//BLK):
        a = p0 + i*BLK; b = a + BLK - 1
        lo = jnp.where(a >= e1, e1, jnp.where(a >= e0, e0, 0))
        hi = jnp.where(b >= e1, G, jnp.where(b >= e0, e1, e0))
        j0 = lo // BLK; j1 = (hi + BLK - 1)//BLK
        ib = a // BLK
        qb = q_ref[i*BLK:(i+1)*BLK, :]
        row_pos = a + lax.broadcasted_iota(jnp.int32, (BLK,1), 0)
        row_seg = jnp.broadcast_to(seg_of(row_pos, e0, e1),(BLK,128))
        zero = jnp.zeros_like(qb)
        qh = [jnp.where(left, qb, zero), jnp.where(left, zero, qb)]
        def score(j, carry):
            kt = kt_scr[lax.rem(j*BLK + G - p0, G) // BLK]
            kpos = j*BLK + lax.broadcasted_iota(jnp.int32, (1,BLK), 1)
            kseg = seg_of(kpos, e0, e1)
            same = jnp.concatenate([row_seg == kseg[:, :128], row_seg == kseg[:,128:]],axis=1)
            d = jnp.clip(j - ib, -2, 2) + 2
            out = []
            for hh in range(2):
                s = nn(qh[hh], kt) + tiles[hh, d]
                s = jnp.where(same, s, NEG)
                s_scr[hh, j] = s
                out.append(jnp.maximum(carry[hh], jnp.maximum(s[:, :128], s[:, 128:])))
            return tuple(out)
        init = jnp.full((BLK,128), NEG, jnp.float32)
        mx = lax.fori_loop(j0, j1, score, (init, init))
        top = [jnp.max(m, axis=1, keepdims=True) for m in mx]
        def weigh(j, carry):
            koff = pl.multiple_of(lax.rem(j*BLK + G - p0, G), BLK)
            vb = v_ref[pl.ds(koff, BLK), :]
            one = jnp.ones_like(vb)
            vh = [jnp.where(left, vb, one), jnp.where(left, one, vb)]
            out = []
            for hh in range(2):
                p = jnp.exp(s_scr[hh, j] - top[hh]).astype(jnp.bfloat16)
                out.append(carry[hh] + nn(p, vh[hh]))
            return tuple(out)
        zf = jnp.zeros((BLK,128), jnp.float32)
        acc = lax.fori_loop(j0, j1, weigh, (zf, zf))
        tot = [jnp.where(left, pltpu.roll(acc[0], HEAD, 1), pltpu.roll(acc[1], HEAD, 1))]
        num = jnp.where(left, acc[0], acc[1])
        total = tot[0]
        ctx_ref[i*BLK:(i+1)*BLK, :] = (num / total).astype(jnp.bfloat16)
        lse_ref[i*BLK:(i+1)*BLK, :] = jnp.where(left, top[0], top[1]) + jnp.log(total)

def attn_fwd(info, band, q, k, v):
    T=q.shape[0]; G=k.shape[0]; W=q.shape[1]
    pairs=W//128
    return pl.pallas_call(
        fwd_kernel,
        grid=(pairs,),
        in_specs=[pl.BlockSpec(memory_space=pltpu.SMEM),
                  pl.BlockSpec((None,2,BAND), lambda p:(p,0,0)),
                  pl.BlockSpec((T,128), lambda p:(0,p)),
                  pl.BlockSpec((G,128), lambda p:(0,p)),
                  pl.BlockSpec((G,128), lambda p:(0,p))],
        out_specs=[pl.BlockSpec((T,128), lambda p:(0,p)), pl.BlockSpec((T,128), lambda p:(0,p))],
        out_shape=[jax.ShapeDtypeStruct((T,W), jnp.bfloat16), jax.ShapeDtypeStruct((T,W), jnp.float32)],
        scratch_shapes=[pltpu.VMEM((2,5,BLK,BLK), jnp.float32), pltpu.VMEM((2,G//BLK,BLK,BLK), jnp.float32),
                        pltpu.VMEM((G//BLK,128,BLK), jnp.bfloat16)],
        compiler_params=pltpu.CompilerParams(vmem_limit_bytes=24<<20),
        cost_estimate=pl.CostEstimate(flops=4*HEADS*T*1280*128, bytes_accessed=4*G*W+8*T*W, transcendentals=HEADS*T*1280),
    )(info, band, q, k, v)

def bwd_kernel(info, band_ref, q_ref, k_ref, v_ref, g_ref, ctx_ref, lse_ref, gq_ref, gk_ref, gv_ref, gb_ref, gf_ref, tiles, gt, gk_acc, gv_acc, kt_scr):
    p0, e0, e1 = info[0], info[1], info[2]
    T = q_ref.shape[0]; G = k_ref.shape[0]
    lane = lax.broadcasted_iota(jnp.int32, (1,128), 1)
    left = lane < HEAD
    sub_left = lax.broadcasted_iota(jnp.int32, (128,1), 0) < HEAD
    for hh in range(2):
        build_tiles(band_ref, tiles, hh, True)
    for c in range(G//BLK//2):
        kt_scr[c] = k_ref[c*2*BLK:(c+1)*2*BLK, :].T
    gt[...] = jnp.zeros_like(gt)
    gk_acc[...] = jnp.zeros_like(gk_acc)
    gv_acc[...] = jnp.zeros_like(gv_acc)
    for i in range(T//BLK):
        a = p0 + i*BLK; b = a + BLK - 1
        lo = jnp.where(a >= e1, e1, jnp.where(a >= e0, e0, 0))
        hi = jnp.where(b >= e1, G, jnp.where(b >= e0, e1, e0))
        j0 = lo // BLK; j1 = (hi + BLK - 1)//BLK
        ib = a // BLK
        rows = slice(i*BLK,(i+1)*BLK)
        qb = q_ref[rows, :]; gb = g_ref[rows, :]
        zero = jnp.zeros_like(qb)
        qh = [jnp.where(left, qb, zero), jnp.where(left, zero, qb)]
        gh = [jnp.where(left, gb, zero), jnp.where(left, zero, gb)]
        qt = [x.T for x in qh]; gth = [x.T for x in gh]
        prod = (gb.astype(jnp.float32) * ctx_ref[rows,:].astype(jnp.float32)).T
        lse_t = lse_ref[rows,:].T
        dot = [jnp.sum(prod[hh*HEAD:(hh+1)*HEAD], axis=0, keepdims=True) for hh in range(2)]
        lse = [lse_t[hh*HEAD:hh*HEAD+1] for hh in range(2)]
        q_pos = a + lax.broadcasted_iota(jnp.int32, (1,BLK), 1)
        q_seg = seg_of(q_pos, e0, e1)
        def step(jj, carry):
            koff = pl.multiple_of(lax.rem(jj*2*BLK + G - p0, G), 2*BLK)
            kb = k_ref[pl.ds(koff, 2*BLK), :]
            vb = v_ref[pl.ds(koff, 2*BLK), :]
            kt = kt_scr[koff // (2*BLK)]
            same = []
            for half in range(2):
                kpos = (jj*2+half)*BLK + lax.broadcasted_iota(jnp.int32, (BLK,1), 0)
                same.append(jnp.broadcast_to(seg_of(kpos, e0, e1), (BLK,BLK)) == jnp.broadcast_to(q_seg, (BLK,BLK)))
            gqs=[]
            gk = None; gv=None
            for hh in range(2):
                s_all = nn(kb, qt[hh]); gp_all = nn(vb, gth[hh])
                ps = []; gss = []
                for half in range(2):
                    d = jnp.clip(jj*2 + half - ib, -2, 2) + 2
                    s = s_all[half*BLK:(half+1)*BLK] + tiles[hh, d]
                    s = jnp.where(same[half], s, NEG)
                    p = jnp.exp(s - lse[hh])
                    gs = p * (gp_all[half*BLK:(half+1)*BLK] - dot[hh])
                    gt[hh, d] += gs
                    ps.append(p.astype(jnp.bfloat16)); gss.append(gs.astype(jnp.bfloat16))
                pb = jnp.concatenate(ps, axis=0); gsb = jnp.concatenate(gss, axis=0)
                tk = nn(gsb, qh[hh]); tv = nn(pb, gh[hh])
                gk = tk if gk is None else gk + tk
                gv = tv if gv is None else gv + tv
                gqs.append(carry[hh] + nn(kt[hh*HEAD:(hh+1)*HEAD], gsb))
            gk_acc[pl.ds(koff,2*BLK), :] += gk
            gv_acc[pl.ds(koff,2*BLK), :] += gv
            return tuple(gqs)
        zf = jnp.zeros((HEAD,BLK), jnp.float32)
        gq = lax.fori_loop(j0 // 2, (j1 + 1) // 2, step, (zf, zf))
        gq_ref[rows,:] = jnp.concatenate(gq, axis=0).T.astype(jnp.bfloat16)
    gk_ref[...] = gk_acc[...].astype(jnp.bfloat16)
    gv_ref[...] = gv_acc[...].astype(jnp.bfloat16)
    for hh in range(2):
        near = [None]*3; low = None; high = None
        for d in range(5):
            for r in range(2):
                for c in range(2):
                    off = r - c + 2*(d-2)
                    x = gt[hh, d, r*SUB:(r+1)*SUB, c*SUB:(c+1)*SUB]
                    if off < -1: low = x if low is None else low + x
                    elif off > 1: high = x if high is None else high + x
                    else: near[off+1] = x if near[off+1] is None else near[off+1] + x
        x = jnp.concatenate([near[2], near[1], near[0], jnp.zeros((SUB,SUB),jnp.float32)], axis=1)
        rows_left = SUB
        while rows_left > 1:
            rows_left //= 2
            x = x[:rows_left] + pltpu.roll(x[rows_left:], BAND - rows_left, 1)
        gb_ref[hh:hh+1,:] = x
        gf_ref[hh:hh+1,:] = jnp.concatenate([jnp.sum(low, axis=0, keepdims=True), jnp.sum(high, axis=0, keepdims=True)], axis=1)

def attn_bwd(info, band, q, k, v, g, ctx, lse, first_pair, count, into):
    T=q.shape[0]; G=k.shape[0]; W=q.shape[1]
    at = lambda rows: pl.BlockSpec((rows,128), lambda p:(0,p+first_pair))
    kernel = bwd_kernel
    if into is not None:
        kernel = lambda *refs: bwd_kernel(*refs[:8], *refs[13:])
    extra = [] if into is None else list(into)
    small = lambda n: pl.BlockSpec((None,2,n), lambda p:(p+first_pair,0,0))
    pairs=W//128
    return pl.pallas_call(
        kernel,
        grid=(count,),
        in_specs=[pl.BlockSpec(memory_space=pltpu.SMEM), small(BAND),
                  at(T), at(G), at(G), at(T), at(T), at(T)] + [pl.BlockSpec(memory_space=pl.ANY)]*len(extra),
        out_specs=[at(T), at(G), at(G), small(BAND), small(2*SUB)],
        out_shape=[jax.ShapeDtypeStruct((T,W), jnp.bfloat16), jax.ShapeDtypeStruct((G,W), jnp.bfloat16), jax.ShapeDtypeStruct((G,W), jnp.bfloat16),
                   jax.ShapeDtypeStruct((pairs,2,BAND), jnp.float32), jax.ShapeDtypeStruct((pairs,2,2*SUB), jnp.float32)],
        scratch_shapes=[pltpu.VMEM((2,5,BLK,BLK), jnp.float32), pltpu.VMEM((2,5,BLK,BLK), jnp.float32),
                        pltpu.VMEM((G,128), jnp.float32), pltpu.VMEM((G,128), jnp.float32),
                        pltpu.VMEM((G//BLK//2,128,2*BLK), jnp.bfloat16)],
        input_output_aliases={8+n: n for n in range(len(extra))},
        compiler_params=pltpu.CompilerParams(vmem_limit_bytes=24<<20),
        cost_estimate=pl.CostEstimate(flops=count*10*2*T*1280*128*4, bytes_accessed=(8*G*W+12*T*W)*count//pairs, transcendentals=2*count*T*1280),
    )(info, band, q, k, v, g, ctx, lse, *extra)

def make_band(table, sign):
    off = band_offsets(sign)
    oh = (bucket_of(off)[None,:] == jnp.arange(BUCKETS, dtype=jnp.int32)[:,None]).astype(jnp.bfloat16)
    return jnp.dot(table, oh, preferred_element_type=jnp.float32).reshape(HEADS//2, 2, BAND)

def table_grad(gb, gf):
    oh = (bucket_of(band_offsets(-1))[:,None] == jnp.arange(BUCKETS, dtype=jnp.int32)[None,:]).astype(jnp.float32)
    t = jnp.dot(gb.reshape(HEADS,BAND), oh, precision=lax.Precision.HIGHEST)
    f = gf.reshape(HEADS, 2, SUB).sum(axis=2)
    return t.at[:,15].add(f[:,0]).at[:,31].add(f[:,1])


DOC_MAX = 1024


def swap(values, axis, bit):
    count = lax.axis_size(axis)
    return lax.ppermute(values, axis, [(n, n ^ bit) for n in range(count)])


def shift(values, axis, step):
    count = lax.axis_size(axis)
    return lax.ppermute(values, axis, [(n, n + step) for n in range(count) if 0 <= n + step < count])


def bits_of(axis):
    bits = []
    while 1 << len(bits) < lax.axis_size(axis):
        bits.append(1 << len(bits))
    return bits


def pick_at(values, index, dim):
    return lax.dynamic_index_in_dim(values, index, dim, keepdims=False)


def add_low(left, right):
    return (left.astype(jnp.float32) + right.astype(jnp.float32)).astype(jnp.bfloat16)


def scatter_core(pieces):
    index = lax.axis_index("fsdp")
    core = index % 2
    halves = [piece.reshape((piece.shape[0] // 2, 2) + piece.shape[1:]) for piece in pieces]
    send = jnp.concatenate([pick_at(half, 1 - core, 1) for half in halves], axis=2)
    keep = jnp.concatenate([pick_at(half, core, 1) for half in halves], axis=2)
    return add_low(keep, swap(send, "fsdp", 1))


def scatter_chips(piece):
    index = lax.axis_index("fsdp") // 2
    done = 2
    while piece.shape[0] > 1:
        step = min(4, piece.shape[0])
        piece = piece.reshape((piece.shape[0] // step, step) + piece.shape[1:])
        place = index % step
        total = pick_at(piece, place, 1).astype(jnp.float32)
        for other in range(1, step):
            total = total + swap(pick_at(piece, place ^ other, 1), "fsdp", other * done).astype(jnp.float32)
        piece = total.astype(jnp.bfloat16)
        index = index // step
        done = done * step
    return piece[0]


def halve_seq(piece, bit, dim):
    mine = lax.axis_index("seq") // bit % 2
    low, high = jnp.split(piece, 2, axis=dim)
    return add_low(jnp.where(mine == 0, low, high), swap(jnp.where(mine == 0, high, low), "seq", bit))


def join_seq(pieces, dims, bit, width):
    mine = lax.axis_index("seq") // bit % 2
    flat = [jnp.concatenate(jnp.split(piece, piece.shape[1] // width, axis=1), axis=0) for piece in pieces]
    come = swap(jnp.concatenate(flat, axis=0), "seq", bit)
    at = 0
    joined = []
    for piece, rows_of, dim in zip(pieces, flat, dims):
        other = come[at : at + rows_of.shape[0]]
        at += rows_of.shape[0]
        other = jnp.concatenate(jnp.split(other, piece.shape[1] // width, axis=0), axis=1)
        low, high = jnp.where(mine == 0, piece, other), jnp.where(mine == 0, other, piece)
        joined.append(jnp.concatenate([low, high], axis=dim))
    return joined


def gather_seq(values):
    index = lax.axis_index("seq")
    count = lax.axis_size("seq")
    turn = lambda step: lax.ppermute(values, "seq", [(n, (n + step) % count) for n in range(count)])
    found = jnp.stack([values] + [turn(step) for step in range(count - 1, 0, -1)])
    order = (jnp.arange(count) - index) % count
    return jnp.stack([pick_at(found, order[n], 0) for n in range(count)])


def window_blocks(rows):
    return min(lax.axis_size("seq") - 1, -(-(DOC_MAX - 1) // rows))


def gather_window(values, beside):
    rows = values.shape[0]
    count, reach = lax.axis_size("seq"), window_blocks(rows)
    left, right = [values], [values]
    for far in range(reach):
        left.append(shift(left[-1], "seq", 1))
        right.append(shift(right[-1], "seq", -1))
        if far == 0:
            left[1], right[1], beside = lax.optimization_barrier((left[1], right[1], beside))
    slots = [values]
    for place in range(1, count):
        found = [right[place]] if place <= reach else []
        found += [left[count - place]] if count - place <= reach else []
        slots.append(sum(found[1:], found[0]) if found else jnp.zeros_like(values))
    return jnp.concatenate(slots, axis=0), beside


eps = 1e-06
GELU_COEF = 0.044715
GELU_ROOT = math.sqrt(2.0 / math.pi)
bf16 = jnp.bfloat16
f32 = jnp.float32


def gelu_both(values):
    inner = GELU_ROOT * (values + GELU_COEF * values * values * values)
    tanh_val = jnp.tanh(inner)
    half = 0.5 * (1.0 + tanh_val)
    slope = half + 0.5 * values * (1.0 - tanh_val * tanh_val) * GELU_ROOT * (
        1.0 + 3.0 * GELU_COEF * values * values
    )
    return values * half, slope


def norm_forward(values, gain_vec):
    inverse = lax.rsqrt(jnp.mean(values * values, axis=-1, keepdims=True) + eps)
    return (values * inverse * gain_vec).astype(bf16), inverse


def norm_backward(values, inverse, gain_vec, grad_normed):
    scaled = grad_normed * gain_vec
    cubed = inverse * inverse * inverse
    grad_values = inverse * scaled - values * cubed * jnp.mean(
        scaled * values, axis=-1, keepdims=True
    )
    return grad_values


def body(
    tokens, doc_lengths, gain_attn, query_weight, key_weight, value_weight, out_weight, bias_table,
    gain_ff, ff_in, ff_out, gain_self, self_value, self_out, gain_cross, cross_query, cross_key,
    cross_value, cross_out, gain_dff, dff_in, dff_out, enc_cot, dec_cot,
):
    seq_index = lax.axis_index("seq")
    seq_count = lax.axis_size("seq")
    own = lax.axis_index("fsdp")
    fsdp = lax.axis_size("fsdp")
    rows = tokens.shape[0]
    width = tokens.shape[1]
    group_tok = rows * seq_count
    part = query_weight.shape[0]
    buckets_part = bias_table.shape[0]
    docs = doc_lengths.shape[1]

    columns = [gain_attn, gain_ff, gain_self, gain_cross, gain_dff,
               jnp.pad(bias_table, (0, part - buckets_part))]
    small = jnp.pad(jnp.stack(columns, axis=1), ((0, 0), (0, 128 - len(columns))))
    over_fsdp = lambda pieces: lax.all_gather(jnp.concatenate(pieces, axis=1), "fsdp", axis=0, tiled=True)
    held = (out_weight, ff_in, self_value, self_out, cross_query, cross_key, cross_value, cross_out, dff_in)
    group, held = gather_window(tokens, held)
    first_weights = over_fsdp([query_weight, key_weight, value_weight, small])
    out_weight_b, ff_in_b, self_value_b, self_out_b, cross_query_b, cross_key_b, cross_value_b, cross_out_b, dff_in_b = held
    wide = dff_out.shape[0] // part
    units = dff_out.shape[0] // seq_count
    dff_in_part = pick_at(dff_in_b.reshape(part, fsdp, seq_count, units), seq_index, 2).reshape(part, fsdp * units)
    dff_out_part = lax.dynamic_slice_in_dim(dff_out, seq_index * units, units, 0)
    second_weights = over_fsdp([out_weight_b, ff_in_b, self_value_b, self_out_b, cross_query_b, cross_key_b])
    ff_out_full = over_fsdp([ff_out])
    third_weights = over_fsdp([cross_value_b, cross_out_b, dff_in_part, dff_out_part])

    query_full = first_weights[:, :width]
    kv_full = first_weights[:, width : 3 * width]
    vectors = first_weights[:, 3 * width : 3 * width + len(columns)].astype(f32)
    gain_attn_f, gain_ff_f, gain_self_f, gain_cross_f, gain_dff_f = (vectors[:, n] for n in range(5))
    table = vectors[:, 5].reshape(fsdp, part)[:, :buckets_part].reshape(HEADS, BUCKETS).astype(bf16)
    span = lambda start, count: second_weights[:, start * width : (start + count) * width]
    out_full = span(0, 1)
    ff_in_full = span(1, wide)
    self_value_full, self_out_full, cross_query_full, cross_key_full = (span(1 + wide + n, 1) for n in range(4))
    cross_value_full, cross_out_full, dff_in_full, dff_out_full = (
        third_weights[:, n * width : (n + 1) * width] for n in range(4))
    lengths = doc_lengths[0]
    end_zero = lengths[0]
    end_one = lengths[0] + lengths[1]
    here = seq_index * rows
    info = jnp.stack([here.astype(jnp.int32), end_zero, end_one])
    local_seg = seg_of(here + jnp.arange(rows, dtype=jnp.int32), end_zero, end_one)
    starts = jnp.stack([jnp.zeros_like(end_zero), end_zero, end_one])

    tokens_f = tokens.astype(f32)
    normed_all, inverse_all = norm_forward(group.astype(f32), gain_attn_f)
    normed, inverse_attn = normed_all[:rows], inverse_all[:rows]
    query = nn(normed, query_full).astype(bf16)
    key = nn(normed_all, kv_full[:, :width]).astype(bf16)
    value = nn(normed_all, kv_full[:, width:]).astype(bf16)
    context, lse = attn_fwd(info, make_band(table, 1), query, key, value)
    middle = tokens_f + nn(context, out_full)
    normed_ff, inverse_ff = norm_forward(middle, gain_ff_f)
    pre_act = nn(normed_ff, ff_in_full)
    hidden_f, slope = gelu_both(pre_act)
    hidden = hidden_f.astype(bf16)
    enc_hidden = middle + nn(hidden, ff_out_full)
    memory = enc_hidden.astype(bf16)

    local_pick = starts[:, None] == here + jnp.arange(rows, dtype=jnp.int32)[None, :]
    first = jnp.sum(gather_seq(nn(local_pick.astype(bf16), tokens).astype(bf16)).astype(f32), axis=0)
    self_low, self_inv = norm_forward(first, gain_self_f)
    self_vals = nn(self_low, self_value_full).astype(bf16)
    state_one = first + nn(self_vals, self_out_full)
    cross_low, cross_inv = norm_forward(state_one, gain_cross_f)
    cross_q = nn(cross_low, cross_query_full).astype(bf16)
    head_of = jnp.arange(width, dtype=jnp.int32) // HEAD
    head_rows = -(-HEADS // 8) * 8
    head_mask = (jnp.arange(head_rows, dtype=jnp.int32)[:, None] == head_of[None, :])[None]

    def by_head(values):
        return jnp.where(head_mask, values[:, None, :], 0).reshape(-1, width)

    def from_heads(values):
        return jnp.sum(jnp.where(head_mask, values.reshape(docs, head_rows, width), 0), axis=1)

    probe = nt(by_head(cross_q), cross_key_full).astype(bf16)
    doc_rows = jnp.repeat(jnp.arange(docs, dtype=jnp.int32), head_rows)
    in_doc = doc_rows[:, None] == local_seg[None, :]
    scores = jnp.where(in_doc, nt(probe, memory), NEG)
    top = jnp.max(scores, axis=1, keepdims=True)
    powers = jnp.where(in_doc, jnp.exp(scores - top), 0.0)
    total = jnp.sum(powers, axis=1, keepdims=True)
    mixed = nn(powers.astype(bf16), memory)
    stat_lanes = jnp.where(jnp.arange(128, dtype=jnp.int32)[None, :] == 0, top, total)
    parts = gather_seq(jnp.concatenate([mixed, stat_lanes], axis=1))
    tops = parts[:, :, width : width + 1]
    top_all = jnp.max(tops, axis=0)
    scale = jnp.exp(tops - top_all[None])
    total_all = jnp.sum(scale * parts[:, :, width + 1 : width + 2], axis=0)
    mixed_f = jnp.sum(scale * parts[:, :, :width], axis=0) / total_all
    mixed_all = mixed_f.astype(bf16)
    cross_ctx = from_heads(nn(mixed_all, cross_value_full)).astype(bf16)
    state_two = state_one + nn(cross_ctx, cross_out_full)
    ffn_low, ffn_inv = norm_forward(state_two, gain_dff_f)
    dec_hid_f, dec_slope = gelu_both(nn(ffn_low, dff_in_full))
    dec_hid = dec_hid_f.astype(bf16)

    grad_dec_pre = (dec_slope * nt(dec_cot, dff_out_full)).astype(bf16)
    halves = jnp.sum(gather_seq(jnp.concatenate([nn(dec_hid, dff_out_full), nt(grad_dec_pre, dff_in_full)])), axis=0)
    dec_hidden = state_two + halves[:docs]
    back_values = norm_backward(state_two, ffn_inv, gain_dff_f, halves[docs:])
    grad_two = dec_cot.astype(f32) + back_values
    grad_two_low = grad_two.astype(bf16)
    grad_cross_ctx = nt(grad_two_low, cross_out_full).astype(bf16)
    pull = nt(by_head(grad_cross_ctx), cross_value_full).astype(bf16)
    probs = powers * (jnp.exp(top - top_all) / total_all)
    row_dot = jnp.sum(mixed_f * pull.astype(f32), axis=1, keepdims=True)
    grad_scores = (probs * (nt(pull, memory) - row_dot)).astype(bf16)
    grad_memory = tn(jnp.concatenate([grad_scores, probs.astype(bf16)], axis=0),
                     jnp.concatenate([probe, pull], axis=0))
    joint = gather_seq(jnp.concatenate([nn(grad_scores, memory).astype(bf16), dec_hid, grad_dec_pre], axis=0))
    heads_rows = head_rows * docs
    grad_mixed = jnp.sum(joint[:, :heads_rows].astype(f32), axis=0).astype(bf16)
    grad_cross_q = from_heads(nn(grad_mixed, cross_key_full)).astype(bf16)
    back_values = norm_backward(state_one, cross_inv, gain_cross_f, nt(grad_cross_q, cross_query_full))
    grad_one = grad_two + back_values
    grad_one_low = grad_one.astype(bf16)
    grad_self_vals = nt(grad_one_low, self_out_full).astype(bf16)
    back_values = norm_backward(first, self_inv, gain_self_f, nt(grad_self_vals, self_value_full))
    grad_first = grad_one + back_values

    both = joint[:, heads_rows:].reshape(seq_count, 2, docs, fsdp, units)
    both = both.transpose(1, 2, 3, 0, 4).reshape(2, docs, fsdp * seq_count * units)
    pack = [self_low, grad_self_vals, self_vals, grad_one_low, cross_low, grad_cross_q, cross_q, grad_cross_ctx,
            cross_ctx, grad_two_low, ffn_low, dec_cot]
    pack += [both[0, :, n * width : (n + 1) * width] for n in range(wide)]
    pack += [both[1, :, n * width : (n + 1) * width] for n in range(wide)]
    tile = 8
    pack = [jnp.pad(rows_of, ((0, tile - docs), (0, 0))) for rows_of in pack] + [grad_mixed, mixed_all]
    pack = jnp.concatenate(pack, axis=0)

    grad_enc = enc_cot.astype(f32) + grad_memory
    grad_enc_low = grad_enc.astype(bf16)
    blocks = tn(hidden, grad_enc_low).astype(bf16).reshape(fsdp, wide, part, width)
    grad_pre = (slope * nt(grad_enc_low, ff_out_full)).astype(bf16)
    back_values = norm_backward(middle, inverse_ff, gain_ff_f, nt(grad_pre, ff_in_full))
    grad_middle = grad_enc + back_values
    grad_middle_low = grad_middle.astype(bf16)
    early = [blocks[:, n] for n in range(wide)] + [tn(context, grad_middle_low).astype(bf16).reshape(fsdp, part, width)]
    across = [tn(normed_ff, grad_pre).astype(bf16).reshape(fsdp, part, wide * width)]
    early, across = scatter_core(early), scatter_core(across)
    grad_context = nt(grad_middle_low, out_full).astype(bf16)
    band, early, across, pack = lax.optimization_barrier((make_band(table, -1), early, across, pack))
    early = scatter_chips(early)
    seq_bits = bits_of("seq")
    pairs = HEADS // 2
    across = halve_seq(across, seq_bits[0], 2)
    grads = attn_bwd(info, band, query, key, value, grad_context, context, lse, 0, pairs, None)
    grads, early, across, pack = lax.optimization_barrier((grads, early, across, pack))
    packs = lax.all_gather(pack, "fsdp", axis=0)
    stack = lambda shard: jnp.concatenate(
        [shard[:, n * width : (n + 1) * width] for n in range(shard.shape[1] // width)], axis=0)
    unstack = lambda rows_of: jnp.concatenate(
        [rows_of[n * part : (n + 1) * part] for n in range(rows_of.shape[0] // part)], axis=1)
    grad_query, grad_key, grad_value, grad_band, grad_far = grads
    reach = window_blocks(rows)

    def term(step):
        place = step % seq_count * rows
        block = lambda values: values[place : place + rows]
        return nt(block(grad_key), kv_full[:, :width]) + nt(block(grad_value), kv_full[:, width:])

    signs = (1, -1)
    moving = [shift(term(sign * reach).astype(bf16), "seq", sign) for sign in signs]
    early = halve_seq(stack(early), seq_bits[0], 0)
    for bit in seq_bits[1:]:
        across = halve_seq(across, bit, 2)
    late = [tn(normed, grad_query), tn(normed_all, grad_key), tn(normed_all, grad_value)]
    late = [piece.astype(bf16).reshape(fsdp, part, width) for piece in late]
    grad_table = table_grad(grad_band, grad_far).reshape(fsdp, 1, buckets_part).astype(bf16)
    late += [jnp.pad(grad_table, ((0, 0), (0, part - 1), (0, 128 - buckets_part)))]
    late = scatter_core(late)
    near = [[term(sign * far) for sign in signs] for far in range(reach - 1, 0, -1)]
    moving, early, across, late, near = lax.optimization_barrier((moving, early, across, late, near))
    for terms in near:
        moving = [shift(add_low(one, come), "seq", sign) for one, come, sign in zip(terms, moving, signs)]
    for bit in seq_bits[1:]:
        early = halve_seq(early, bit, 0)
    late, across = scatter_chips(late), scatter_chips(across)
    rowset = lambda n: packs[:, n * tile : (n + 1) * tile].reshape(fsdp * tile, width)
    mine = lambda values: lax.dynamic_slice_in_dim(values, own * part, part, 1)
    at = 12
    hid_all = jnp.concatenate([rowset(at + n) for n in range(wide)], axis=1)
    pre_all = jnp.concatenate([rowset(at + wide + n) for n in range(wide)], axis=1)
    part_ff = dff_out.shape[0]
    at = (12 + 2 * wide) * tile
    heads_rows = head_rows * docs
    mixed_g = packs[:, at : at + heads_rows].reshape(fsdp * heads_rows, width)
    mixed_m = packs[:, at + heads_rows : at + 2 * heads_rows].reshape(fsdp * heads_rows, width)
    spread = lambda n: jnp.where(head_mask[None], packs[:, n * tile : n * tile + docs, None], 0).reshape(
        fsdp * heads_rows, width)
    dec_shards = [
        tn(mine(rowset(0)), rowset(1)), tn(mine(rowset(2)), rowset(3)), tn(mine(rowset(4)), rowset(5)),
        tn(mine(mixed_g), spread(6)), tn(mine(mixed_m), spread(7)), tn(mine(rowset(8)), rowset(9)),
        tn(mine(rowset(10)), pre_all),
        tn(lax.dynamic_slice_in_dim(hid_all, own * part_ff, part_ff, 1), rowset(11)),
    ]
    moving, early, across, late, dec_shards = lax.optimization_barrier((moving, early, across, late, dec_shards))
    shard_self_value, shard_self_out, shard_cross_query, shard_cross_key = dec_shards[:4]
    shard_cross_value, shard_cross_out, shard_dff_in, shard_dff_out = dec_shards[4:]
    table_rows = jnp.pad(late[:1, 3 * width :], ((0, 31), (0, width - 128)))
    late = jnp.concatenate([stack(late[:, : 3 * width]), table_rows], axis=0)
    for back, bit in zip(seq_bits[::-1], seq_bits):
        across, early = join_seq([across, early], [1, 0], back, width)
        late = halve_seq(late, bit, 0)
        across, early, late = lax.optimization_barrier((across, early, late))
    for back in seq_bits[::-1]:
        (late,) = join_seq([late], [0], back, width)
    shard_ff_out = early[: wide * part].astype(f32)
    shard_ff_in = across.astype(f32)
    shard_out = early[wide * part :].astype(f32)
    late = late.astype(f32)
    shard_query, shard_key, shard_value = (late[n * part : (n + 1) * part] for n in range(3))
    shard_table = late[3 * part, :buckets_part]
    grad_normed = term(0) + nt(grad_query, query_full)
    grad_normed = grad_normed + (moving[0].astype(f32) + moving[1].astype(f32))
    back_values = norm_backward(tokens_f, inverse_attn, gain_attn_f, grad_normed)
    first_back = lax.dot_general(local_pick.astype(f32), grad_first, (((0,), (0,)), ((), ())),
                                 precision=lax.Precision.HIGHEST, preferred_element_type=f32)
    tokens_grad = grad_middle + back_values + first_back

    def gain_grad(gain_vec, *pairs_of):
        return sum(jnp.sum(grad * weight.astype(f32), axis=1) for grad, weight in pairs_of) / gain_vec.astype(f32)

    grad_gain_attn = gain_grad(gain_attn, (shard_query, query_weight), (shard_key, key_weight), (shard_value, value_weight))
    grad_gain_ff = gain_grad(gain_ff, (shard_ff_in, ff_in))
    grad_gain_self = gain_grad(gain_self, (shard_self_value, self_value))
    grad_gain_cross = gain_grad(gain_cross, (shard_cross_query, cross_query))
    grad_gain_dff = gain_grad(gain_dff, (shard_dff_in, dff_in))
    return (
        enc_hidden, dec_hidden, tokens_grad, grad_gain_attn, shard_query, shard_key, shard_value, shard_out,
        shard_table, grad_gain_ff, shard_ff_in, shard_ff_out, grad_gain_self, shard_self_value, shard_self_out,
        grad_gain_cross, shard_cross_query, shard_cross_key, shard_cross_value, shard_cross_out, grad_gain_dff,
        shard_dff_in, shard_dff_out,
    )


def solution(mesh):
    tok, wide, one = P(("fsdp", "seq"), None), P("fsdp", None), P("fsdp")
    return jax.shard_map(
        body,
        mesh=mesh,
        in_specs=(tok, wide, one, wide, wide, wide, wide, one, one, wide, wide, one, wide, wide, one, wide, wide, wide,
                  wide, one, wide, wide, tok, wide),
        out_specs=(tok, wide, tok, one, wide, wide, wide, wide, one, one, wide, wide, one, wide, wide, one, wide, wide,
                   wide, wide, one, wide, wide),
        check_vma=False,
    )
```
